32 devices in a mesh: seq: 4 (over y, core), shard: 8 (over z, x).
Axes of the slice: x: 2, y: 2, z: 4, core: 2. Of those that a mesh axis runs over, the one named last changes fastest.
Arguments:
- inputs: bfloat16 [16, 1184, 1024], P('shard', 'seq'), may hold values from -24 to 24
- cotangent: bfloat16 [16, 1184, 1024], P('shard', 'seq'), may hold values from -6 to 6
- first_gain: bfloat16 [1024], P('shard'), may hold values from 0.5 to 1.5
- first_shift: bfloat16 [1024], P('shard'), may hold values from -4 to 4
- joint_weight: bfloat16 [1024, 3072], P('shard'), may hold values from -0.203125 to 0.203125
- joint_bias: bfloat16 [2048], P('shard'), may hold values from -1.5 to 1.5
- output_weight: bfloat16 [1024, 1024], P('shard'), may hold values from -1.5 to 1.5
- output_bias: bfloat16 [1024], P('shard'), may hold values from -6 to 6
- second_gain: bfloat16 [1024], P('shard'), may hold values from 0.5 to 1.5
- second_shift: bfloat16 [1024], P('shard'), may hold values from -4 to 4
- expand_weight: bfloat16 [1024, 4096], P('shard'), may hold values from -0.203125 to 0.203125
- expand_bias: bfloat16 [4096], P('shard'), may hold values from -6 to 6
- reduce_weight: bfloat16 [4096, 1024], P('shard'), may hold values from -0.09375 to 0.09375
- reduce_bias: bfloat16 [1024], P('shard'), may hold values from -6 to 6
Outputs:
- layer_out: bfloat16 [16, 1184, 1024], P('shard', 'seq')
- input_grad: bfloat16 [16, 1184, 1024], P('shard', 'seq')
- first_gain_grad: float32 [1024], P(('seq', 'shard'))
- first_shift_grad: float32 [1024], P(('seq', 'shard'))
- joint_weight_grad: float32 [1024, 3072], P(('seq', 'shard'))
- joint_bias_grad: float32 [2048], P(('seq', 'shard'))
- output_weight_grad: float32 [1024, 1024], P(('seq', 'shard'))
- output_bias_grad: float32 [1024], P(('seq', 'shard'))
- second_gain_grad: float32 [1024], P(('seq', 'shard'))
- second_shift_grad: float32 [1024], P(('seq', 'shard'))
- expand_weight_grad: float32 [1024, 4096], P(('seq', 'shard'))
- expand_bias_grad: float32 [4096], P(('seq', 'shard'))
- reduce_weight_grad: float32 [4096, 1024], P(('seq', 'shard'))
- reduce_bias_grad: float32 [1024], P(('seq', 'shard'))
- root_means: float32 [3], replicated
The draws below stay inside these ranges and needn't reach their ends.
All inputs are finite; a program needn't handle non-finite values.
Results may differ from the reference program's by a relative error of at most 0.009.
Values may be sent and summed in bfloat16 or wider, within the bound.
A program may use at most 256 MiB of HBM per device.

```python
import math
import jax
import jax.numpy as jnp
from jax import lax

D = 1024
HEADS = 16
HEAD_DIM = 64
FF = 4096
LEN = 592
VALID = 577
PACK = 2
SEQ = 1184
ROWS = 16


def draw_inputs(key, part):
    row_pos = jnp.arange(ROWS, dtype=jnp.float32) / max(ROWS - 1, 1)
    tok_pos = jnp.arange(SEQ, dtype=jnp.float32) / max(SEQ - 1, 1)
    noise = jnp.clip(jax.random.normal(key, (ROWS, SEQ, D), jnp.float32), -6.0, 6.0)
    top_amp = 4.0
    amplitude = top_amp ** (0.5 * row_pos[:, None] + 0.5 * tok_pos[None, :])
    return (noise * amplitude[:, :, None]).astype(jnp.bfloat16)


def column_offset(noise, offset_key, columns, fan_in):
    offset = jnp.clip(jax.random.normal(offset_key, (columns,), jnp.float32), -3.0, 3.0) * 0.7
    return (noise + offset[None, :]) * (0.8 / math.sqrt(fan_in))


def draw_joint_weight(key, part):
    key = jax.random.fold_in(key, 11)
    noise_key, offset_key = jax.random.split(key)
    noise = jnp.clip(jax.random.normal(noise_key, (D, 3 * D), jnp.float32), -6.0, 6.0)
    return column_offset(noise, offset_key, 3 * D, D).astype(jnp.bfloat16)


def draw_expand_weight(key, part):
    key = jax.random.fold_in(key, 23)
    noise_key, offset_key = jax.random.split(key)
    noise = jnp.clip(jax.random.normal(noise_key, (D, FF), jnp.float32), -6.0, 6.0)
    return column_offset(noise, offset_key, FF, D).astype(jnp.bfloat16)


def levels(key, dims, pieces, smallest, high):
    factor_of, own = 1.0, jax.random.fold_in(key, 6)
    for axis_at, shards_of in pieces:
        draws = jnp.exp(jax.random.uniform(jax.random.fold_in(own, axis_at), (shards_of,), jnp.float32, smallest / len(pieces), high / len(pieces)))
        factor_of = factor_of * jnp.repeat(draws, dims[axis_at] // shards_of).reshape([-1 if axis == axis_at else 1 for axis in range(len(dims))])
    return factor_of


def normal_values(rng, extent, deviation, most, cuts=(), held_as=jnp.bfloat16):
    level = levels(rng, extent, cuts, -0.22, 0.18) if cuts else 1.0
    values = jax.random.normal(rng, extent, jnp.float32) * deviation * level
    return jnp.minimum(jnp.maximum(values, -most), most).astype(held_as)


def setup_inputs(seed: int = 0) -> dict:
    arg_keys = jax.random.split(jax.random.key(seed), 15)
    inputs = draw_inputs(jax.random.fold_in(arg_keys[14], 71), 0)
    cotangent = normal_values(arg_keys[1], (ROWS, SEQ, D), 1.0, 6.0, ((0, 8), (1, 4)))
    first_gain = jnp.clip(1.0 + 0.1 * jax.random.normal(arg_keys[2], (D,), jnp.float32), 0.5, 1.5).astype(jnp.bfloat16)
    first_shift = normal_values(arg_keys[3], (D,), 0.3, 4.0, ((0, 8),))
    joint_weight = draw_joint_weight(jax.random.fold_in(arg_keys[14], 71), 0)
    joint_bias = normal_values(arg_keys[5], (2 * D,), 0.1, 1.5, ((0, 8),))
    output_weight = normal_values(arg_keys[6], (D, D), (max(D // 64, 1)) ** -0.5, 1.5, ((0, 8),))
    output_bias = normal_values(arg_keys[7], (D,), 0.5, 6.0, ((0, 8),))
    second_gain = jnp.clip(1.0 + 0.1 * jax.random.normal(arg_keys[8], (D,), jnp.float32), 0.5, 1.5).astype(jnp.bfloat16)
    second_shift = normal_values(arg_keys[9], (D,), 0.3, 4.0, ((0, 8),))
    expand_weight = draw_expand_weight(jax.random.fold_in(arg_keys[14], 71), 0)
    expand_bias = normal_values(arg_keys[11], (FF,), 0.5, 6.0, ((0, 8),))
    reduce_weight = normal_values(arg_keys[12], (FF, D), FF ** -0.5, 0.09375, ((0, 8),))
    reduce_bias = normal_values(arg_keys[13], (D,), 0.5, 6.0, ((0, 8),))
    return {"inputs": inputs, "cotangent": cotangent, "first_gain": first_gain, "first_shift": first_shift, "joint_weight": joint_weight, "joint_bias": joint_bias, "output_weight": output_weight, "output_bias": output_bias, "second_gain": second_gain, "second_shift": second_shift, "expand_weight": expand_weight, "expand_bias": expand_bias, "reduce_weight": reduce_weight, "reduce_bias": reduce_bias}


@jax.custom_vjp
def low(v):
    return lax.optimization_barrier(v.astype(jnp.bfloat16)).astype(jnp.float32)

@jax.custom_vjp
def low_back(v):
    return v

def low_keep(v):
    return (low(v), None)

def low_pass(kept, grad):
    return (grad,)

def back_keep(v):
    return (v, None)

def back_low(kept, grad):
    return (low(grad),)
low.defvjp(low_keep, low_pass)
low_back.defvjp(back_keep, back_low)

def matmul(left, right):
    return jnp.dot(left, right, precision=lax.Precision.HIGHEST, preferred_element_type=jnp.float32)

def layer_norm(value, gain, shift):
    center = value - lax.optimization_barrier(jnp.mean(value, axis=-1, keepdims=True))
    spread = lax.optimization_barrier(jnp.mean(center * center, axis=-1, keepdims=True))
    return center * lax.rsqrt(spread + 1e-06) * gain + shift

def reference(inputs, cotangent, first_gain, first_shift, joint_weight, joint_bias, output_weight, output_bias, second_gain, second_shift, expand_weight, expand_bias, reduce_weight, reduce_bias):
    params = (first_gain.astype(jnp.float32), first_shift.astype(jnp.float32), joint_weight.astype(jnp.float32), joint_bias.astype(jnp.float32), output_weight.astype(jnp.float32), output_bias.astype(jnp.float32), second_gain.astype(jnp.float32), second_shift.astype(jnp.float32), expand_weight.astype(jnp.float32), expand_bias.astype(jnp.float32), reduce_weight.astype(jnp.float32), reduce_bias.astype(jnp.float32))
    places = jnp.arange(SEQ, dtype=jnp.int32)
    row_mask = (places % LEN < VALID).astype(jnp.float32)
    maskf = jnp.broadcast_to(row_mask[None, :], (ROWS, SEQ))
    xfull = inputs.astype(jnp.float32)
    factor = HEAD_DIM ** (-0.5)

    def forward(weights, xvalues):
        g1, s1, wj, bj, wo, bo, g2, s2, w1, b1, w2, b2 = weights
        bias_full = jnp.concatenate([bj[:D], jnp.zeros((D,), jnp.float32), bj[D:]])

        def one_row(item):
            xi, mi = item
            a1 = low(layer_norm(xi, g1, s1))
            qkv = low(low_back(matmul(a1, wj) + bias_full)).reshape(PACK, LEN, 3, HEADS, HEAD_DIM)
            query, keys, values = (qkv[:, :, 0], qkv[:, :, 1], qkv[:, :, 2])
            raw = jnp.einsum('pqhd,pkhd->phqk', query, keys, precision=lax.Precision.HIGHEST)
            scaled = low_back(raw * factor)
            key_mask = mi.reshape(PACK, LEN)[:, None, None, :]
            scores = jnp.where(key_mask > 0.5, scaled, -1000000000.0)
            probs = jax.nn.softmax(scores, axis=-1)
            context = jnp.einsum('phqk,pkhd->pqhd', low(probs), values, precision=lax.Precision.HIGHEST).reshape(SEQ, D)
            context = low(low_back(context))
            attn = low_back(matmul(context, wo) + bo)
            resid = xi + attn
            a2 = low(layer_norm(resid, g2, s2))
            upper = low_back(matmul(a2, w1) + b1)
            hidden = low(jax.nn.gelu(upper, approximate=False))
            branch = matmul(hidden, w2) + b2
            result = resid + branch
            weight = mi[:, None]
            sums = jnp.stack([jnp.sum(result * result * weight), jnp.sum(attn * attn * weight), jnp.sum(branch * branch * weight)])
            return (result, sums)
        outs, sums = lax.map(jax.checkpoint(one_row), (xvalues, maskf))
        return (outs, lax.optimization_barrier(jnp.sum(sums, axis=0)))
    outs, vjp_fn, sums = jax.vjp(forward, params, xfull, has_aux=True)
    grads, xgrad = vjp_fn(cotangent.astype(jnp.float32) * maskf[:, :, None])
    counted = jnp.sum(maskf) * D
    root_means = jnp.sqrt(sums / counted + 1e-06)
    return (outs.astype(jnp.bfloat16), xgrad.astype(jnp.bfloat16), grads[0], grads[1], grads[2], grads[3], grads[4], grads[5], grads[6], grads[7], grads[8], grads[9], grads[10], grads[11], root_means)
```

```python
import functools

import jax
import jax.numpy as jnp
from jax import lax
from jax.experimental import pallas as pl
from jax.experimental.pallas import tpu as pltpu
from jax.sharding import PartitionSpec as P

MESH = pl.DeviceIdType.MESH
HEAD_DIM = 64
LEN = 592
VALID = 577
PACK = 2


def layer_norm(value, gain, shift):
    center = value - jnp.mean(value, axis=-1, keepdims=True)
    spread = jnp.mean(center * center, axis=-1, keepdims=True)
    return center * lax.rsqrt(spread + 1e-06) * gain + shift


def weight_grad(left, right):
    return lax.dot_general(
        left, right, (((0, 1), (0, 1)), ((), ())), preferred_element_type=jnp.float32
    )


def back_product(grad, matrix):
    return lax.dot_general(
        grad, matrix, (((2,), (1,)), ((), ())), preferred_element_type=jnp.float32
    )


def exact_gelu(value):
    return jax.nn.gelu(value, approximate=False)


def on_device(
    inputs,
    cotangent,
    first_gain,
    first_shift,
    joint_weight,
    joint_bias,
    output_weight,
    output_bias,
    second_gain,
    second_shift,
    expand_weight,
    expand_bias,
    reduce_weight,
    reduce_bias,
):
    images = inputs.shape[0]
    tokens = inputs.shape[1]
    full_seq = PACK * LEN
    pieces = images * PACK
    factor = HEAD_DIM ** (-0.5)
    begin = lax.axis_index("seq") * tokens
    local_places = begin + jnp.arange(tokens, dtype=jnp.int32)
    local_row = (local_places % LEN < VALID).astype(jnp.float32)
    local_mask = jnp.broadcast_to(local_row[None, :], (images, tokens))
    key_keep = jnp.arange(LEN, dtype=jnp.int32) < VALID
    weighting = local_mask[:, :, None]
    g1w, s1w, wj, bj, wo, bo, g2w, s2w, w1, b1, w2, b2 = (
        lax.all_gather(first_gain, "shard", axis=0, tiled=True),
        lax.all_gather(first_shift, "shard", axis=0, tiled=True),
        lax.all_gather(joint_weight, "shard", axis=0, tiled=True),
        lax.all_gather(joint_bias, "shard", axis=0, tiled=True),
        lax.all_gather(output_weight, "shard", axis=0, tiled=True),
        lax.all_gather(output_bias, "shard", axis=0, tiled=True),
        lax.all_gather(second_gain, "shard", axis=0, tiled=True),
        lax.all_gather(second_shift, "shard", axis=0, tiled=True),
        lax.all_gather(expand_weight, "shard", axis=0, tiled=True),
        lax.all_gather(expand_bias, "shard", axis=0, tiled=True),
        lax.all_gather(reduce_weight, "shard", axis=0, tiled=True),
        lax.all_gather(reduce_bias, "shard", axis=0, tiled=True),
    )
    g1f = g1w.astype(jnp.float32)
    s1f = s1w.astype(jnp.float32)
    bjf = bj.astype(jnp.float32)
    bof = bo.astype(jnp.float32)
    g2f = g2w.astype(jnp.float32)
    s2f = s2w.astype(jnp.float32)
    b1f = b1.astype(jnp.float32)
    b2f = b2.astype(jnp.float32)
    width = g1f.shape[0]
    xfull = inputs.astype(jnp.float32)
    normed1, first_back = jax.vjp(layer_norm, xfull, g1f, s1f)
    active1 = normed1.astype(jnp.bfloat16)
    bias_full = jnp.concatenate([bjf[:width], jnp.zeros((width,), jnp.float32), bjf[width:]])
    joint = (jnp.dot(active1, wj, preferred_element_type=jnp.float32) + bias_full).astype(
        jnp.bfloat16
    )
    joint = joint.reshape(images, tokens, 3, width)
    heads = lax.all_to_all(joint, "seq", split_axis=3, concat_axis=1, tiled=True)
    local_width = heads.shape[3]
    local_heads = local_width // HEAD_DIM
    query = heads[:, :, 0].reshape(pieces, LEN, local_heads, HEAD_DIM)
    keys = heads[:, :, 1].reshape(pieces, LEN, local_heads, HEAD_DIM)
    values = heads[:, :, 2].reshape(pieces, LEN, local_heads, HEAD_DIM)

    def score_block(qpart, kpart):
        raw = jnp.einsum("qhd,khd->hqk", qpart, kpart, preferred_element_type=jnp.float32) * factor
        return jnp.where(key_keep[None, None, :], raw, -1000000000.0)

    def attend(item):
        qpart, kpart, vpart = item
        scores = score_block(qpart, kpart)
        top = jnp.max(scores, axis=-1, keepdims=True)
        expo = jnp.exp(scores - top)
        total = jnp.sum(expo, axis=-1, keepdims=True)
        probs = expo / total
        logsum = (top + jnp.log(total))[:, :, 0]
        context = jnp.einsum(
            "hqk,khd->qhd", probs.astype(jnp.bfloat16), vpart, preferred_element_type=jnp.float32
        )
        return (context.astype(jnp.bfloat16).reshape(LEN, local_width), logsum)

    context, logsums = lax.map(attend, (query, keys, values))
    context = context.reshape(images, full_seq, local_width)
    gathered_ctx = lax.all_to_all(context, "seq", split_axis=1, concat_axis=2, tiled=True)
    attn = jnp.dot(gathered_ctx, wo, preferred_element_type=jnp.float32) + bof
    resid = xfull + attn
    normed2, second_back = jax.vjp(layer_norm, resid, g2f, s2f)
    active2 = normed2.astype(jnp.bfloat16)
    upper = jnp.dot(active2, w1, preferred_element_type=jnp.float32) + b1f
    activated, gelu_back = jax.vjp(exact_gelu, upper)
    hidden = activated.astype(jnp.bfloat16)
    branch = jnp.dot(hidden, w2, preferred_element_type=jnp.float32) + b2f
    result = resid + branch
    sums = jnp.stack(
        [
            jnp.sum(result * result * weighting),
            jnp.sum(attn * attn * weighting),
            jnp.sum(branch * branch * weighting),
        ]
    )
    counted = jnp.sum(local_mask) * width
    total_sums, total_count = lax.psum((sums, counted), ("seq", "shard"))
    root_means = jnp.sqrt(total_sums / total_count + 1e-06)
    wj, wo, w1, w2 = (
        lax.all_gather(joint_weight, "shard", axis=0, tiled=True),
        lax.all_gather(output_weight, "shard", axis=0, tiled=True),
        lax.all_gather(expand_weight, "shard", axis=0, tiled=True),
        lax.all_gather(reduce_weight, "shard", axis=0, tiled=True),
    )
    dout = cotangent.astype(jnp.float32) * weighting
    dout_low = dout.astype(jnp.bfloat16)
    grad_w2 = weight_grad(hidden, dout_low)
    grad_b2 = jnp.sum(dout, axis=(0, 1))
    dhidden = back_product(dout_low, w2)
    dupper = gelu_back(dhidden)[0].astype(jnp.bfloat16)
    grad_w1 = weight_grad(active2, dupper)
    grad_b1 = jnp.sum(dupper.astype(jnp.float32), axis=(0, 1))
    dactive2 = back_product(dupper, w1)
    dresid_norm, grad_g2, grad_s2 = second_back(dactive2)
    dresid = dout + dresid_norm
    dattn = dresid.astype(jnp.bfloat16)
    grad_wo = weight_grad(gathered_ctx, dattn)
    grad_bo = jnp.sum(dattn.astype(jnp.float32), axis=(0, 1))
    dcontext = back_product(dattn, wo).astype(jnp.bfloat16)
    dctx_heads = lax.all_to_all(dcontext, "seq", split_axis=2, concat_axis=1, tiled=True)
    dctx_heads = dctx_heads.reshape(pieces, LEN, local_heads, HEAD_DIM)

    def attend_back(item):
        qpart, kpart, vpart, logsum, dpart = item
        scores = score_block(qpart, kpart)
        probs = jnp.exp(scores - logsum[:, :, None])
        dprobs = jnp.einsum("qhd,khd->hqk", dpart, vpart, preferred_element_type=jnp.float32)
        dscore = (probs * (dprobs - jnp.sum(probs * dprobs, axis=-1, keepdims=True))).astype(
            jnp.bfloat16
        )
        dquery = (
            jnp.einsum("hqk,khd->qhd", dscore, kpart, preferred_element_type=jnp.float32) * factor
        )
        dkeys = (
            jnp.einsum("hqk,qhd->khd", dscore, qpart, preferred_element_type=jnp.float32) * factor
        )
        dvalues = jnp.einsum(
            "hqk,qhd->khd", probs.astype(jnp.bfloat16), dpart, preferred_element_type=jnp.float32
        )
        stacked = jnp.stack([dquery, dkeys, dvalues], axis=1).astype(jnp.bfloat16)
        return stacked.reshape(LEN, 3, local_width)

    dheads = lax.map(attend_back, (query, keys, values, logsums, dctx_heads))
    dheads = dheads.reshape(images, full_seq, 3, local_width)
    djoint = lax.all_to_all(dheads, "seq", split_axis=1, concat_axis=3, tiled=True)
    djoint = djoint.reshape(images, tokens, 3 * width)
    grad_wj = weight_grad(active1, djoint)
    joint_sums = jnp.sum(djoint.astype(jnp.float32), axis=(0, 1))
    grad_bj = jnp.concatenate([joint_sums[:width], joint_sums[2 * width :]])
    dactive1 = back_product(djoint, wj)
    dinput_norm, grad_g1, grad_s1 = first_back(dactive1)
    dinput = (dresid + dinput_norm).astype(jnp.bfloat16)
    (
        own_g1,
        own_s1,
        own_wj,
        own_bj,
        own_wo,
        own_bo,
        own_g2,
        own_s2,
        own_w1,
        own_b1,
        own_w2,
        own_b2,
    ) = (
        lax.psum_scatter(grad_g1, ("seq", "shard"), scatter_dimension=0, tiled=True),
        lax.psum_scatter(grad_s1, ("seq", "shard"), scatter_dimension=0, tiled=True),
        lax.psum_scatter(grad_wj, ("seq", "shard"), scatter_dimension=0, tiled=True),
        lax.psum_scatter(grad_bj, ("seq", "shard"), scatter_dimension=0, tiled=True),
        lax.psum_scatter(grad_wo, ("seq", "shard"), scatter_dimension=0, tiled=True),
        lax.psum_scatter(grad_bo, ("seq", "shard"), scatter_dimension=0, tiled=True),
        lax.psum_scatter(grad_g2, ("seq", "shard"), scatter_dimension=0, tiled=True),
        lax.psum_scatter(grad_s2, ("seq", "shard"), scatter_dimension=0, tiled=True),
        lax.psum_scatter(grad_w1, ("seq", "shard"), scatter_dimension=0, tiled=True),
        lax.psum_scatter(grad_b1, ("seq", "shard"), scatter_dimension=0, tiled=True),
        lax.psum_scatter(grad_w2, ("seq", "shard"), scatter_dimension=0, tiled=True),
        lax.psum_scatter(grad_b2, ("seq", "shard"), scatter_dimension=0, tiled=True),
    )
    return (
        result.astype(jnp.bfloat16),
        dinput,
        own_g1,
        own_s1,
        own_wj,
        own_bj,
        own_wo,
        own_bo,
        own_g2,
        own_s2,
        own_w1,
        own_b1,
        own_w2,
        own_b2,
        root_means,
    )


def place():
    seq = lax.axis_index("seq")
    shard = lax.axis_index("shard")
    return lax.rem(shard, 2), lax.div(seq, 2), lax.div(shard, 2), lax.rem(seq, 2)


def z_partner(z, k):
    if k == 0:
        return z
    if k == 1:
        return z + 1 - 2 * lax.rem(z, 2)
    if k == 2:
        return lax.rem(z + 2, 4)
    return 3 - z


def dev(x, y, z, c):
    return (y * 2 + c, z * 2 + x)


class Gather:
    def __init__(self, part, full, edge, sems):
        self.part, self.full = part, full
        self.zs, self.xs, self.ys, self.cs, self.es, self.own = sems
        self.rows, self.cols = part.shape
        self.edge = edge
        self.x, self.y, self.z, self.c = place()
        self.duty = pl.ds(pl.multiple_of(self.y * edge, 128), self.cols - edge)
        span = self.cols - edge
        self.mine = pl.ds(pl.multiple_of(self.y * span, 128), edge)
        self.other = pl.ds(pl.multiple_of((1 - self.y) * span, 128), edge)

    def half(self, k, j):
        x = self.x if j == 0 else 1 - self.x
        shard = z_partner(self.z, k) * 2 + x
        half = self.rows // 2
        return pl.ds(pl.multiple_of(shard * self.rows + self.c * half, half), half)

    def copy(self, k, j, cols, sem, target, local=False):
        at = (self.half(k, j), cols)
        if local:
            half = self.rows // 2
            src = self.part.at[pl.ds(pl.multiple_of(self.c * half, half), half), cols]
        else:
            src = self.full.at[at]
        return pltpu.make_async_remote_copy(
            src_ref=src,
            dst_ref=self.full.at[at],
            send_sem=sem.at[0],
            recv_sem=sem.at[1],
            device_id=target,
            device_id_type=MESH,
        )

    def over_z(self, k):
        t = dev(self.x, self.y, z_partner(self.z, k), self.c)
        return self.copy(0, 0, self.duty, self.zs.at[k - 1], t, local=True)

    def over_x(self, k):
        t = dev(1 - self.x, self.y, self.z, self.c)
        return self.copy(k, 0, self.duty, self.xs.at[k], t, local=k == 0)

    def over_y(self, k, j):
        t = dev(self.x, 1 - self.y, self.z, self.c)
        return self.copy(k, j, self.mine, self.ys.at[k * 2 + j], t)

    def over_core(self, k, j):
        t = dev(self.x, self.y, self.z, 1 - self.c)
        return self.copy(k, j, self.duty, self.cs.at[k * 2 + j], t)

    def over_core_rest(self, k, j):
        t = dev(self.x, self.y, self.z, 1 - self.c)
        return self.copy(k, j, self.other, self.es.at[k * 2 + j], t)

    def own_copy(self):
        shard = self.z * 2 + self.x
        rows = pl.ds(pl.multiple_of(shard * self.rows, self.rows), self.rows)
        return pltpu.make_async_copy(self.part, self.full.at[rows], self.own.at[0])

    def step0(self):
        for k in (3, 2, 1):
            self.over_z(k).start()
        self.over_x(0).start()
        self.own_copy().start()

    def step1(self):
        for k in (1, 2, 3):
            self.over_z(k).wait_recv()
            self.over_x(k).start()
            self.over_y(k, 0).start()
            self.over_core(k, 0).start()

    def step2(self):
        for k in (0, 1, 2, 3):
            self.over_x(k).wait_recv()
            self.over_y(k, 1).start()
            self.over_core(k, 1).start()

    def others(self):
        return [(k, 0) for k in (1, 2, 3)] + [(k, 1) for k in (0, 1, 2, 3)]

    def step3(self):
        for k, j in self.others():
            self.over_y(k, j).wait_recv()
            self.over_core_rest(k, j).start()

    def step4(self):
        for k, j in self.others():
            self.over_core(k, j).wait()
            self.over_core_rest(k, j).wait()
            self.over_y(k, j).wait_send()
        for k in (1, 2, 3):
            self.over_z(k).wait_send()
        for k in range(4):
            self.over_x(k).wait_send()
        self.own_copy().wait()


class SmallGather:
    def __init__(self, part, full, zs, xs, own):
        self.part, self.full, self.zs, self.xs, self.own = part, full, zs, xs, own
        self.x, self.y, self.z, self.c = place()
        self.rows = part.shape[0]

    def at(self, k):
        shard = z_partner(self.z, k) * 2 + self.x
        return pl.ds(pl.multiple_of(shard * self.rows, self.rows), self.rows)

    def copy(self, k, sem, target, local=False):
        return pltpu.make_async_remote_copy(
            src_ref=self.part if local else self.full.at[self.at(k)],
            dst_ref=self.full.at[self.at(k)],
            send_sem=sem.at[0],
            recv_sem=sem.at[1],
            device_id=target,
            device_id_type=MESH,
        )

    def over_z(self, k):
        t = dev(self.x, self.y, z_partner(self.z, k), self.c)
        return self.copy(0, self.zs.at[k - 1], t, local=True)

    def over_x(self, k):
        t = dev(1 - self.x, self.y, self.z, self.c)
        return self.copy(k, self.xs.at[k], t, local=k == 0)

    def own_copy(self):
        return pltpu.make_async_copy(self.part, self.full.at[self.at(0)], self.own.at[0])

    def step0(self):
        for k in (3, 2, 1):
            self.over_z(k).start()
        self.over_x(0).start()
        self.own_copy().start()

    def step1(self):
        for k in (1, 2, 3):
            self.over_z(k).wait_recv()
            self.over_x(k).start()

    def step4(self):
        for k in range(4):
            self.over_x(k).wait()
        for k in (1, 2, 3):
            self.over_z(k).wait_send()
        self.own_copy().wait()


def gather_sems():
    dma = pltpu.SemaphoreType.DMA
    return [dma((3, 2)), dma((4, 2)), dma((8, 2)), dma((8, 2)), dma((8, 2)), dma((1,))]


def greet():
    x, y, z, c = place()
    barrier = pltpu.get_barrier_semaphore()
    near = [dev(x, y, z_partner(z, k), c) for k in (1, 2, 3)]
    near += [dev(1 - x, y, z, c), dev(x, 1 - y, z, c), dev(x, y, z, 1 - c)]
    for who in near:
        pl.semaphore_signal(barrier, inc=1, device_id=who, device_id_type=MESH)
    pl.semaphore_wait(barrier, len(near))


def edge_of(cols):
    return max(cols * 3 // 8 // 128 * 128, 128) if cols != 3072 else 1024


def gather_kernel(count, *refs):
    parts, refs = refs[: count + 1], refs[count + 1 :]
    fulls, scratch = refs[: count + 1], refs[count + 1 :]
    greet()
    gathers = [
        Gather(parts[i], fulls[i], edge_of(parts[i].shape[1]), scratch[6 * i : 6 * i + 6])
        for i in range(count)
    ]
    small = SmallGather(parts[count], fulls[count], *scratch[6 * count :])
    small.step0()
    steps = 4
    for turn in range(count + steps - 1):
        for step in range(steps - 1, -1, -1):
            i = turn - step
            if 0 <= i < count:
                getattr(gathers[i], f"step{step}")()
        if turn == 0:
            small.step1()
    for g in [small, *gathers]:
        g.step4()


def gather(parts, ident):
    dma = pltpu.SemaphoreType.DMA
    return pl.pallas_call(
        functools.partial(gather_kernel, len(parts) - 1),
        out_shape=[jax.ShapeDtypeStruct((p.shape[0] * 8, p.shape[1]), p.dtype) for p in parts],
        in_specs=[pl.BlockSpec(memory_space=pl.ANY)] * len(parts),
        out_specs=[pl.BlockSpec(memory_space=pl.ANY)] * len(parts),
        scratch_shapes=[s for _ in parts[1:] for s in gather_sems()]
        + [dma((3, 2)), dma((4, 2)), dma((1,))],
        compiler_params=pltpu.CompilerParams(collective_id=ident, has_side_effects=True),
    )(*parts)

def pair_perm(f):
    pairs = []
    for seq in range(4):
        for shard in range(8):
            y, c, z, x = seq // 2, seq % 2, shard // 2, shard % 2
            y, c, z, x = f(y, c, z, x)
            pairs.append((seq * 8 + shard, (y * 2 + c) * 8 + z * 2 + x))
    return pairs


BOTH = ("seq", "shard")
OVER_CORE = pair_perm(lambda y, c, z, x: (y, 1 - c, z, x))
OVER_X = pair_perm(lambda y, c, z, x: (y, c, z, 1 - x))
OVER_Y = pair_perm(lambda y, c, z, x: (1 - y, c, z, x))
OVER_Z = [None] + [pair_perm(lambda y, c, z, x, k=k: (y, c, z ^ k, x)) for k in (1, 2, 3)]


def send(value, perm):
    return lax.ppermute(value, BOTH, perm)


def pick(value, index, axis):
    return lax.dynamic_index_in_dim(value, index, axis, keepdims=False)


def add_low(left, right):
    return (left.astype(jnp.float32) + right.astype(jnp.float32)).astype(jnp.bfloat16)


def scatter_grad(left, right):
    x, y, z, c = place()
    tokens, rows = left.shape
    cols = right.shape[1]
    split = left.reshape(tokens, 2, 2, rows // 4)

    def part(core):
        chosen = pick(split, core, 2).reshape(tokens, rows // 2)
        return lax.dot_general(
            chosen, right, (((0,), (0,)), ((), ())), preferred_element_type=jnp.float32
        )

    arrived = send(part(1 - c).astype(jnp.bfloat16), OVER_CORE)
    low = (part(c) + arrived.astype(jnp.float32)).astype(jnp.bfloat16)
    low = low.reshape(2, 4, 2, rows // 32, cols)
    half = cols // 2
    first, second = low[..., :half], low[..., half:]
    got_first = send(pick(first, 1 - y, 0), OVER_Y)
    got_second = send(pick(second, 1 - x, 2), OVER_X)
    first = add_low(pick(first, y, 0), got_first)
    second = add_low(pick(second, x, 2), got_second)
    got_first = send(pick(first, 1 - x, 1), OVER_X)
    got_second = send(pick(second, 1 - y, 0), OVER_Y)
    first = pick(first, x, 1).astype(jnp.float32) + got_first.astype(jnp.float32)
    second = pick(second, y, 0).astype(jnp.float32) + got_second.astype(jnp.float32)
    whole = jnp.concatenate([first, second], axis=-1)
    low = whole.astype(jnp.bfloat16)
    total = pick(whole, z, 0)
    for k in (1, 2, 3):
        total += send(pick(low, z_partner(z, k), 0), OVER_Z[k]).astype(jnp.float32)
    return total


def sum_everywhere(value):
    for perm in (OVER_CORE, OVER_X, OVER_Y, OVER_Z[1], OVER_Z[2]):
        value = value + send(value, perm)
    return value


def on_chip(
    inputs,
    cotangent,
    first_gain,
    first_shift,
    joint_weight,
    joint_bias,
    output_weight,
    output_bias,
    second_gain,
    second_shift,
    expand_weight,
    expand_bias,
    reduce_weight,
    reduce_bias,
):
    x, y, z, c = place()
    tokens, width = inputs.shape[1:]
    heads = width // HEAD_DIM
    factor = HEAD_DIM ** (-0.5)
    smalls = [
        first_gain,
        first_shift,
        joint_bias,
        output_bias,
        second_gain,
        second_shift,
        expand_bias,
        reduce_bias,
    ]
    packed = jnp.concatenate([v.reshape(-1, 128) for v in smalls])
    packed = jnp.pad(packed, ((0, -packed.shape[0] % 16), (0, 0)))
    wj, wo, w1, w2, vectors = gather(
        [joint_weight, output_weight, expand_weight, reduce_weight, packed], 1
    )
    vectors = vectors.reshape(8, -1, 128).astype(jnp.float32)
    fulls, at = [], 0
    for v in smalls:
        rows = v.shape[0] // 128
        fulls.append(vectors[:, at : at + rows].reshape(-1))
        at += rows
    g1, s1, bj, bo, g2, s2, b1, b2 = fulls
    bias_full = jnp.concatenate([bj[:width], jnp.zeros((width,), jnp.float32), bj[width:]])

    def whole_image(value):
        own, got = pick(value, c, 0), send(pick(value, 1 - c, 0), OVER_CORE)
        return jnp.concatenate([jnp.where(c == 0, own, got), jnp.where(c == 0, got, own)])

    def own_tokens(value):
        parts = value.reshape(2, tokens, width)
        own, got = pick(parts, c, 0), send(pick(parts, 1 - c, 0), OVER_CORE)
        return jnp.stack([jnp.where(c == 0, own, got), jnp.where(c == 0, got, own)])

    xfull = whole_image(inputs).astype(jnp.float32)
    keep = (jnp.arange(LEN, dtype=jnp.int32) < VALID).astype(jnp.float32)[:, None]
    dout = whole_image(cotangent).astype(jnp.float32) * keep
    dout_low = dout.astype(jnp.bfloat16)
    normed1, first_back = jax.vjp(layer_norm, xfull, g1, s1)
    active1 = normed1.astype(jnp.bfloat16)
    joint = (jnp.dot(active1, wj, preferred_element_type=jnp.float32) + bias_full).astype(
        jnp.bfloat16
    )
    query, keys, values = jnp.moveaxis(joint.reshape(LEN, 3, heads, HEAD_DIM), 1, 0)

    def score_block(qpart, kpart):
        raw = jnp.einsum("qhd,khd->hqk", qpart, kpart, preferred_element_type=jnp.float32) * factor
        return jnp.where(keep[None, None, :, 0] > 0.5, raw, -1000000000.0)

    scores = score_block(query, keys)
    top = jnp.max(scores, axis=-1, keepdims=True)
    expo = jnp.exp(scores - top)
    total = jnp.sum(expo, axis=-1, keepdims=True)
    probs = expo / total
    logsum = top + jnp.log(total)
    context = jnp.einsum(
        "hqk,khd->qhd", probs.astype(jnp.bfloat16), values, preferred_element_type=jnp.float32
    )
    context = context.astype(jnp.bfloat16).reshape(LEN, width)
    attn = jnp.dot(context, wo, preferred_element_type=jnp.float32) + bo
    resid = xfull + attn
    normed2, second_back = jax.vjp(layer_norm, resid, g2, s2)
    active2 = normed2.astype(jnp.bfloat16)
    upper = jnp.dot(active2, w1, preferred_element_type=jnp.float32) + b1
    activated, gelu_back = jax.vjp(exact_gelu, upper)
    hidden = activated.astype(jnp.bfloat16)
    branch = jnp.dot(hidden, w2, preferred_element_type=jnp.float32) + b2
    result = resid + branch
    sums = jnp.stack(
        [
            jnp.sum(result * result * keep),
            jnp.sum(attn * attn * keep),
            jnp.sum(branch * branch * keep),
            jnp.sum(keep) * width,
        ]
    )
    layer_out = own_tokens(result.astype(jnp.bfloat16))
    own_w2 = scatter_grad(hidden, dout_low)
    grad_b2 = jnp.sum(dout, axis=0)

    def back(grad, matrix):
        return lax.dot_general(
            grad, matrix, (((1,), (1,)), ((), ())), preferred_element_type=jnp.float32
        )

    dupper = gelu_back(back(dout_low, w2))[0].astype(jnp.bfloat16)
    own_w1 = scatter_grad(active2, dupper)
    grad_b1 = jnp.sum(dupper.astype(jnp.float32), axis=0)
    dresid_norm, grad_g2, grad_s2 = second_back(back(dupper, w1))
    dresid = dout + dresid_norm
    dattn = dresid.astype(jnp.bfloat16)
    own_wo = scatter_grad(context, dattn)
    grad_bo = jnp.sum(dattn.astype(jnp.float32), axis=0)
    dcontext = back(dattn, wo).astype(jnp.bfloat16).reshape(LEN, heads, HEAD_DIM)
    probs = jnp.exp(score_block(query, keys) - logsum)
    dprobs = jnp.einsum("qhd,khd->hqk", dcontext, values, preferred_element_type=jnp.float32)
    dscore = probs * (dprobs - jnp.sum(probs * dprobs, axis=-1, keepdims=True))
    dscore = dscore.astype(jnp.bfloat16)
    dquery = jnp.einsum("hqk,khd->qhd", dscore, keys, preferred_element_type=jnp.float32)
    dkeys = jnp.einsum("hqk,qhd->khd", dscore, query, preferred_element_type=jnp.float32)
    dvalues = jnp.einsum(
        "hqk,qhd->khd", probs.astype(jnp.bfloat16), dcontext, preferred_element_type=jnp.float32
    )
    djoint = jnp.stack([dquery * factor, dkeys * factor, dvalues], axis=1).astype(jnp.bfloat16)
    djoint = djoint.reshape(LEN, 3 * width)
    own_wj = scatter_grad(active1, djoint)
    joint_sums = jnp.sum(djoint.astype(jnp.float32), axis=0)
    grad_bj = jnp.concatenate([joint_sums[:width], joint_sums[2 * width :]])
    dinput_norm, grad_g1, grad_s1 = first_back(back(djoint, wj))
    input_grad = own_tokens((dresid + dinput_norm).astype(jnp.bfloat16))
    grads = [grad_g1, grad_s1, grad_bj, grad_bo, grad_g2, grad_s2, grad_b1, grad_b2]
    totals = sum_everywhere(jnp.concatenate([*grads, jnp.pad(sums, (0, 124))]))
    rank = lax.axis_index("seq") * 8 + lax.axis_index("shard")
    own, at = [], 0
    for g in grads:
        size = g.shape[0]
        own.append(lax.dynamic_slice(totals, (at + rank * (size // 32),), (size // 32,)))
        at += size
    root_means = jnp.sqrt(totals[at : at + 3] / totals[at + 3] + 1e-06)
    own_g1, own_s1, own_bj, own_bo, own_g2, own_s2, own_b1, own_b2 = own
    return (
        layer_out,
        input_grad,
        own_g1,
        own_s1,
        own_wj,
        own_bj,
        own_wo,
        own_bo,
        own_g2,
        own_s2,
        own_w1,
        own_b1,
        own_w2,
        own_b2,
        root_means,
    )


def solution(mesh):
    whole_images = mesh.shape["seq"] == 4 and mesh.shape["shard"] == 8
    return jax.shard_map(
        on_chip if whole_images else on_device,
        mesh=mesh,
        in_specs=(
            P("shard", "seq", None),
            P("shard", "seq", None),
            P("shard"),
            P("shard"),
            P("shard", None),
            P("shard"),
            P("shard", None),
            P("shard"),
            P("shard"),
            P("shard"),
            P("shard", None),
            P("shard"),
            P("shard", None),
            P("shard"),
        ),
        out_specs=(
            P("shard", "seq", None),
            P("shard", "seq", None),
            P(("seq", "shard")),
            P(("seq", "shard")),
            P(("seq", "shard"), None),
            P(("seq", "shard")),
            P(("seq", "shard"), None),
            P(("seq", "shard")),
            P(("seq", "shard")),
            P(("seq", "shard")),
            P(("seq", "shard"), None),
            P(("seq", "shard")),
            P(("seq", "shard"), None),
            P(("seq", "shard")),
            P(),
        ),
        check_vma=False,
    )
```

```python
import functools

import jax
import jax.numpy as jnp
from jax import lax
from jax.experimental import pallas as pl
from jax.experimental.pallas import tpu as pltpu
from jax.sharding import PartitionSpec as P

MESH = pl.DeviceIdType.MESH
F32 = jnp.float32
LOW = jnp.bfloat16
HEAD_DIM = 64
LEN = 592
VALID = 577
PACK = 2
CUT = VALID // 16 * 16
SLOTS = 8
LEAD = (0, 2, 3, 4, 6)
VMEM_LIMIT = 58 << 20


def layer_norm(value, gain, shift):
    center = value - jnp.mean(value, axis=-1, keepdims=True)
    spread = jnp.mean(center * center, axis=-1, keepdims=True)
    return center * lax.rsqrt(spread + 1e-06) * gain + shift


def weight_grad(left, right):
    return lax.dot_general(
        left, right, (((0, 1), (0, 1)), ((), ())), preferred_element_type=jnp.float32
    )


def back_product(grad, matrix):
    return lax.dot_general(
        grad, matrix, (((2,), (1,)), ((), ())), preferred_element_type=jnp.float32
    )


def exact_gelu(value):
    return jax.nn.gelu(value, approximate=False)


def on_device(
    inputs,
    cotangent,
    first_gain,
    first_shift,
    joint_weight,
    joint_bias,
    output_weight,
    output_bias,
    second_gain,
    second_shift,
    expand_weight,
    expand_bias,
    reduce_weight,
    reduce_bias,
):
    images = inputs.shape[0]
    tokens = inputs.shape[1]
    full_seq = PACK * LEN
    pieces = images * PACK
    factor = HEAD_DIM ** (-0.5)
    begin = lax.axis_index("seq") * tokens
    local_places = begin + jnp.arange(tokens, dtype=jnp.int32)
    local_row = (local_places % LEN < VALID).astype(jnp.float32)
    local_mask = jnp.broadcast_to(local_row[None, :], (images, tokens))
    key_keep = jnp.arange(LEN, dtype=jnp.int32) < VALID
    weighting = local_mask[:, :, None]
    g1w, s1w, wj, bj, wo, bo, g2w, s2w, w1, b1, w2, b2 = (
        lax.all_gather(first_gain, "shard", axis=0, tiled=True),
        lax.all_gather(first_shift, "shard", axis=0, tiled=True),
        lax.all_gather(joint_weight, "shard", axis=0, tiled=True),
        lax.all_gather(joint_bias, "shard", axis=0, tiled=True),
        lax.all_gather(output_weight, "shard", axis=0, tiled=True),
        lax.all_gather(output_bias, "shard", axis=0, tiled=True),
        lax.all_gather(second_gain, "shard", axis=0, tiled=True),
        lax.all_gather(second_shift, "shard", axis=0, tiled=True),
        lax.all_gather(expand_weight, "shard", axis=0, tiled=True),
        lax.all_gather(expand_bias, "shard", axis=0, tiled=True),
        lax.all_gather(reduce_weight, "shard", axis=0, tiled=True),
        lax.all_gather(reduce_bias, "shard", axis=0, tiled=True),
    )
    g1f = g1w.astype(jnp.float32)
    s1f = s1w.astype(jnp.float32)
    bjf = bj.astype(jnp.float32)
    bof = bo.astype(jnp.float32)
    g2f = g2w.astype(jnp.float32)
    s2f = s2w.astype(jnp.float32)
    b1f = b1.astype(jnp.float32)
    b2f = b2.astype(jnp.float32)
    width = g1f.shape[0]
    xfull = inputs.astype(jnp.float32)
    normed1, first_back = jax.vjp(layer_norm, xfull, g1f, s1f)
    active1 = normed1.astype(jnp.bfloat16)
    bias_full = jnp.concatenate([bjf[:width], jnp.zeros((width,), jnp.float32), bjf[width:]])
    joint = (jnp.dot(active1, wj, preferred_element_type=jnp.float32) + bias_full).astype(
        jnp.bfloat16
    )
    joint = joint.reshape(images, tokens, 3, width)
    heads = lax.all_to_all(joint, "seq", split_axis=3, concat_axis=1, tiled=True)
    local_width = heads.shape[3]
    local_heads = local_width // HEAD_DIM
    query = heads[:, :, 0].reshape(pieces, LEN, local_heads, HEAD_DIM)
    keys = heads[:, :, 1].reshape(pieces, LEN, local_heads, HEAD_DIM)
    values = heads[:, :, 2].reshape(pieces, LEN, local_heads, HEAD_DIM)

    def score_block(qpart, kpart):
        raw = jnp.einsum("qhd,khd->hqk", qpart, kpart, preferred_element_type=jnp.float32) * factor
        return jnp.where(key_keep[None, None, :], raw, -1000000000.0)

    def attend(item):
        qpart, kpart, vpart = item
        scores = score_block(qpart, kpart)
        top = jnp.max(scores, axis=-1, keepdims=True)
        expo = jnp.exp(scores - top)
        total = jnp.sum(expo, axis=-1, keepdims=True)
        probs = expo / total
        logsum = (top + jnp.log(total))[:, :, 0]
        context = jnp.einsum(
            "hqk,khd->qhd", probs.astype(jnp.bfloat16), vpart, preferred_element_type=jnp.float32
        )
        return (context.astype(jnp.bfloat16).reshape(LEN, local_width), logsum)

    context, logsums = lax.map(attend, (query, keys, values))
    context = context.reshape(images, full_seq, local_width)
    gathered_ctx = lax.all_to_all(context, "seq", split_axis=1, concat_axis=2, tiled=True)
    attn = jnp.dot(gathered_ctx, wo, preferred_element_type=jnp.float32) + bof
    resid = xfull + attn
    normed2, second_back = jax.vjp(layer_norm, resid, g2f, s2f)
    active2 = normed2.astype(jnp.bfloat16)
    upper = jnp.dot(active2, w1, preferred_element_type=jnp.float32) + b1f
    activated, gelu_back = jax.vjp(exact_gelu, upper)
    hidden = activated.astype(jnp.bfloat16)
    branch = jnp.dot(hidden, w2, preferred_element_type=jnp.float32) + b2f
    result = resid + branch
    sums = jnp.stack(
        [
            jnp.sum(result * result * weighting),
            jnp.sum(attn * attn * weighting),
            jnp.sum(branch * branch * weighting),
        ]
    )
    counted = jnp.sum(local_mask) * width
    total_sums, total_count = lax.psum((sums, counted), ("seq", "shard"))
    root_means = jnp.sqrt(total_sums / total_count + 1e-06)
    wj, wo, w1, w2 = (
        lax.all_gather(joint_weight, "shard", axis=0, tiled=True),
        lax.all_gather(output_weight, "shard", axis=0, tiled=True),
        lax.all_gather(expand_weight, "shard", axis=0, tiled=True),
        lax.all_gather(reduce_weight, "shard", axis=0, tiled=True),
    )
    dout = cotangent.astype(jnp.float32) * weighting
    dout_low = dout.astype(jnp.bfloat16)
    grad_w2 = weight_grad(hidden, dout_low)
    grad_b2 = jnp.sum(dout, axis=(0, 1))
    dhidden = back_product(dout_low, w2)
    dupper = gelu_back(dhidden)[0].astype(jnp.bfloat16)
    grad_w1 = weight_grad(active2, dupper)
    grad_b1 = jnp.sum(dupper.astype(jnp.float32), axis=(0, 1))
    dactive2 = back_product(dupper, w1)
    dresid_norm, grad_g2, grad_s2 = second_back(dactive2)
    dresid = dout + dresid_norm
    dattn = dresid.astype(jnp.bfloat16)
    grad_wo = weight_grad(gathered_ctx, dattn)
    grad_bo = jnp.sum(dattn.astype(jnp.float32), axis=(0, 1))
    dcontext = back_product(dattn, wo).astype(jnp.bfloat16)
    dctx_heads = lax.all_to_all(dcontext, "seq", split_axis=2, concat_axis=1, tiled=True)
    dctx_heads = dctx_heads.reshape(pieces, LEN, local_heads, HEAD_DIM)

    def attend_back(item):
        qpart, kpart, vpart, logsum, dpart = item
        scores = score_block(qpart, kpart)
        probs = jnp.exp(scores - logsum[:, :, None])
        dprobs = jnp.einsum("qhd,khd->hqk", dpart, vpart, preferred_element_type=jnp.float32)
        dscore = (probs * (dprobs - jnp.sum(probs * dprobs, axis=-1, keepdims=True))).astype(
            jnp.bfloat16
        )
        dquery = (
            jnp.einsum("hqk,khd->qhd", dscore, kpart, preferred_element_type=jnp.float32) * factor
        )
        dkeys = (
            jnp.einsum("hqk,qhd->khd", dscore, qpart, preferred_element_type=jnp.float32) * factor
        )
        dvalues = jnp.einsum(
            "hqk,qhd->khd", probs.astype(jnp.bfloat16), dpart, preferred_element_type=jnp.float32
        )
        stacked = jnp.stack([dquery, dkeys, dvalues], axis=1).astype(jnp.bfloat16)
        return stacked.reshape(LEN, 3, local_width)

    dheads = lax.map(attend_back, (query, keys, values, logsums, dctx_heads))
    dheads = dheads.reshape(images, full_seq, 3, local_width)
    djoint = lax.all_to_all(dheads, "seq", split_axis=1, concat_axis=3, tiled=True)
    djoint = djoint.reshape(images, tokens, 3 * width)
    grad_wj = weight_grad(active1, djoint)
    joint_sums = jnp.sum(djoint.astype(jnp.float32), axis=(0, 1))
    grad_bj = jnp.concatenate([joint_sums[:width], joint_sums[2 * width :]])
    dactive1 = back_product(djoint, wj)
    dinput_norm, grad_g1, grad_s1 = first_back(dactive1)
    dinput = (dresid + dinput_norm).astype(jnp.bfloat16)
    (
        own_g1,
        own_s1,
        own_wj,
        own_bj,
        own_wo,
        own_bo,
        own_g2,
        own_s2,
        own_w1,
        own_b1,
        own_w2,
        own_b2,
    ) = (
        lax.psum_scatter(grad_g1, ("seq", "shard"), scatter_dimension=0, tiled=True),
        lax.psum_scatter(grad_s1, ("seq", "shard"), scatter_dimension=0, tiled=True),
        lax.psum_scatter(grad_wj, ("seq", "shard"), scatter_dimension=0, tiled=True),
        lax.psum_scatter(grad_bj, ("seq", "shard"), scatter_dimension=0, tiled=True),
        lax.psum_scatter(grad_wo, ("seq", "shard"), scatter_dimension=0, tiled=True),
        lax.psum_scatter(grad_bo, ("seq", "shard"), scatter_dimension=0, tiled=True),
        lax.psum_scatter(grad_g2, ("seq", "shard"), scatter_dimension=0, tiled=True),
        lax.psum_scatter(grad_s2, ("seq", "shard"), scatter_dimension=0, tiled=True),
        lax.psum_scatter(grad_w1, ("seq", "shard"), scatter_dimension=0, tiled=True),
        lax.psum_scatter(grad_b1, ("seq", "shard"), scatter_dimension=0, tiled=True),
        lax.psum_scatter(grad_w2, ("seq", "shard"), scatter_dimension=0, tiled=True),
        lax.psum_scatter(grad_b2, ("seq", "shard"), scatter_dimension=0, tiled=True),
    )
    return (
        result.astype(jnp.bfloat16),
        dinput,
        own_g1,
        own_s1,
        own_wj,
        own_bj,
        own_wo,
        own_bo,
        own_g2,
        own_s2,
        own_w1,
        own_b1,
        own_w2,
        own_b2,
        root_means,
    )


def place():
    seq = lax.axis_index("seq")
    shard = lax.axis_index("shard")
    return lax.rem(shard, 2), lax.div(seq, 2), lax.div(shard, 2), lax.rem(seq, 2)


def z_partner(z, k):
    if k == 0:
        return z
    if k == 1:
        return z + 1 - 2 * lax.rem(z, 2)
    if k == 2:
        return lax.rem(z + 2, 4)
    return 3 - z


def dev(x, y, z, c):
    return (y * 2 + c, z * 2 + x)


def remote(src, dst, sem, target):
    return pltpu.make_async_remote_copy(
        src_ref=src,
        dst_ref=dst,
        send_sem=sem.at[0],
        recv_sem=sem.at[1],
        device_id=target,
        device_id_type=MESH,
    )


def greet():
    x, y, z, c = place()
    barrier = pltpu.get_barrier_semaphore()
    near = [dev(x, y, z_partner(z, k), c) for k in (1, 2, 3)]
    near += [dev(1 - x, y, z, c), dev(x, 1 - y, z, c), dev(x, y, z, 1 - c)]
    for who in near:
        pl.semaphore_signal(barrier, inc=1, device_id=who, device_id_type=MESH)
    pl.semaphore_wait(barrier, len(near))


class Gather:
    def __init__(self, part, full, piece, sems, slot):
        self.part, self.full = part, full
        self.zs, self.xs, self.ys, self.cs, self.es, self.own = [s.at[slot] for s in sems]
        self.shard_rows = part.shape[0]
        self.row, self.rows, self.col, self.cols = piece
        edge = self.cols * 3 // 8 // 128 * 128
        span = self.cols - edge
        self.x, self.y, self.z, self.c = place()
        self.duty = pl.ds(pl.multiple_of(self.col + self.y * edge, 128), span)
        self.mine = pl.ds(pl.multiple_of(self.col + self.y * span, 128), edge)
        self.other = pl.ds(pl.multiple_of(self.col + (1 - self.y) * span, 128), edge)

    def half(self, k, j):
        x = self.x if j == 0 else 1 - self.x
        shard = z_partner(self.z, k) * 2 + x
        half = self.rows // 2
        first = shard * self.shard_rows + self.row + self.c * half
        return pl.ds(pl.multiple_of(first, 16), half)

    def copy(self, k, j, cols, sem, target, local=False):
        at = (self.half(k, j), cols)
        src = self.full.at[at]
        if local:
            half = self.rows // 2
            src = self.part.at[pl.ds(pl.multiple_of(self.row + self.c * half, 16), half), cols]
        return remote(src, self.full.at[at], sem, target)

    def over_z(self, k):
        target = dev(self.x, self.y, z_partner(self.z, k), self.c)
        return self.copy(0, 0, self.duty, self.zs.at[k - 1], target, local=True)

    def over_x(self, k):
        target = dev(1 - self.x, self.y, self.z, self.c)
        return self.copy(k, 0, self.duty, self.xs.at[k], target, local=k == 0)

    def over_y(self, k, j):
        target = dev(self.x, 1 - self.y, self.z, self.c)
        return self.copy(k, j, self.mine, self.ys.at[k * 2 + j], target)

    def over_core(self, k, j):
        target = dev(self.x, self.y, self.z, 1 - self.c)
        return self.copy(k, j, self.duty, self.cs.at[k * 2 + j], target)

    def over_core_rest(self, k, j):
        target = dev(self.x, self.y, self.z, 1 - self.c)
        return self.copy(k, j, self.other, self.es.at[k * 2 + j], target)

    def own_copy(self):
        shard = self.z * 2 + self.x
        cols = pl.ds(self.col, self.cols)
        rows = pl.ds(pl.multiple_of(shard * self.shard_rows + self.row, 16), self.rows)
        src = self.part.at[pl.ds(self.row, self.rows), cols]
        return pltpu.make_async_copy(src, self.full.at[rows, cols], self.own.at[0])

    def step0(self):
        for k in (1, 2, 3):
            self.over_z(k).start()
        self.over_x(0).start()
        self.own_copy().start()

    def step1(self):
        for k in (1, 2, 3):
            self.over_z(k).wait_recv()
            self.over_x(k).start()
            self.over_y(k, 0).start()
            self.over_core(k, 0).start()

    def step2(self):
        for k in (0, 1, 2, 3):
            self.over_x(k).wait_recv()
            self.over_y(k, 1).start()
            self.over_core(k, 1).start()

    def others(self):
        return [(k, 0) for k in (1, 2, 3)] + [(k, 1) for k in (0, 1, 2, 3)]

    def step3(self):
        for k, j in self.others():
            self.over_y(k, j).wait_recv()
            self.over_core_rest(k, j).start()

    def step4(self):
        for k, j in self.others():
            self.over_core(k, j).wait()
            self.over_core_rest(k, j).wait()
            self.over_y(k, j).wait_send()
        for k in (1, 2, 3):
            self.over_z(k).wait_send()
        for k in range(4):
            self.over_x(k).wait_send()
        self.own_copy().wait()


class SmallGather:
    def __init__(self, part, full, zs, xs, own):
        self.part, self.full, self.zs, self.xs, self.own = part, full, zs, xs, own
        self.x, self.y, self.z, self.c = place()

    def at(self, k):
        rows = self.part.shape[0]
        shard = z_partner(self.z, k) * 2 + self.x
        return pl.ds(pl.multiple_of(shard * rows, rows), rows)

    def over_z(self, k):
        target = dev(self.x, self.y, z_partner(self.z, k), self.c)
        return remote(self.part, self.full.at[self.at(0)], self.zs.at[k - 1], target)

    def over_x(self, k):
        target = dev(1 - self.x, self.y, self.z, self.c)
        src = self.full.at[self.at(k)] if k else self.part
        return remote(src, self.full.at[self.at(k)], self.xs.at[k], target)

    def own_copy(self):
        return pltpu.make_async_copy(self.part, self.full.at[self.at(0)], self.own.at[0])

    def step0(self):
        for k in (1, 2, 3):
            self.over_z(k).start()
        self.over_x(0).start()
        self.own_copy().start()

    def step1(self):
        for k in (1, 2, 3):
            self.over_z(k).wait_recv()
            self.over_x(k).start()

    def step4(self):
        for k in range(4):
            self.over_x(k).wait()
        for k in (1, 2, 3):
            self.over_z(k).wait_send()
        self.own_copy().wait()


def dot(left, right, left_axis=1, right_axis=0):
    return lax.dot_general(
        left,
        right,
        (((left_axis,), (right_axis,)), ((), ())),
        preferred_element_type=F32,
    )


def norm_parts(value):
    center = value - jnp.mean(value, axis=-1, keepdims=True)
    inverse = lax.rsqrt(jnp.mean(center * center, axis=-1, keepdims=True) + 1e-06)
    return center * inverse, inverse


def norm_back(grad, gain, hat, inverse):
    scaled = grad * gain
    mean = jnp.mean(scaled, axis=-1, keepdims=True)
    return inverse * (scaled - mean - hat * jnp.mean(scaled * hat, axis=-1, keepdims=True))


def keep_keys(scores):
    row = lax.broadcasted_iota(jnp.int32, (LEN - CUT, scores.shape[1]), 0) + CUT
    last = jnp.where(row < VALID, scores[CUT:], -1000000000.0)
    return jnp.concatenate([scores[:CUT], last], axis=0)


def by_head(value):
    lane = lax.broadcasted_iota(jnp.int32, value.shape, 1)
    none = jnp.zeros_like(value)
    return jnp.where(lane < HEAD_DIM, value, none), jnp.where(lane < HEAD_DIM, none, value)


def attend_pair(query, keys, values, store_logsum):
    total_ctx = None
    for i, (q, v) in enumerate(zip(by_head(query), by_head(values))):
        scores = keep_keys(dot(keys, q, 1, 1))
        top = jnp.max(scores, axis=0, keepdims=True)
        expo = jnp.exp(scores - top)
        total = jnp.sum(expo, axis=0, keepdims=True)
        store_logsum(i, top + jnp.log(total))
        ctx = dot((expo * (1.0 / total)).astype(LOW), v, 0, 0)
        total_ctx = ctx if total_ctx is None else total_ctx + ctx
    return total_ctx


def vector_row(table, rows, first, count):
    at = [s * rows + first + i for s in range(8) for i in range(count)]
    pieces = [table[r : r + 1] for r in at]
    return jnp.concatenate(pieces, axis=1)


def front_plan(shapes):
    (dj, cj), (do, co), (de, ce), (dr, cr) = shapes
    plan = [(0, (0, dj, i * (cj // 3), cj // 3)) for i in range(3)]
    plan += [(1, (0, do, 0, co))]
    plan += [(2, (0, de, i * (ce // 4), ce // 4)) for i in range(4)]
    plan += [(3, (i * (dr // 4), dr // 4, 0, cr)) for i in range(4)]
    return plan


def front_kernel(x_part, packed, wj, wo, w1, w2, *refs):
    outs, refs = refs[:9], refs[9:]
    fulls, (table_out, image, active, joint, ctx) = outs[:4], outs[4:]
    (logsum, table, own_half, far_half, weight, xf, *sems) = refs
    parts = (wj, wo, w1, w2)
    half_sem, fetch_sem, small_sems, sems = sems[0], sems[1], sems[2:5], sems[5:]
    x, y, z, c = place()
    greet()
    small = SmallGather(packed, table, *small_sems)
    small.step0()
    swap = remote(x_part.at[1 - c], far_half, half_sem.at[0], dev(x, y, z, 1 - c))
    keep = pltpu.make_async_copy(x_part.at[c], own_half, half_sem.at[1, 0])
    swap.start()
    keep.start()
    plan = front_plan([p.shape for p in parts])
    pieces = [
        Gather(parts[w], fulls[w], piece, sems, i % SLOTS) for i, (w, piece) in enumerate(plan)
    ]
    turns = len(pieces) + LEAD[4]

    def turn(t):
        for step in (4, 3, 2, 1, 0):
            i = t - LEAD[step]
            if 0 <= i < len(pieces):
                getattr(pieces[i], f"step{step}")()

    width = active.shape[1]
    for t in range(9):
        turn(t)
        if t == 1:
            small.step1()
        if t == 2:
            keep.wait()
            swap.wait()
            own, far = own_half[...].astype(F32), far_half[...].astype(F32)
            first, second = jnp.where(c == 0, own, far), jnp.where(c == 0, far, own)
            xf[...] = jnp.concatenate([first, second], axis=0)
            image[...] = xf[...].astype(LOW)
        if t == 3:
            small.step4()
            table_out[...] = table[...]
            rows = packed.shape[0]
            hat, _ = norm_parts(xf[...])
            vectors = table[...].astype(F32)
            gain, shift = vector_row(vectors, rows, 0, 1), vector_row(vectors, rows, 1, 1)
            active[...] = (hat * gain + shift).astype(LOW)
        if t >= 6:
            cols = pl.ds((t - 6) * width, width)
            fetch = pltpu.make_async_copy(fulls[0].at[:, cols], weight, fetch_sem.at[0])
            fetch.start()
            fetch.wait()
            product = dot(active[...], weight[...])
            if t != 7:
                bias = vector_row(table[...].astype(F32), packed.shape[0], 2, 2)
                product += bias[:, :width] if t == 6 else bias[:, width:]
            joint[:, cols] = product.astype(LOW)

    @pl.loop(0, turns - 9)
    def _(t):
        for k in range(turns - 9):
            pl.when(t == k)(functools.partial(turn, k + 9))

        @pl.when(t < width // 128)
        def _():
            def at(i):
                return pl.ds(pl.multiple_of(i * width + t * 128, 128), 128)

            def store(i, value):
                logsum[t, i : i + 1, :] = value

            query = joint[:, at(0)] * jnp.asarray(HEAD_DIM**-0.5, LOW)
            ctx[:, at(0)] = attend_pair(query, joint[:, at(1)], joint[:, at(2)], store).astype(LOW)


def front(x_part, packed, parts):
    sds = jax.ShapeDtypeStruct
    dma = pltpu.SemaphoreType.DMA
    tokens, width = x_part.shape[1:]
    pairs = width // 128
    hbm, vmem = pl.BlockSpec(memory_space=pl.ANY), pl.BlockSpec(memory_space=pltpu.VMEM)
    return pl.pallas_call(
        front_kernel,
        out_shape=[sds((p.shape[0] * 8, p.shape[1]), LOW) for p in parts]
        + [
            sds((packed.shape[0] * 8, 128), LOW),
            sds((LEN, width), LOW),
            sds((LEN, width), LOW),
            sds((LEN, 3 * width), LOW),
            sds((LEN, width), LOW),
            sds((pairs, 8, LEN), F32),
        ],
        in_specs=[hbm] * 6,
        out_specs=[hbm] * 4 + [vmem] * 6,
        scratch_shapes=[
            pltpu.VMEM((packed.shape[0] * 8, 128), LOW),
            pltpu.VMEM((tokens, width), LOW),
            pltpu.VMEM((tokens, width), LOW),
            pltpu.VMEM((width, width), LOW),
            pltpu.VMEM((LEN, width), F32),
            dma((2, 2)),
            dma((1,)),
            dma((3, 2)),
            dma((4, 2)),
            dma((1,)),
            dma((SLOTS, 3, 2)),
            dma((SLOTS, 4, 2)),
            dma((SLOTS, 8, 2)),
            dma((SLOTS, 8, 2)),
            dma((SLOTS, 8, 2)),
            dma((SLOTS, 1)),
        ],
        compiler_params=pltpu.CompilerParams(
            collective_id=1, has_side_effects=True, vmem_limit_bytes=VMEM_LIMIT
        ),
    )(x_part, packed, *parts)


def middle_kernel(
    chunks,
    ctx,
    image,
    dout,
    wo,
    rows,
    w1,
    b1,
    w2,
    out,
    hidden,
    dupper,
    active,
    dattn,
    dresid,
    dctx,
    small,
    grad_b1,
    resid,
    total,
    dtotal,
):
    j = pl.program_id(0)
    bo, gain, shift, b2 = rows[0:1], rows[1:2], rows[2:3], rows[3:4]
    keep = (lax.broadcasted_iota(jnp.int32, (LEN, 1), 0) < VALID).astype(F32)

    @pl.when(j == 0)
    def _():
        attn = dot(ctx[...], wo[...]) + bo
        value = image[...].astype(F32) + attn
        resid[...] = value
        hat, _ = norm_parts(value)
        active[...] = (hat * gain + shift).astype(LOW)
        total[...] = jnp.zeros_like(total)
        dtotal[...] = jnp.zeros_like(dtotal)
        small[3:4] = jnp.sum(dout[...].astype(F32), axis=0, keepdims=True)
        small[4:5] = jnp.sum(attn * attn * keep, axis=0, keepdims=True)
        small[7:8] = jnp.zeros_like(small[7:8])

    upper = dot(active[...], w1[...]) + b1[...]
    dhidden = dot(dout[...], w2[...], 1, 1)
    share = 0.5 * (1.0 + lax.erf(upper * 0.7071067811865476))
    density = jnp.exp(upper * upper * -0.5) * 0.3989422804014327
    low = (upper * share).astype(LOW)
    dlow = (dhidden * (share + upper * density)).astype(LOW)
    hidden[...] = low
    dupper[...] = dlow
    grad_b1[...] = jnp.sum(dlow.astype(F32), axis=0, keepdims=True)
    total[...] += dot(low, w2[...])
    dtotal[...] += dot(dlow, w1[...], 1, 1)

    @pl.when(j == chunks - 1)
    def _():
        branch = total[...] + b2
        value = resid[...]
        result = value + branch
        out[...] = result.astype(LOW)
        small[5:6] = jnp.sum(result * result * keep, axis=0, keepdims=True)
        small[6:7] = jnp.sum(branch * branch * keep, axis=0, keepdims=True)
        hat, inverse = norm_parts(value)
        dactive = dtotal[...]
        small[0:1] = jnp.sum(dactive * hat, axis=0, keepdims=True)
        small[1:2] = jnp.sum(dactive, axis=0, keepdims=True)
        grad = dout[...].astype(F32) + norm_back(dactive, gain, hat, inverse)
        dresid[...] = grad
        low = grad.astype(LOW)
        dattn[...] = low
        small[2:3] = jnp.sum(low.astype(F32), axis=0, keepdims=True)
        dctx[...] = dot(low, wo[...], 1, 1).astype(LOW)


def middle(ctx, image, dout, wo, rows, w1, b1, w2, step=512):
    width, hidden = w1.shape
    sds = jax.ShapeDtypeStruct
    full, wide = (LEN, width), (LEN, hidden)

    def whole(shape):
        return pl.BlockSpec(shape, lambda j: (0, 0))

    def by_column(size):
        return pl.BlockSpec((size, step), lambda j: (0, j))

    return pl.pallas_call(
        functools.partial(middle_kernel, hidden // step),
        grid=(hidden // step,),
        in_specs=[whole(full)] * 3
        + [whole((width, width)), whole((8, width)), by_column(width), by_column(1)]
        + [pl.BlockSpec((step, width), lambda j: (j, 0))],
        out_specs=[whole(full), by_column(LEN), by_column(LEN)]
        + [whole(full)] * 4
        + [whole((8, width)), by_column(1)],
        out_shape=[sds(full, LOW), sds(wide, LOW), sds(wide, LOW)]
        + [sds(full, LOW), sds(full, LOW), sds(full, F32), sds(full, LOW)]
        + [sds((8, width), F32), sds((1, hidden), F32)],
        scratch_shapes=[pltpu.VMEM(full, F32)] * 3,
        compiler_params=pltpu.CompilerParams(vmem_limit_bytes=VMEM_LIMIT),
        cost_estimate=pl.CostEstimate(
            flops=12 * LEN * width * hidden,
            bytes_accessed=4 * width * hidden + 4 * LEN * hidden + 24 * LEN * width,
            transcendentals=2 * LEN * hidden,
        ),
    )(ctx, image, dout, wo, rows, w1, b1, w2)


def attend_pair_back(query, keys, values, logsum, dctx):
    heads = [by_head(v) for v in (query, keys, dctx)]
    sums = None
    for i in range(2):
        q, k, d = [h[i] for h in heads]
        probs = jnp.exp(keep_keys(dot(keys, q, 1, 1)) - logsum[i : i + 1])
        dprobs = dot(values, d, 1, 1)
        inner = jnp.sum(probs * dprobs, axis=0, keepdims=True)
        dscore = (probs * (dprobs - inner)).astype(LOW)
        grads = (dot(dscore, k, 0, 0), dot(dscore, q), dot(probs.astype(LOW), d))
        sums = grads if sums is None else tuple(a + b for a, b in zip(sums, grads))
    return sums


def attention_back_kernel(query, keys, values, logsum, dctx, djoint):
    h = pl.program_id(0)
    factor = HEAD_DIM**-0.5
    scaled = query[...] * jnp.asarray(factor, LOW)
    dq, dk, dv = attend_pair_back(scaled, keys[...], values[...], logsum[0], dctx[...])
    width = djoint.shape[1] // 3
    for i, grad in enumerate((dq * factor, dk, dv)):
        djoint[:, pl.ds(pl.multiple_of(i * width + h * 128, 128), 128)] = grad.astype(LOW)


def attention_back(joint, logsum, dctx):
    width = dctx.shape[1]
    pairs = width // 128

    def column(i):
        return pl.BlockSpec((LEN, 128), lambda h: (0, i * pairs + h))

    return pl.pallas_call(
        attention_back_kernel,
        grid=(pairs,),
        in_specs=[column(0), column(1), column(2)]
        + [pl.BlockSpec((1, 8, LEN), lambda h: (h, 0, 0)), column(0)],
        out_specs=pl.BlockSpec((LEN, 3 * width), lambda h: (0, 0)),
        out_shape=jax.ShapeDtypeStruct((LEN, 3 * width), LOW),
        compiler_params=pltpu.CompilerParams(vmem_limit_bytes=VMEM_LIMIT),
        cost_estimate=pl.CostEstimate(
            flops=20 * LEN * LEN * width,
            bytes_accessed=16 * LEN * width,
            transcendentals=LEN * LEN * 2 * pairs,
        ),
    )(joint, joint, joint, logsum, dctx)


def pair_perm(f):
    pairs = []
    for seq in range(4):
        for shard in range(8):
            y, c, z, x = f(seq // 2, seq % 2, shard // 2, shard % 2)
            pairs.append((seq * 8 + shard, (y * 2 + c) * 8 + z * 2 + x))
    return pairs


BOTH = ("seq", "shard")
OVER_CORE = pair_perm(lambda y, c, z, x: (y, 1 - c, z, x))
OVER_X = pair_perm(lambda y, c, z, x: (y, c, z, 1 - x))
OVER_Y = pair_perm(lambda y, c, z, x: (1 - y, c, z, x))
OVER_Z = [None] + [pair_perm(lambda y, c, z, x, k=k: (y, c, z ^ k, x)) for k in (1, 2, 3)]


def send(value, perm):
    return lax.ppermute(value, BOTH, perm)


def pick(value, index, axis):
    return lax.dynamic_index_in_dim(value, index, axis, keepdims=False)


def add_low(left, right):
    return (left.astype(F32) + right.astype(F32)).astype(LOW)


def partial_grad(left, right):
    c = place()[3]
    tokens, rows = left.shape
    split = left.reshape(tokens, 2, 2, rows // 4)

    def part(core):
        return dot(pick(split, core, 2).reshape(tokens, rows // 2), right, 0, 0).astype(LOW)

    return part(1 - c), part(c)


def scatter_grad(theirs, low):
    x, y, z, c = place()
    rows, cols = low.shape
    low = add_low(low, send(theirs, OVER_CORE))
    low = low.reshape(2, 4, 2, rows // 16, cols)
    half = cols // 2
    first, second = low[..., :half], low[..., half:]
    got_first = send(pick(first, 1 - y, 0), OVER_Y)
    got_second = send(pick(second, 1 - x, 2), OVER_X)
    first = add_low(pick(first, y, 0), got_first)
    second = add_low(pick(second, x, 2), got_second)
    got_first = send(pick(first, 1 - x, 1), OVER_X)
    got_second = send(pick(second, 1 - y, 0), OVER_Y)
    first = pick(first, x, 1).astype(F32) + got_first.astype(F32)
    second = pick(second, y, 0).astype(F32) + got_second.astype(F32)
    whole = jnp.concatenate([first, second], axis=-1)
    low = whole.astype(LOW)
    total = pick(whole, z, 0)
    for k in (1, 2, 3):
        total += send(pick(low, z_partner(z, k), 0), OVER_Z[k]).astype(F32)
    return total


def sum_everywhere(value):
    for perm in (OVER_CORE, OVER_X, OVER_Y, OVER_Z[1], OVER_Z[2]):
        value = value + send(value, perm)
    return value


def on_chip(
    inputs,
    cotangent,
    first_gain,
    first_shift,
    joint_weight,
    joint_bias,
    output_weight,
    output_bias,
    second_gain,
    second_shift,
    expand_weight,
    expand_bias,
    reduce_weight,
    reduce_bias,
):
    c = place()[3]
    tokens, width = inputs.shape[1:]
    smalls = [
        first_gain,
        first_shift,
        joint_bias,
        output_bias,
        second_gain,
        second_shift,
        expand_bias,
        reduce_bias,
    ]
    packed = jnp.concatenate([v.reshape(-1, 128) for v in smalls])
    packed = jnp.pad(packed, ((0, -packed.shape[0] % 16), (0, 0)))

    def whole_image(value):
        own, got = pick(value, c, 0), send(pick(value, 1 - c, 0), OVER_CORE)
        return jnp.concatenate([jnp.where(c == 0, own, got), jnp.where(c == 0, got, own)])

    def own_tokens(value):
        parts = value.reshape(2, tokens, width)
        own, got = pick(parts, c, 0), send(pick(parts, 1 - c, 0), OVER_CORE)
        return jnp.stack([jnp.where(c == 0, own, got), jnp.where(c == 0, got, own)])

    keep = jnp.arange(LEN, dtype=jnp.int32)[:, None] < VALID
    dout = jnp.where(keep, whole_image(cotangent), 0)
    wj, wo, w1, w2, vectors, image, active1, joint, context, logsum = front(
        inputs, packed, (joint_weight, output_weight, expand_weight, reduce_weight)
    )
    vectors = vectors.reshape(8, -1, 128).astype(F32)
    fulls, at = [], 0
    for v in smalls:
        rows = v.shape[0] // 128
        fulls.append(vectors[:, at : at + rows].reshape(-1))
        at += rows
    g1, s1, bj, bo, g2, s2, b1, b2 = fulls
    rows = jnp.pad(jnp.stack([bo, g2, s2, b2]), ((0, 4), (0, 0)))
    result, hidden, dupper, active2, dattn, dresid, dcontext, small, grad_b1 = middle(
        context, image, dout, wo, rows, w1, b1[None], w2
    )
    parts_w2 = partial_grad(hidden, dout)
    parts_w1 = partial_grad(active2, dupper)
    parts_wo = partial_grad(context, dattn)
    parts_w2, parts_w1, parts_wo, dcontext = lax.optimization_barrier(
        (parts_w2, parts_w1, parts_wo, dcontext)
    )
    own_w2, own_w1, own_wo = [scatter_grad(*p) for p in (parts_w2, parts_w1, parts_wo)]
    layer_out = own_tokens(result)
    djoint = attention_back(joint, logsum, dcontext)
    parts_wj = partial_grad(active1, djoint)
    own_wj = scatter_grad(*parts_wj)
    joint_sums = jnp.sum(djoint.astype(F32), axis=0)
    dactive = dot(djoint, wj, 1, 1)
    hat, inverse = norm_parts(image.astype(F32))
    grad_g1, grad_s1 = jnp.sum(dactive * hat, axis=0), jnp.sum(dactive, axis=0)
    dimage = dresid + norm_back(dactive, g1, hat, inverse)
    input_grad = own_tokens(dimage.astype(LOW))
    counted = jnp.full((1,), VALID * width, F32)
    grads = [grad_g1, grad_s1, joint_sums[:width], joint_sums[2 * width :]]
    grads += [small[2], small[0], small[1], grad_b1[0], small[3]]
    sums = [jnp.sum(small[i])[None] for i in (5, 4, 6)] + [counted]
    totals = sum_everywhere(jnp.concatenate(grads + sums + [jnp.zeros((124,), F32)]))
    rank = lax.axis_index("seq") * 8 + lax.axis_index("shard")
    own, at = [], 0
    for v in smalls:
        size = v.shape[0] * 8
        own.append(lax.dynamic_slice(totals, (at + rank * (size // 32),), (size // 32,)))
        at += size
    own_g1, own_s1, own_bj, own_bo, own_g2, own_s2, own_b1, own_b2 = own
    root_means = jnp.sqrt(totals[at : at + 3] / totals[at + 3] + 1e-06)
    return (
        layer_out,
        input_grad,
        own_g1,
        own_s1,
        own_wj,
        own_bj,
        own_wo,
        own_bo,
        own_g2,
        own_s2,
        own_w1,
        own_b1,
        own_w2,
        own_b2,
        root_means,
    )


def solution(mesh):
    whole_images = mesh.shape["seq"] == 4 and mesh.shape["shard"] == 8
    return jax.shard_map(
        on_chip if whole_images else on_device,
        mesh=mesh,
        in_specs=(
            P("shard", "seq", None),
            P("shard", "seq", None),
            P("shard"),
            P("shard"),
            P("shard", None),
            P("shard"),
            P("shard", None),
            P("shard"),
            P("shard"),
            P("shard"),
            P("shard", None),
            P("shard"),
            P("shard", None),
            P("shard"),
        ),
        out_specs=(
            P("shard", "seq", None),
            P("shard", "seq", None),
            P(("seq", "shard")),
            P(("seq", "shard")),
            P(("seq", "shard"), None),
            P(("seq", "shard")),
            P(("seq", "shard"), None),
            P(("seq", "shard")),
            P(("seq", "shard")),
            P(("seq", "shard")),
            P(("seq", "shard"), None),
            P(("seq", "shard")),
            P(("seq", "shard"), None),
            P(("seq", "shard")),
            P(),
        ),
        check_vma=False,
    )
```

```python
import functools

import jax
import jax.numpy as jnp
from jax import lax
from jax.experimental import pallas as pl
from jax.experimental.pallas import tpu as pltpu
from jax.sharding import PartitionSpec as P

MESH = pl.DeviceIdType.MESH
F32 = jnp.float32
LOW = jnp.bfloat16
HEAD_DIM = 64
LEN = 592
VALID = 577
PACK = 2
CUT = VALID // 16 * 16
SLOTS = 8
LEAD = (0, 2, 3, 4, 6)
VMEM_LIMIT = 60 << 20


def layer_norm(value, gain, shift):
    center = value - jnp.mean(value, axis=-1, keepdims=True)
    spread = jnp.mean(center * center, axis=-1, keepdims=True)
    return center * lax.rsqrt(spread + 1e-06) * gain + shift


def weight_grad(left, right):
    return lax.dot_general(
        left, right, (((0, 1), (0, 1)), ((), ())), preferred_element_type=jnp.float32
    )


def back_product(grad, matrix):
    return lax.dot_general(
        grad, matrix, (((2,), (1,)), ((), ())), preferred_element_type=jnp.float32
    )


def exact_gelu(value):
    return jax.nn.gelu(value, approximate=False)


def on_device(
    inputs,
    cotangent,
    first_gain,
    first_shift,
    joint_weight,
    joint_bias,
    output_weight,
    output_bias,
    second_gain,
    second_shift,
    expand_weight,
    expand_bias,
    reduce_weight,
    reduce_bias,
):
    images = inputs.shape[0]
    tokens = inputs.shape[1]
    full_seq = PACK * LEN
    pieces = images * PACK
    factor = HEAD_DIM ** (-0.5)
    begin = lax.axis_index("seq") * tokens
    local_places = begin + jnp.arange(tokens, dtype=jnp.int32)
    local_row = (local_places % LEN < VALID).astype(jnp.float32)
    local_mask = jnp.broadcast_to(local_row[None, :], (images, tokens))
    key_keep = jnp.arange(LEN, dtype=jnp.int32) < VALID
    weighting = local_mask[:, :, None]
    g1w, s1w, wj, bj, wo, bo, g2w, s2w, w1, b1, w2, b2 = (
        lax.all_gather(first_gain, "shard", axis=0, tiled=True),
        lax.all_gather(first_shift, "shard", axis=0, tiled=True),
        lax.all_gather(joint_weight, "shard", axis=0, tiled=True),
        lax.all_gather(joint_bias, "shard", axis=0, tiled=True),
        lax.all_gather(output_weight, "shard", axis=0, tiled=True),
        lax.all_gather(output_bias, "shard", axis=0, tiled=True),
        lax.all_gather(second_gain, "shard", axis=0, tiled=True),
        lax.all_gather(second_shift, "shard", axis=0, tiled=True),
        lax.all_gather(expand_weight, "shard", axis=0, tiled=True),
        lax.all_gather(expand_bias, "shard", axis=0, tiled=True),
        lax.all_gather(reduce_weight, "shard", axis=0, tiled=True),
        lax.all_gather(reduce_bias, "shard", axis=0, tiled=True),
    )
    g1f = g1w.astype(jnp.float32)
    s1f = s1w.astype(jnp.float32)
    bjf = bj.astype(jnp.float32)
    bof = bo.astype(jnp.float32)
    g2f = g2w.astype(jnp.float32)
    s2f = s2w.astype(jnp.float32)
    b1f = b1.astype(jnp.float32)
    b2f = b2.astype(jnp.float32)
    width = g1f.shape[0]
    xfull = inputs.astype(jnp.float32)
    normed1, first_back = jax.vjp(layer_norm, xfull, g1f, s1f)
    active1 = normed1.astype(jnp.bfloat16)
    bias_full = jnp.concatenate([bjf[:width], jnp.zeros((width,), jnp.float32), bjf[width:]])
    joint = (jnp.dot(active1, wj, preferred_element_type=jnp.float32) + bias_full).astype(
        jnp.bfloat16
    )
    joint = joint.reshape(images, tokens, 3, width)
    heads = lax.all_to_all(joint, "seq", split_axis=3, concat_axis=1, tiled=True)
    local_width = heads.shape[3]
    local_heads = local_width // HEAD_DIM
    query = heads[:, :, 0].reshape(pieces, LEN, local_heads, HEAD_DIM)
    keys = heads[:, :, 1].reshape(pieces, LEN, local_heads, HEAD_DIM)
    values = heads[:, :, 2].reshape(pieces, LEN, local_heads, HEAD_DIM)

    def score_block(qpart, kpart):
        raw = jnp.einsum("qhd,khd->hqk", qpart, kpart, preferred_element_type=jnp.float32) * factor
        return jnp.where(key_keep[None, None, :], raw, -1000000000.0)

    def attend(item):
        qpart, kpart, vpart = item
        scores = score_block(qpart, kpart)
        top = jnp.max(scores, axis=-1, keepdims=True)
        expo = jnp.exp(scores - top)
        total = jnp.sum(expo, axis=-1, keepdims=True)
        probs = expo / total
        logsum = (top + jnp.log(total))[:, :, 0]
        context = jnp.einsum(
            "hqk,khd->qhd", probs.astype(jnp.bfloat16), vpart, preferred_element_type=jnp.float32
        )
        return (context.astype(jnp.bfloat16).reshape(LEN, local_width), logsum)

    context, logsums = lax.map(attend, (query, keys, values))
    context = context.reshape(images, full_seq, local_width)
    gathered_ctx = lax.all_to_all(context, "seq", split_axis=1, concat_axis=2, tiled=True)
    attn = jnp.dot(gathered_ctx, wo, preferred_element_type=jnp.float32) + bof
    resid = xfull + attn
    normed2, second_back = jax.vjp(layer_norm, resid, g2f, s2f)
    active2 = normed2.astype(jnp.bfloat16)
    upper = jnp.dot(active2, w1, preferred_element_type=jnp.float32) + b1f
    activated, gelu_back = jax.vjp(exact_gelu, upper)
    hidden = activated.astype(jnp.bfloat16)
    branch = jnp.dot(hidden, w2, preferred_element_type=jnp.float32) + b2f
    result = resid + branch
    sums = jnp.stack(
        [
            jnp.sum(result * result * weighting),
            jnp.sum(attn * attn * weighting),
            jnp.sum(branch * branch * weighting),
        ]
    )
    counted = jnp.sum(local_mask) * width
    total_sums, total_count = lax.psum((sums, counted), ("seq", "shard"))
    root_means = jnp.sqrt(total_sums / total_count + 1e-06)
    wj, wo, w1, w2 = (
        lax.all_gather(joint_weight, "shard", axis=0, tiled=True),
        lax.all_gather(output_weight, "shard", axis=0, tiled=True),
        lax.all_gather(expand_weight, "shard", axis=0, tiled=True),
        lax.all_gather(reduce_weight, "shard", axis=0, tiled=True),
    )
    dout = cotangent.astype(jnp.float32) * weighting
    dout_low = dout.astype(jnp.bfloat16)
    grad_w2 = weight_grad(hidden, dout_low)
    grad_b2 = jnp.sum(dout, axis=(0, 1))
    dhidden = back_product(dout_low, w2)
    dupper = gelu_back(dhidden)[0].astype(jnp.bfloat16)
    grad_w1 = weight_grad(active2, dupper)
    grad_b1 = jnp.sum(dupper.astype(jnp.float32), axis=(0, 1))
    dactive2 = back_product(dupper, w1)
    dresid_norm, grad_g2, grad_s2 = second_back(dactive2)
    dresid = dout + dresid_norm
    dattn = dresid.astype(jnp.bfloat16)
    grad_wo = weight_grad(gathered_ctx, dattn)
    grad_bo = jnp.sum(dattn.astype(jnp.float32), axis=(0, 1))
    dcontext = back_product(dattn, wo).astype(jnp.bfloat16)
    dctx_heads = lax.all_to_all(dcontext, "seq", split_axis=2, concat_axis=1, tiled=True)
    dctx_heads = dctx_heads.reshape(pieces, LEN, local_heads, HEAD_DIM)

    def attend_back(item):
        qpart, kpart, vpart, logsum, dpart = item
        scores = score_block(qpart, kpart)
        probs = jnp.exp(scores - logsum[:, :, None])
        dprobs = jnp.einsum("qhd,khd->hqk", dpart, vpart, preferred_element_type=jnp.float32)
        dscore = (probs * (dprobs - jnp.sum(probs * dprobs, axis=-1, keepdims=True))).astype(
            jnp.bfloat16
        )
        dquery = (
            jnp.einsum("hqk,khd->qhd", dscore, kpart, preferred_element_type=jnp.float32) * factor
        )
        dkeys = (
            jnp.einsum("hqk,qhd->khd", dscore, qpart, preferred_element_type=jnp.float32) * factor
        )
        dvalues = jnp.einsum(
            "hqk,qhd->khd", probs.astype(jnp.bfloat16), dpart, preferred_element_type=jnp.float32
        )
        stacked = jnp.stack([dquery, dkeys, dvalues], axis=1).astype(jnp.bfloat16)
        return stacked.reshape(LEN, 3, local_width)

    dheads = lax.map(attend_back, (query, keys, values, logsums, dctx_heads))
    dheads = dheads.reshape(images, full_seq, 3, local_width)
    djoint = lax.all_to_all(dheads, "seq", split_axis=1, concat_axis=3, tiled=True)
    djoint = djoint.reshape(images, tokens, 3 * width)
    grad_wj = weight_grad(active1, djoint)
    joint_sums = jnp.sum(djoint.astype(jnp.float32), axis=(0, 1))
    grad_bj = jnp.concatenate([joint_sums[:width], joint_sums[2 * width :]])
    dactive1 = back_product(djoint, wj)
    dinput_norm, grad_g1, grad_s1 = first_back(dactive1)
    dinput = (dresid + dinput_norm).astype(jnp.bfloat16)
    (
        own_g1,
        own_s1,
        own_wj,
        own_bj,
        own_wo,
        own_bo,
        own_g2,
        own_s2,
        own_w1,
        own_b1,
        own_w2,
        own_b2,
    ) = (
        lax.psum_scatter(grad_g1, ("seq", "shard"), scatter_dimension=0, tiled=True),
        lax.psum_scatter(grad_s1, ("seq", "shard"), scatter_dimension=0, tiled=True),
        lax.psum_scatter(grad_wj, ("seq", "shard"), scatter_dimension=0, tiled=True),
        lax.psum_scatter(grad_bj, ("seq", "shard"), scatter_dimension=0, tiled=True),
        lax.psum_scatter(grad_wo, ("seq", "shard"), scatter_dimension=0, tiled=True),
        lax.psum_scatter(grad_bo, ("seq", "shard"), scatter_dimension=0, tiled=True),
        lax.psum_scatter(grad_g2, ("seq", "shard"), scatter_dimension=0, tiled=True),
        lax.psum_scatter(grad_s2, ("seq", "shard"), scatter_dimension=0, tiled=True),
        lax.psum_scatter(grad_w1, ("seq", "shard"), scatter_dimension=0, tiled=True),
        lax.psum_scatter(grad_b1, ("seq", "shard"), scatter_dimension=0, tiled=True),
        lax.psum_scatter(grad_w2, ("seq", "shard"), scatter_dimension=0, tiled=True),
        lax.psum_scatter(grad_b2, ("seq", "shard"), scatter_dimension=0, tiled=True),
    )
    return (
        result.astype(jnp.bfloat16),
        dinput,
        own_g1,
        own_s1,
        own_wj,
        own_bj,
        own_wo,
        own_bo,
        own_g2,
        own_s2,
        own_w1,
        own_b1,
        own_w2,
        own_b2,
        root_means,
    )


def place():
    seq = lax.axis_index("seq")
    shard = lax.axis_index("shard")
    return lax.rem(shard, 2), lax.div(seq, 2), lax.div(shard, 2), lax.rem(seq, 2)


def z_partner(z, k):
    if k == 0:
        return z
    if k == 1:
        return z + 1 - 2 * lax.rem(z, 2)
    if k == 2:
        return lax.rem(z + 2, 4)
    return 3 - z


def dev(x, y, z, c):
    return (y * 2 + c, z * 2 + x)


def remote(src, dst, sem, target):
    return pltpu.make_async_remote_copy(
        src_ref=src,
        dst_ref=dst,
        send_sem=sem.at[0],
        recv_sem=sem.at[1],
        device_id=target,
        device_id_type=MESH,
    )


def greet():
    x, y, z, c = place()
    barrier = pltpu.get_barrier_semaphore()
    near = [dev(x, y, z_partner(z, k), c) for k in (1, 2, 3)]
    near += [dev(1 - x, y, z, c), dev(x, 1 - y, z, c), dev(x, y, z, 1 - c)]
    for who in near:
        pl.semaphore_signal(barrier, inc=1, device_id=who, device_id_type=MESH)
    pl.semaphore_wait(barrier, len(near))


class Gather:
    def __init__(self, part, full, piece, sems, slot):
        self.part, self.full = part, full
        self.zs, self.xs, self.ys, self.cs, self.es, self.own = [s.at[slot] for s in sems]
        self.shard_rows = part.shape[0]
        self.row, self.rows, self.col, self.cols = piece
        edge = self.cols * 3 // 8 // 128 * 128
        span = self.cols - edge
        self.x, self.y, self.z, self.c = place()
        self.duty = pl.ds(pl.multiple_of(self.col + self.y * edge, 128), span)
        self.mine = pl.ds(pl.multiple_of(self.col + self.y * span, 128), edge)
        self.other = pl.ds(pl.multiple_of(self.col + (1 - self.y) * span, 128), edge)

    def half(self, k, j):
        x = self.x if j == 0 else 1 - self.x
        shard = z_partner(self.z, k) * 2 + x
        half = self.rows // 2
        first = shard * self.shard_rows + self.row + self.c * half
        return pl.ds(pl.multiple_of(first, 16), half)

    def copy(self, k, j, cols, sem, target, local=False):
        at = (self.half(k, j), cols)
        src = self.full.at[at]
        if local:
            half = self.rows // 2
            src = self.part.at[pl.ds(pl.multiple_of(self.row + self.c * half, 16), half), cols]
        return remote(src, self.full.at[at], sem, target)

    def over_z(self, k):
        target = dev(self.x, self.y, z_partner(self.z, k), self.c)
        return self.copy(0, 0, self.duty, self.zs.at[k - 1], target, local=True)

    def over_x(self, k):
        target = dev(1 - self.x, self.y, self.z, self.c)
        return self.copy(k, 0, self.duty, self.xs.at[k], target, local=k == 0)

    def over_y(self, k, j):
        target = dev(self.x, 1 - self.y, self.z, self.c)
        return self.copy(k, j, self.mine, self.ys.at[k * 2 + j], target)

    def over_core(self, k, j):
        target = dev(self.x, self.y, self.z, 1 - self.c)
        return self.copy(k, j, self.duty, self.cs.at[k * 2 + j], target)

    def over_core_rest(self, k, j):
        target = dev(self.x, self.y, self.z, 1 - self.c)
        return self.copy(k, j, self.other, self.es.at[k * 2 + j], target)

    def own_copy(self):
        shard = self.z * 2 + self.x
        cols = pl.ds(self.col, self.cols)
        rows = pl.ds(pl.multiple_of(shard * self.shard_rows + self.row, 16), self.rows)
        src = self.part.at[pl.ds(self.row, self.rows), cols]
        return pltpu.make_async_copy(src, self.full.at[rows, cols], self.own.at[0])

    def step0(self):
        for k in (1, 2, 3):
            self.over_z(k).start()
        self.over_x(0).start()
        self.own_copy().start()

    def step1(self):
        for k in (1, 2, 3):
            self.over_z(k).wait_recv()
            self.over_x(k).start()
            self.over_y(k, 0).start()
            self.over_core(k, 0).start()

    def step2(self):
        for k in (0, 1, 2, 3):
            self.over_x(k).wait_recv()
            self.over_y(k, 1).start()
            self.over_core(k, 1).start()

    def others(self):
        return [(k, 0) for k in (1, 2, 3)] + [(k, 1) for k in (0, 1, 2, 3)]

    def step3(self):
        for k, j in self.others():
            self.over_y(k, j).wait_recv()
            self.over_core_rest(k, j).start()

    def step4(self):
        for k, j in self.others():
            self.over_core(k, j).wait()
            self.over_core_rest(k, j).wait()
            self.over_y(k, j).wait_send()
        for k in (1, 2, 3):
            self.over_z(k).wait_send()
        for k in range(4):
            self.over_x(k).wait_send()
        self.own_copy().wait()


class SmallGather:
    def __init__(self, part, full, zs, xs, own):
        self.part, self.full, self.zs, self.xs, self.own = part, full, zs, xs, own
        self.x, self.y, self.z, self.c = place()

    def at(self, k):
        rows = self.part.shape[0]
        shard = z_partner(self.z, k) * 2 + self.x
        return pl.ds(pl.multiple_of(shard * rows, rows), rows)

    def over_z(self, k):
        target = dev(self.x, self.y, z_partner(self.z, k), self.c)
        return remote(self.part, self.full.at[self.at(0)], self.zs.at[k - 1], target)

    def over_x(self, k):
        target = dev(1 - self.x, self.y, self.z, self.c)
        src = self.full.at[self.at(k)] if k else self.part
        return remote(src, self.full.at[self.at(k)], self.xs.at[k], target)

    def own_copy(self):
        return pltpu.make_async_copy(self.part, self.full.at[self.at(0)], self.own.at[0])

    def step0(self):
        for k in (1, 2, 3):
            self.over_z(k).start()
        self.over_x(0).start()
        self.own_copy().start()

    def step1(self):
        for k in (1, 2, 3):
            self.over_z(k).wait_recv()
            self.over_x(k).start()

    def step4(self):
        for k in range(4):
            self.over_x(k).wait()
        for k in (1, 2, 3):
            self.over_z(k).wait_send()
        self.own_copy().wait()


def dot(left, right, left_axis=1, right_axis=0):
    return lax.dot_general(
        left,
        right,
        (((left_axis,), (right_axis,)), ((), ())),
        preferred_element_type=F32,
    )


def norm_parts(value):
    center = value - jnp.mean(value, axis=-1, keepdims=True)
    inverse = lax.rsqrt(jnp.mean(center * center, axis=-1, keepdims=True) + 1e-06)
    return center * inverse, inverse


def norm_back(grad, gain, hat, inverse):
    scaled = grad * gain
    mean = jnp.mean(scaled, axis=-1, keepdims=True)
    return inverse * (scaled - mean - hat * jnp.mean(scaled * hat, axis=-1, keepdims=True))


def keep_keys(scores):
    row = lax.broadcasted_iota(jnp.int32, (LEN - CUT, scores.shape[1]), 0) + CUT
    last = jnp.where(row < VALID, scores[CUT:], -1000000000.0)
    return jnp.concatenate([scores[:CUT], last], axis=0)


def by_head(value):
    lane = lax.broadcasted_iota(jnp.int32, value.shape, 1)
    none = jnp.zeros_like(value)
    return jnp.where(lane < HEAD_DIM, value, none), jnp.where(lane < HEAD_DIM, none, value)


def attend_pair(query, keys, values, store_logsum):
    total_ctx = None
    for i, (q, v) in enumerate(zip(by_head(query), by_head(values))):
        scores = keep_keys(dot(keys, q, 1, 1))
        top = jnp.max(scores, axis=0, keepdims=True)
        expo = jnp.exp(scores - top)
        total = jnp.sum(expo, axis=0, keepdims=True)
        store_logsum(i, top + jnp.log(total))
        ctx = dot((expo * (1.0 / total)).astype(LOW), v, 0, 0)
        total_ctx = ctx if total_ctx is None else total_ctx + ctx
    return total_ctx


def vector_row(table, rows, first, count):
    at = [s * rows + first + i for s in range(8) for i in range(count)]
    pieces = [table[r : r + 1] for r in at]
    return jnp.concatenate(pieces, axis=1)


def front_plan(shapes):
    (dj, cj), (do, co), (de, ce), (dr, cr) = shapes
    plan = [(0, (0, dj, i * (cj // 3), cj // 3)) for i in range(3)]
    plan += [(1, (0, do, 0, co))]
    plan += [(2, (0, de, i * (ce // 4), ce // 4)) for i in range(4)]
    plan += [(3, (i * (dr // 4), dr // 4, 0, cr)) for i in range(4)]
    return plan


def front_kernel(x_part, d_part, packed, wj, wo, w1, w2, *refs):
    fulls, (rows_out, b1_out, dout, image, active, joint, ctx, logsum) = refs[:4], refs[4:12]
    table, own_half, far_half, weight, xf, *sems = refs[12:]
    parts = (wj, wo, w1, w2)
    half_sem, fetch_sem, small_sems, sems = sems[0], sems[1], sems[2:5], sems[5:]
    x, y, z, c = place()
    greet()
    small = SmallGather(packed, table, *small_sems)
    small.step0()
    swaps, keeps = [], []
    for i, source in enumerate((x_part, d_part)):
        partner = dev(x, y, z, 1 - c)
        swaps.append(remote(source.at[1 - c], far_half.at[i], half_sem.at[2 * i], partner))
        keeps.append(
            pltpu.make_async_copy(source.at[c], own_half.at[i], half_sem.at[2 * i + 1, 0])
        )
        swaps[i].start()
        keeps[i].start()

    def whole(i):
        keeps[i].wait()
        swaps[i].wait()
        own, far = own_half[i].astype(F32), far_half[i].astype(F32)
        first, second = jnp.where(c == 0, own, far), jnp.where(c == 0, far, own)
        return jnp.concatenate([first, second], axis=0)

    plan = front_plan([p.shape for p in parts])
    pieces = [
        Gather(parts[w], fulls[w], piece, sems, i % SLOTS) for i, (w, piece) in enumerate(plan)
    ]
    turns = len(pieces) + LEAD[4]

    def turn(t):
        for step in (4, 3, 2, 1, 0):
            i = t - LEAD[step]
            if 0 <= i < len(pieces):
                getattr(pieces[i], f"step{step}")()

    width = active.shape[1]
    for t in range(9):
        turn(t)
        if t == 1:
            small.step1()
        if t == 2:
            xf[...] = whole(0)
            image[...] = xf[...].astype(LOW)
        if t == 3:
            small.step4()
            rows = packed.shape[0]
            hat, _ = norm_parts(xf[...])
            vectors = table[...].astype(F32)
            gain, shift = vector_row(vectors, rows, 0, 1), vector_row(vectors, rows, 1, 1)
            active[...] = (hat * gain + shift).astype(LOW)
            for i, first in enumerate((4, 5, 6, 11, 0, 0, 0, 0)):
                rows_out[i : i + 1] = vector_row(vectors, rows, first, 1)
            b1_out[...] = vector_row(vectors, rows, 7, 4)
        if t == 4:
            token = lax.broadcasted_iota(jnp.int32, (LEN, 1), 0)
            dout[...] = jnp.where(token < VALID, whole(1), 0.0).astype(LOW)
        if t >= 6:
            cols = pl.ds((t - 6) * width, width)
            fetch = pltpu.make_async_copy(fulls[0].at[:, cols], weight, fetch_sem.at[0])
            fetch.start()
            fetch.wait()
            product = dot(active[...], weight[...])
            if t != 7:
                bias = vector_row(table[...].astype(F32), packed.shape[0], 2, 2)
                product += bias[:, :width] if t == 6 else bias[:, width:]
            joint[:, cols] = product.astype(LOW)

    @pl.loop(0, turns - 9)
    def _(t):
        for k in range(turns - 9):
            pl.when(t == k)(functools.partial(turn, k + 9))

        @pl.when(t < width // 128)
        def _():
            def at(i):
                return pl.ds(pl.multiple_of(i * width + t * 128, 128), 128)

            def store(i, value):
                logsum[t, i : i + 1, :] = value

            query = joint[:, at(0)] * jnp.asarray(HEAD_DIM**-0.5, LOW)
            ctx[:, at(0)] = attend_pair(query, joint[:, at(1)], joint[:, at(2)], store).astype(LOW)


def front(x_part, d_part, packed, parts):
    sds = jax.ShapeDtypeStruct
    dma = pltpu.SemaphoreType.DMA
    tokens, width = x_part.shape[1:]
    pairs = width // 128
    hbm, vmem = pl.BlockSpec(memory_space=pl.ANY), pl.BlockSpec(memory_space=pltpu.VMEM)
    return pl.pallas_call(
        front_kernel,
        out_shape=[sds((p.shape[0] * 8, p.shape[1]), LOW) for p in parts]
        + [
            sds((8, width), F32),
            sds((1, parts[2].shape[1]), F32),
            sds((LEN, width), LOW),
            sds((LEN, width), LOW),
            sds((LEN, width), LOW),
            sds((LEN, 3 * width), LOW),
            sds((LEN, width), LOW),
            sds((pairs, 8, LEN), F32),
        ],
        in_specs=[hbm] * 7,
        out_specs=[hbm] * 4 + [vmem] * 8,
        scratch_shapes=[
            pltpu.VMEM((packed.shape[0] * 8, 128), LOW),
            pltpu.VMEM((2, tokens, width), LOW),
            pltpu.VMEM((2, tokens, width), LOW),
            pltpu.VMEM((width, width), LOW),
            pltpu.VMEM((LEN, width), F32),
            dma((4, 2)),
            dma((1,)),
            dma((3, 2)),
            dma((4, 2)),
            dma((1,)),
            dma((SLOTS, 3, 2)),
            dma((SLOTS, 4, 2)),
            dma((SLOTS, 8, 2)),
            dma((SLOTS, 8, 2)),
            dma((SLOTS, 8, 2)),
            dma((SLOTS, 1)),
        ],
        compiler_params=pltpu.CompilerParams(
            collective_id=1, has_side_effects=True, vmem_limit_bytes=VMEM_LIMIT
        ),
    )(x_part, d_part, packed, *parts)


def middle_kernel(
    chunks,
    ctx,
    image,
    dout,
    wo,
    rows,
    w1,
    b1,
    w2,
    out,
    hidden,
    dupper,
    active,
    dattn,
    dresid,
    dctx,
    small,
    grad_b1,
    resid,
    total,
    dtotal,
):
    j = pl.program_id(0)
    bo, gain, shift, b2 = rows[0:1], rows[1:2], rows[2:3], rows[3:4]
    keep = (lax.broadcasted_iota(jnp.int32, (LEN, 1), 0) < VALID).astype(F32)

    @pl.when(j == 0)
    def _():
        attn = dot(ctx[...], wo[...]) + bo
        value = image[...].astype(F32) + attn
        resid[...] = value
        hat, _ = norm_parts(value)
        active[...] = (hat * gain + shift).astype(LOW)
        total[...] = jnp.zeros_like(total)
        dtotal[...] = jnp.zeros_like(dtotal)
        small[3:4] = jnp.sum(dout[...].astype(F32), axis=0, keepdims=True)
        small[4:5] = jnp.sum(attn * attn * keep, axis=0, keepdims=True)
        small[7:8] = jnp.zeros_like(small[7:8])

    upper = dot(active[...], w1[...]) + b1[...]
    dhidden = dot(dout[...], w2[...], 1, 1)
    share = 0.5 * (1.0 + lax.erf(upper * 0.7071067811865476))
    density = jnp.exp(upper * upper * -0.5) * 0.3989422804014327
    low = (upper * share).astype(LOW)
    dlow = (dhidden * (share + upper * density)).astype(LOW)
    hidden[...] = low
    dupper[...] = dlow
    grad_b1[...] = jnp.sum(dlow.astype(F32), axis=0, keepdims=True)
    total[...] += dot(low, w2[...])
    dtotal[...] += dot(dlow, w1[...], 1, 1)

    @pl.when(j == chunks - 1)
    def _():
        branch = total[...] + b2
        value = resid[...]
        result = value + branch
        half = LEN // 2
        for i in range(2):
            out[i] = result[i * half : (i + 1) * half].astype(LOW)
        small[5:6] = jnp.sum(result * result * keep, axis=0, keepdims=True)
        small[6:7] = jnp.sum(branch * branch * keep, axis=0, keepdims=True)
        hat, inverse = norm_parts(value)
        dactive = dtotal[...]
        small[0:1] = jnp.sum(dactive * hat, axis=0, keepdims=True)
        small[1:2] = jnp.sum(dactive, axis=0, keepdims=True)
        grad = dout[...].astype(F32) + norm_back(dactive, gain, hat, inverse)
        dresid[...] = grad
        low = grad.astype(LOW)
        dattn[...] = low
        small[2:3] = jnp.sum(low.astype(F32), axis=0, keepdims=True)
        dctx[...] = dot(low, wo[...], 1, 1).astype(LOW)


def middle(ctx, image, dout, wo, rows, w1, b1, w2, step=512):
    width, hidden = w1.shape
    sds = jax.ShapeDtypeStruct
    full, wide = (LEN, width), (LEN, hidden)

    def whole(shape):
        return pl.BlockSpec(shape, lambda j: (0, 0))

    def by_column(size):
        return pl.BlockSpec((size, step), lambda j: (0, j))

    return pl.pallas_call(
        functools.partial(middle_kernel, hidden // step),
        grid=(hidden // step,),
        in_specs=[whole(full)] * 3
        + [whole((width, width)), whole((8, width)), by_column(width), by_column(1)]
        + [pl.BlockSpec((step, width), lambda j: (j, 0))],
        out_specs=[pl.BlockSpec((2, LEN // 2, width), lambda j: (0, 0, 0))]
        + [by_column(LEN), by_column(LEN)]
        + [whole(full)] * 4
        + [whole((8, width)), by_column(1)],
        out_shape=[sds((2, LEN // 2, width), LOW), sds(wide, LOW), sds(wide, LOW)]
        + [sds(full, LOW), sds(full, LOW), sds(full, F32), sds(full, LOW)]
        + [sds((8, width), F32), sds((1, hidden), F32)],
        scratch_shapes=[pltpu.VMEM(full, F32)] * 3,
        compiler_params=pltpu.CompilerParams(vmem_limit_bytes=VMEM_LIMIT),
        cost_estimate=pl.CostEstimate(
            flops=12 * LEN * width * hidden,
            bytes_accessed=4 * width * hidden + 4 * LEN * hidden + 24 * LEN * width,
            transcendentals=2 * LEN * hidden,
        ),
    )(ctx, image, dout, wo, rows, w1, b1, w2)


def attend_pair_back(query, keys, values, logsum, dctx):
    heads = [by_head(v) for v in (query, keys, dctx)]
    sums = None
    for i in range(2):
        q, k, d = [h[i] for h in heads]
        probs = jnp.exp(keep_keys(dot(keys, q, 1, 1)) - logsum[i : i + 1])
        dprobs = dot(values, d, 1, 1)
        inner = jnp.sum(probs * dprobs, axis=0, keepdims=True)
        dscore = (probs * (dprobs - inner)).astype(LOW)
        grads = (dot(dscore, k, 0, 0), dot(dscore, q), dot(probs.astype(LOW), d))
        sums = grads if sums is None else tuple(a + b for a, b in zip(sums, grads))
    return sums


ORDER = (3, 2, 1, 0)


class Scatter:
    def __init__(self, grad, got1, got2, got3, sems, x_first):
        self.grad, self.got1, self.got2, self.got3 = grad, got1, got2, got3
        self.sem1, self.sem2, self.sem3 = sems
        self.x_first = x_first
        self.size = grad.shape[0] // 16
        self.x, self.y, self.z, self.c = place()
        self.over_x = dev(1 - self.x, self.y, self.z, self.c)
        self.over_y = dev(self.x, 1 - self.y, self.z, self.c)

    def rows(self, index, count=1):
        return pl.ds(pl.multiple_of(index * self.size, 16), count * self.size)

    def block(self, y, z, x):
        return self.rows((y * 4 + z) * 2 + x)

    def add(self, rows, got, at):
        self.grad[rows] = (self.grad[rows].astype(F32) + got[at].astype(F32)).astype(LOW)

    def firsts(self, k):
        z = z_partner(self.z, k)
        if self.x_first:
            return [
                (self.block(y, z, 1 - self.x), self.rows(2 * k + i), self.block(y, z, self.x))
                for i, y in enumerate((1 - self.y, self.y))
            ]
        theirs, own = [(y * 4 + z) * 2 for y in (1 - self.y, self.y)]
        return [(self.rows(theirs, 2), self.rows(2 * k, 2), self.rows(own, 2))]

    def copy1(self, k, i):
        src, dst, _ = self.firsts(k)[i]
        target = self.over_x if self.x_first else self.over_y
        return remote(self.grad.at[src], self.got1.at[dst], self.sem1.at[2 * k + i], target)

    def copy2(self, k):
        z = z_partner(self.z, k)
        if self.x_first:
            src, target = self.block(1 - self.y, z, self.x), self.over_y
        else:
            src, target = self.block(self.y, z, 1 - self.x), self.over_x
        return remote(self.grad.at[src], self.got2.at[self.rows(k)], self.sem2.at[k], target)

    def copy3(self, k):
        z = z_partner(self.z, k)
        src = self.grad.at[self.block(self.y, z, self.x)]
        target = dev(self.x, self.y, z, self.c)
        return remote(src, self.got3.at[self.rows(k - 1)], self.sem3.at[k - 1], target)

    def start(self, i=0):
        for k in ORDER:
            self.copy1(k, i).start()

    def step1(self, k):
        for i, (_, at, own) in enumerate(self.firsts(k)):
            self.copy1(k, i).wait_recv()
            self.add(own, self.got1, at)
            if i == 0:
                self.copy2(k).start()

    def step2(self, k):
        self.copy2(k).wait_recv()
        z = z_partner(self.z, k)
        self.add(self.block(self.y, z, self.x), self.got2, self.rows(k))
        if k:
            self.copy3(k).start()

    def finish(self, out, first=0):
        cols = pl.ds(first, self.grad.shape[1])
        total = self.grad[self.block(self.y, self.z, self.x)].astype(F32)
        for k in (1, 2, 3):
            self.copy3(k).wait_recv()
            total += self.got3[self.rows(k - 1)].astype(F32)
        out[:, cols] = total
        for k in range(4):
            for i in range(len(self.firsts(k))):
                self.copy1(k, i).wait_send()
            self.copy2(k).wait_send()
            if k:
                self.copy3(k).wait_send()


def back_kernel(*refs):
    hbm, refs = refs[:14], refs[14:]
    hid_h, du_h, dout_h, a2_h, ctx_h, dattn_h, joint_h, dctx_h, a1_h = hbm[:9]
    image_h, dresid_h, wj_h, result_h, logsum_h = hbm[9:]
    (small, grad_b1, rows), refs = refs[:3], refs[3:]
    (layer_out, input_grad, own_wj, own_wo, own_w1, own_w2, totals), refs = refs[:7], refs[7:]
    (du, hid, dout, a2, qkv, logsum), refs = refs[:6], refs[6:]
    (dresid, wj, dact, igrad, sent, sums, got_sums), refs = refs[:7], refs[7:]
    stages, refs = [refs[5 * i : 5 * i + 5] for i in range(4)], refs[20:]
    (load_sem, tile_sem, sum_sem, swap_sem), refs = refs[:4], refs[4:]
    x, y, z, c = place()
    width = a2.shape[1]
    partner = dev(x, y, z, 1 - c)
    x_first = (False, True, False, False, True)
    w2, w1, wo, wja, wjb = [
        Scatter(*[s[i] for s in stages], refs[3 * i : 3 * i + 3], x_first[i]) for i in range(5)
    ]
    greet()

    def load(src, dst, n):
        copy = pltpu.make_async_copy(src, dst, load_sem.at[n])
        copy.start()
        return copy

    def span(index, size):
        return pl.ds(pl.multiple_of(index * size, 128), size)

    def quarter(yy, cc):
        return span(yy * 2 + cc, width)

    loads = [
        load(dout_h, dout, 0),
        load(hid_h.at[:, quarter(1 - y, 1 - c)], hid.at[0], 1),
        load(hid_h.at[:, quarter(1 - y, c)], hid.at[1], 2),
        load(a2_h, a2, 3),
        *[load(du_h.at[:, span(j, width)], du.at[j], 4 + j) for j in range(4)],
        load(joint_h, qkv, 8),
        load(logsum_h, logsum, 9),
        load(dresid_h, dresid, 10),
        load(result_h.at[c], layer_out.at[c], 11),
    ]
    give = remote(result_h.at[1 - c], layer_out.at[c], swap_sem.at[0], partner)
    give.start()

    def half_grad(phase, tiles, slot, grad, tile, product):
        def copy(j):
            rows_at, cols_at = tile(j)
            src = sent.at[slot + j, :, pl.ds(0, cols_at.size)]
            return remote(src, grad.at[rows_at, cols_at], tile_sem.at[phase, j], partner)

        @pl.loop(0, tiles)
        def _(j):
            sent[slot + j, :, pl.ds(0, tile(j)[1].size)] = product(j, False).astype(LOW)
            copy(j).start()

        @pl.loop(0, tiles)
        def _(j):
            copy(j).wait_recv()
            at = tile(j)
            grad[at] = (product(j, True) + grad[at].astype(F32)).astype(LOW)

        def drain():
            @pl.loop(0, tiles)
            def _(j):
                copy(j).wait_send()

        return drain

    def left(array, yy, own):
        return array[:, span(yy * 2 + (c if own else 1 - c), 256)]

    def w2_half(phase, yy):
        def product(j, own):
            return dot(hid[1 if own else 0, :, span(j, 256)], dout[...], 0, 0)

        def tile(j):
            return span(yy * 4 + j, 256), pl.ds(0, width)

        return half_grad(phase, 4, 0, w2.grad, tile, product)

    def w1_half(phase, yy):
        def tile(j):
            return span(yy, 256), span(j, width)

        return half_grad(
            phase, 4, 0, w1.grad, tile, lambda j, own: dot(left(a2, yy, own), du[j], 0, 0)
        )

    def wo_both(phase):
        def tile(j):
            return span(j, 256), pl.ds(0, width)

        return half_grad(
            phase, 2, 0, wo.grad, tile, lambda j, own: dot(left(ctx, j, own), dattn[...], 0, 0)
        )

    part = wja.grad.shape[1] // 2

    def wj_half(phase, yy, second):
        first = 2 if second else 0

        def tile(j):
            return span(yy, 256), span(j, part)

        def product(j, own):
            return dot(left(a1, yy, own), qkv[:, span(first + j, part)], 0, 0)

        return half_grad(phase, 2, first, (wjb if second else wja).grad, tile, product)

    for n in (0, 1, 2):
        loads[n].wait()
    drain = w2_half(0, 1 - y)
    w2.start()
    drain()
    again = [
        load(hid_h.at[:, quarter(y, 1 - c)], hid.at[0], 1),
        load(hid_h.at[:, quarter(y, c)], hid.at[1], 2),
    ]
    for n in range(3, 8):
        loads[n].wait()
    drain = w1_half(1, 1 - y)
    w1.start(0)
    drain()
    drain = w1_half(2, y)
    w1.start(1)
    drain()
    ctx, dattn, dctx, a1 = [du.at[i] for i in range(4)]
    later = [load(src, du.at[i], 4 + i) for i, src in enumerate((ctx_h, dattn_h, dctx_h, a1_h))]
    image = load(image_h, a2, 3)
    for copy in again:
        copy.wait()
    w2_half(3, y)()
    for copy in later:
        copy.wait()
    drain = wo_both(4)
    wo.start()
    loads[8].wait()
    loads[9].wait()
    factor = HEAD_DIM**-0.5
    pairs = width // 128

    def progress(k):
        w2.step1(k)
        w1.step1(k)

    @pl.loop(0, pairs)
    def _(t):
        pl.when(t == pairs // 2)(functools.partial(progress, 3))
        pl.when(t == pairs - 1)(functools.partial(progress, 2))

        def at(i):
            return span(i * pairs + t, 128)

        scaled = qkv[:, at(0)] * jnp.asarray(factor, LOW)
        dq, dk, dv = attend_pair_back(
            scaled, qkv[:, at(1)], qkv[:, at(2)], logsum[t], dctx[:, at(0)]
        )
        for i, grad in enumerate((dq * factor, dk, dv)):
            qkv[:, at(i)] = grad.astype(LOW)

    fetch = [load(wj_h.at[:, pl.ds(i * 512, 512)], wj.at[i], 4 + i) for i in range(2)]
    progress(1)
    drain()
    drains = [wj_half(5, 1 - y, False), wj_half(6, 1 - y, True)]
    wja.start()
    wjb.start(0)
    progress(0)
    for drain in drains:
        drain()
    drains = [wj_half(7, y, False), wj_half(8, y, True)]
    wjb.start(1)
    for k in ORDER:
        wo.step1(k)
    for k in ORDER:
        w2.step2(k)
        w1.step2(k)
    chunks = qkv.shape[1] // 512
    for i in range(chunks):
        fetch[i].wait()
        product = dot(qkv[:, pl.ds(i * 512, 512)], wj[i % 2], 1, 1)
        dact[...] = dact[...] + product if i else product
        if i + 2 < chunks:
            fetch.append(load(wj_h.at[:, pl.ds((i + 2) * 512, 512)], wj.at[i % 2], 4 + i % 2))
    image.wait()
    loads[10].wait()
    hat, inverse = norm_parts(a2[...].astype(F32))
    dactive = dact[...]
    grad = dresid[...] + norm_back(dactive, rows[4:5], hat, inverse)
    half = grad.shape[0] // 2
    for i in range(2):
        igrad[i] = grad[i * half : (i + 1) * half].astype(LOW)
    give_grad = remote(igrad.at[1 - c], input_grad.at[c], swap_sem.at[1], partner)
    give_grad.start()
    keep_grad = load(igrad.at[c], input_grad.at[c], 10)

    def column_sum(value):
        return jnp.sum(value.astype(F32), axis=0, keepdims=True)

    sums[0, 0:1] = column_sum(dactive * hat)
    sums[0, 1:2] = column_sum(dactive)
    sums[0, 2:3] = column_sum(qkv[:, :width])
    sums[0, 3:4] = column_sum(qkv[:, 2 * width :])
    sums[0, 4:5] = small[2:3]
    sums[0, 5:7] = small[0:2]
    sums[0, 7:8] = small[3:4]
    for i in range(4):
        sums[0, 8 + i : 9 + i] = grad_b1[:, i * width : (i + 1) * width]
    sums[0, 12:16] = small[4:8]
    near = [partner, dev(1 - x, y, z, c), dev(x, 1 - y, z, c)]
    near += [dev(x, y, z_partner(z, k), c) for k in (1, 2, 3)]
    sum_copies = [
        remote(sums.at[min(n, 3)], got_sums.at[n], sum_sem.at[n], near[n]) for n in range(6)
    ]
    sum_copies[0].start()
    for k in ORDER:
        wo.step2(k)
    for n in range(3):
        sum_copies[n].wait_recv()
        sums[n + 1] = sums[n] + got_sums[n]
        for copy in sum_copies[n + 1 : n + 2 if n < 2 else 6]:
            copy.start()
        for k in ORDER[n : n + 1 if n < 2 else 4]:
            wja.step1(k)
            wjb.step1(k)
    w2.finish(own_w2)
    w1.finish(own_w1)
    wo.finish(own_wo)
    for k in ORDER:
        wja.step2(k)
        wjb.step2(k)
    for copy in sum_copies[3:]:
        copy.wait_recv()
    totals[...] = (sums[3] + got_sums[3]) + (got_sums[4] + got_sums[5])
    wja.finish(own_wj)
    wjb.finish(own_wj, wja.grad.shape[1])
    for drain in drains:
        drain()
    for copy in sum_copies:
        copy.wait_send()
    loads[11].wait()
    give.wait()
    keep_grad.wait()
    give_grad.wait()


def back(hidden, dupper, dout, active2, ctx, dattn, joint, dctx, active1, image, dresid, wj, *rest):
    result, logsum, small, grad_b1, rows = rest
    sds, vmem, dma = jax.ShapeDtypeStruct, pltpu.VMEM, pltpu.SemaphoreType.DMA
    width, wide = image.shape[1], hidden.shape[1]
    grads = [(wide // 2, width), (width // 2, wide), (width // 2, width)]
    grads += [(width // 2, 3 * width // 2)] * 2
    in_hbm = pl.BlockSpec(memory_space=pl.ANY)
    in_vmem = pl.BlockSpec(memory_space=pltpu.VMEM)
    low = vmem((LEN, width), LOW)

    def stage(top, bottom):
        return [vmem((r * top // bottom, n), LOW) for r, n in grads]

    return pl.pallas_call(
        back_kernel,
        out_shape=[
            sds((2, LEN // 2, width), LOW),
            sds((2, LEN // 2, width), LOW),
            sds((width // 32, 3 * width), F32),
            sds((width // 32, width), F32),
            sds((width // 32, wide), F32),
            sds((wide // 32, width), F32),
            sds((16, width), F32),
        ],
        in_specs=[in_hbm] * 14 + [in_vmem] * 3,
        out_specs=[in_hbm] * 2 + [in_vmem] * 5,
        scratch_shapes=[
            vmem((4, LEN, width), LOW),
            vmem((2, LEN, width), LOW),
            low,
            low,
            vmem((LEN, 3 * width), LOW),
            vmem(logsum.shape, F32),
            vmem((LEN, width), F32),
            vmem((2, width, 512), LOW),
            vmem((LEN, width), F32),
            vmem((2, LEN // 2, width), LOW),
            vmem((4, 256, width), LOW),
            vmem((4, 16, width), F32),
            vmem((6, 16, width), F32),
            *stage(1, 1),
            *stage(1, 2),
            *stage(1, 4),
            *stage(3, 16),
            dma((12,)),
            dma((9, 4, 2)),
            dma((6, 2)),
            dma((2, 2)),
            *[s for _ in grads for s in (dma((8, 2)), dma((4, 2)), dma((3, 2)))],
        ],
        compiler_params=pltpu.CompilerParams(
            collective_id=2, has_side_effects=True, vmem_limit_bytes=VMEM_LIMIT
        ),
    )(
        hidden,
        dupper,
        dout,
        active2,
        ctx,
        dattn,
        joint,
        dctx,
        active1,
        image,
        dresid,
        wj,
        result,
        logsum,
        small,
        grad_b1,
        rows,
    )


def on_chip(
    inputs,
    cotangent,
    first_gain,
    first_shift,
    joint_weight,
    joint_bias,
    output_weight,
    output_bias,
    second_gain,
    second_shift,
    expand_weight,
    expand_bias,
    reduce_weight,
    reduce_bias,
):
    width = inputs.shape[2]
    smalls = [
        first_gain,
        first_shift,
        joint_bias,
        output_bias,
        second_gain,
        second_shift,
        expand_bias,
        reduce_bias,
    ]
    packed = jnp.concatenate([v.reshape(-1, 128) for v in smalls])
    packed = jnp.pad(packed, ((0, -packed.shape[0] % 16), (0, 0)))

    wj, wo, w1, w2, rows, b1, dout, image, active1, joint, context, logsum = front(
        inputs, cotangent, packed, (joint_weight, output_weight, expand_weight, reduce_weight)
    )
    result, hidden, dupper, active2, dattn, dresid, dcontext, small, grad_b1 = middle(
        context, image, dout, wo, rows, w1, b1, w2
    )
    layer_out, input_grad, own_wj, own_wo, own_w1, own_w2, totals = back(
        hidden,
        dupper,
        dout,
        active2,
        context,
        dattn,
        joint,
        dcontext,
        active1,
        image,
        dresid,
        wj,
        result,
        logsum,
        small,
        grad_b1,
        rows,
    )
    rank = lax.axis_index("seq") * 8 + lax.axis_index("shard")

    def own(first, count=1):
        size = count * width // 32
        return lax.dynamic_slice(totals.reshape(-1), (first * width + rank * size,), (size,))

    own_g1, own_s1, own_bj, own_bo = own(0), own(1), own(2, 2), own(4)
    own_g2, own_s2, own_b2, own_b1 = own(5), own(6), own(7), own(8, b1.shape[1] // width)
    means = jnp.sum(totals[12:15], axis=1) / (VALID * width * 32)
    root_means = jnp.sqrt(means[jnp.array([1, 0, 2])] + 1e-06)
    return (
        layer_out,
        input_grad,
        own_g1,
        own_s1,
        own_wj,
        own_bj,
        own_wo,
        own_bo,
        own_g2,
        own_s2,
        own_w1,
        own_b1,
        own_w2,
        own_b2,
        root_means,
    )


def solution(mesh):
    whole_images = mesh.shape["seq"] == 4 and mesh.shape["shard"] == 8
    return jax.shard_map(
        on_chip if whole_images else on_device,
        mesh=mesh,
        in_specs=(
            P("shard", "seq", None),
            P("shard", "seq", None),
            P("shard"),
            P("shard"),
            P("shard", None),
            P("shard"),
            P("shard", None),
            P("shard"),
            P("shard"),
            P("shard"),
            P("shard", None),
            P("shard"),
            P("shard", None),
            P("shard"),
        ),
        out_specs=(
            P("shard", "seq", None),
            P("shard", "seq", None),
            P(("seq", "shard")),
            P(("seq", "shard")),
            P(("seq", "shard"), None),
            P(("seq", "shard")),
            P(("seq", "shard"), None),
            P(("seq", "shard")),
            P(("seq", "shard")),
            P(("seq", "shard")),
            P(("seq", "shard"), None),
            P(("seq", "shard")),
            P(("seq", "shard"), None),
            P(("seq", "shard")),
            P(),
        ),
        check_vma=False,
    )
```

```python
import functools

import jax
import jax.numpy as jnp
from jax import lax
from jax.experimental import pallas as pl
from jax.experimental.pallas import tpu as pltpu
from jax.sharding import PartitionSpec as P

MESH = pl.DeviceIdType.MESH
F32 = jnp.float32
LOW = jnp.bfloat16
HEAD_DIM = 64
LEN = 592
VALID = 577
PACK = 2
CUT = VALID // 16 * 16
SLOTS = 8
LEAD = (0, 2, 3, 4, 6)
VMEM_LIMIT = 61 << 20


def layer_norm(value, gain, shift):
    center = value - jnp.mean(value, axis=-1, keepdims=True)
    spread = jnp.mean(center * center, axis=-1, keepdims=True)
    return center * lax.rsqrt(spread + 1e-06) * gain + shift


def weight_grad(left, right):
    return lax.dot_general(
        left, right, (((0, 1), (0, 1)), ((), ())), preferred_element_type=jnp.float32
    )


def back_product(grad, matrix):
    return lax.dot_general(
        grad, matrix, (((2,), (1,)), ((), ())), preferred_element_type=jnp.float32
    )


def exact_gelu(value):
    return jax.nn.gelu(value, approximate=False)


def on_device(
    inputs,
    cotangent,
    first_gain,
    first_shift,
    joint_weight,
    joint_bias,
    output_weight,
    output_bias,
    second_gain,
    second_shift,
    expand_weight,
    expand_bias,
    reduce_weight,
    reduce_bias,
):
    images = inputs.shape[0]
    tokens = inputs.shape[1]
    full_seq = PACK * LEN
    pieces = images * PACK
    factor = HEAD_DIM ** (-0.5)
    begin = lax.axis_index("seq") * tokens
    local_places = begin + jnp.arange(tokens, dtype=jnp.int32)
    local_row = (local_places % LEN < VALID).astype(jnp.float32)
    local_mask = jnp.broadcast_to(local_row[None, :], (images, tokens))
    key_keep = jnp.arange(LEN, dtype=jnp.int32) < VALID
    weighting = local_mask[:, :, None]
    g1w, s1w, wj, bj, wo, bo, g2w, s2w, w1, b1, w2, b2 = (
        lax.all_gather(first_gain, "shard", axis=0, tiled=True),
        lax.all_gather(first_shift, "shard", axis=0, tiled=True),
        lax.all_gather(joint_weight, "shard", axis=0, tiled=True),
        lax.all_gather(joint_bias, "shard", axis=0, tiled=True),
        lax.all_gather(output_weight, "shard", axis=0, tiled=True),
        lax.all_gather(output_bias, "shard", axis=0, tiled=True),
        lax.all_gather(second_gain, "shard", axis=0, tiled=True),
        lax.all_gather(second_shift, "shard", axis=0, tiled=True),
        lax.all_gather(expand_weight, "shard", axis=0, tiled=True),
        lax.all_gather(expand_bias, "shard", axis=0, tiled=True),
        lax.all_gather(reduce_weight, "shard", axis=0, tiled=True),
        lax.all_gather(reduce_bias, "shard", axis=0, tiled=True),
    )
    g1f = g1w.astype(jnp.float32)
    s1f = s1w.astype(jnp.float32)
    bjf = bj.astype(jnp.float32)
    bof = bo.astype(jnp.float32)
    g2f = g2w.astype(jnp.float32)
    s2f = s2w.astype(jnp.float32)
    b1f = b1.astype(jnp.float32)
    b2f = b2.astype(jnp.float32)
    width = g1f.shape[0]
    xfull = inputs.astype(jnp.float32)
    normed1, first_back = jax.vjp(layer_norm, xfull, g1f, s1f)
    active1 = normed1.astype(jnp.bfloat16)
    bias_full = jnp.concatenate([bjf[:width], jnp.zeros((width,), jnp.float32), bjf[width:]])
    joint = (jnp.dot(active1, wj, preferred_element_type=jnp.float32) + bias_full).astype(
        jnp.bfloat16
    )
    joint = joint.reshape(images, tokens, 3, width)
    heads = lax.all_to_all(joint, "seq", split_axis=3, concat_axis=1, tiled=True)
    local_width = heads.shape[3]
    local_heads = local_width // HEAD_DIM
    query = heads[:, :, 0].reshape(pieces, LEN, local_heads, HEAD_DIM)
    keys = heads[:, :, 1].reshape(pieces, LEN, local_heads, HEAD_DIM)
    values = heads[:, :, 2].reshape(pieces, LEN, local_heads, HEAD_DIM)

    def score_block(qpart, kpart):
        raw = jnp.einsum("qhd,khd->hqk", qpart, kpart, preferred_element_type=jnp.float32) * factor
        return jnp.where(key_keep[None, None, :], raw, -1000000000.0)

    def attend(item):
        qpart, kpart, vpart = item
        scores = score_block(qpart, kpart)
        top = jnp.max(scores, axis=-1, keepdims=True)
        expo = jnp.exp(scores - top)
        total = jnp.sum(expo, axis=-1, keepdims=True)
        probs = expo / total
        logsum = (top + jnp.log(total))[:, :, 0]
        context = jnp.einsum(
            "hqk,khd->qhd", probs.astype(jnp.bfloat16), vpart, preferred_element_type=jnp.float32
        )
        return (context.astype(jnp.bfloat16).reshape(LEN, local_width), logsum)

    context, logsums = lax.map(attend, (query, keys, values))
    context = context.reshape(images, full_seq, local_width)
    gathered_ctx = lax.all_to_all(context, "seq", split_axis=1, concat_axis=2, tiled=True)
    attn = jnp.dot(gathered_ctx, wo, preferred_element_type=jnp.float32) + bof
    resid = xfull + attn
    normed2, second_back = jax.vjp(layer_norm, resid, g2f, s2f)
    active2 = normed2.astype(jnp.bfloat16)
    upper = jnp.dot(active2, w1, preferred_element_type=jnp.float32) + b1f
    activated, gelu_back = jax.vjp(exact_gelu, upper)
    hidden = activated.astype(jnp.bfloat16)
    branch = jnp.dot(hidden, w2, preferred_element_type=jnp.float32) + b2f
    result = resid + branch
    sums = jnp.stack(
        [
            jnp.sum(result * result * weighting),
            jnp.sum(attn * attn * weighting),
            jnp.sum(branch * branch * weighting),
        ]
    )
    counted = jnp.sum(local_mask) * width
    total_sums, total_count = lax.psum((sums, counted), ("seq", "shard"))
    root_means = jnp.sqrt(total_sums / total_count + 1e-06)
    wj, wo, w1, w2 = (
        lax.all_gather(joint_weight, "shard", axis=0, tiled=True),
        lax.all_gather(output_weight, "shard", axis=0, tiled=True),
        lax.all_gather(expand_weight, "shard", axis=0, tiled=True),
        lax.all_gather(reduce_weight, "shard", axis=0, tiled=True),
    )
    dout = cotangent.astype(jnp.float32) * weighting
    dout_low = dout.astype(jnp.bfloat16)
    grad_w2 = weight_grad(hidden, dout_low)
    grad_b2 = jnp.sum(dout, axis=(0, 1))
    dhidden = back_product(dout_low, w2)
    dupper = gelu_back(dhidden)[0].astype(jnp.bfloat16)
    grad_w1 = weight_grad(active2, dupper)
    grad_b1 = jnp.sum(dupper.astype(jnp.float32), axis=(0, 1))
    dactive2 = back_product(dupper, w1)
    dresid_norm, grad_g2, grad_s2 = second_back(dactive2)
    dresid = dout + dresid_norm
    dattn = dresid.astype(jnp.bfloat16)
    grad_wo = weight_grad(gathered_ctx, dattn)
    grad_bo = jnp.sum(dattn.astype(jnp.float32), axis=(0, 1))
    dcontext = back_product(dattn, wo).astype(jnp.bfloat16)
    dctx_heads = lax.all_to_all(dcontext, "seq", split_axis=2, concat_axis=1, tiled=True)
    dctx_heads = dctx_heads.reshape(pieces, LEN, local_heads, HEAD_DIM)

    def attend_back(item):
        qpart, kpart, vpart, logsum, dpart = item
        scores = score_block(qpart, kpart)
        probs = jnp.exp(scores - logsum[:, :, None])
        dprobs = jnp.einsum("qhd,khd->hqk", dpart, vpart, preferred_element_type=jnp.float32)
        dscore = (probs * (dprobs - jnp.sum(probs * dprobs, axis=-1, keepdims=True))).astype(
            jnp.bfloat16
        )
        dquery = (
            jnp.einsum("hqk,khd->qhd", dscore, kpart, preferred_element_type=jnp.float32) * factor
        )
        dkeys = (
            jnp.einsum("hqk,qhd->khd", dscore, qpart, preferred_element_type=jnp.float32) * factor
        )
        dvalues = jnp.einsum(
            "hqk,qhd->khd", probs.astype(jnp.bfloat16), dpart, preferred_element_type=jnp.float32
        )
        stacked = jnp.stack([dquery, dkeys, dvalues], axis=1).astype(jnp.bfloat16)
        return stacked.reshape(LEN, 3, local_width)

    dheads = lax.map(attend_back, (query, keys, values, logsums, dctx_heads))
    dheads = dheads.reshape(images, full_seq, 3, local_width)
    djoint = lax.all_to_all(dheads, "seq", split_axis=1, concat_axis=3, tiled=True)
    djoint = djoint.reshape(images, tokens, 3 * width)
    grad_wj = weight_grad(active1, djoint)
    joint_sums = jnp.sum(djoint.astype(jnp.float32), axis=(0, 1))
    grad_bj = jnp.concatenate([joint_sums[:width], joint_sums[2 * width :]])
    dactive1 = back_product(djoint, wj)
    dinput_norm, grad_g1, grad_s1 = first_back(dactive1)
    dinput = (dresid + dinput_norm).astype(jnp.bfloat16)
    (
        own_g1,
        own_s1,
        own_wj,
        own_bj,
        own_wo,
        own_bo,
        own_g2,
        own_s2,
        own_w1,
        own_b1,
        own_w2,
        own_b2,
    ) = (
        lax.psum_scatter(grad_g1, ("seq", "shard"), scatter_dimension=0, tiled=True),
        lax.psum_scatter(grad_s1, ("seq", "shard"), scatter_dimension=0, tiled=True),
        lax.psum_scatter(grad_wj, ("seq", "shard"), scatter_dimension=0, tiled=True),
        lax.psum_scatter(grad_bj, ("seq", "shard"), scatter_dimension=0, tiled=True),
        lax.psum_scatter(grad_wo, ("seq", "shard"), scatter_dimension=0, tiled=True),
        lax.psum_scatter(grad_bo, ("seq", "shard"), scatter_dimension=0, tiled=True),
        lax.psum_scatter(grad_g2, ("seq", "shard"), scatter_dimension=0, tiled=True),
        lax.psum_scatter(grad_s2, ("seq", "shard"), scatter_dimension=0, tiled=True),
        lax.psum_scatter(grad_w1, ("seq", "shard"), scatter_dimension=0, tiled=True),
        lax.psum_scatter(grad_b1, ("seq", "shard"), scatter_dimension=0, tiled=True),
        lax.psum_scatter(grad_w2, ("seq", "shard"), scatter_dimension=0, tiled=True),
        lax.psum_scatter(grad_b2, ("seq", "shard"), scatter_dimension=0, tiled=True),
    )
    return (
        result.astype(jnp.bfloat16),
        dinput,
        own_g1,
        own_s1,
        own_wj,
        own_bj,
        own_wo,
        own_bo,
        own_g2,
        own_s2,
        own_w1,
        own_b1,
        own_w2,
        own_b2,
        root_means,
    )


def place():
    seq = lax.axis_index("seq")
    shard = lax.axis_index("shard")
    return lax.rem(shard, 2), lax.div(seq, 2), lax.div(shard, 2), lax.rem(seq, 2)


def z_partner(z, k):
    if k == 0:
        return z
    if k == 1:
        return z + 1 - 2 * lax.rem(z, 2)
    if k == 2:
        return lax.rem(z + 2, 4)
    return 3 - z


def dev(x, y, z, c):
    return (y * 2 + c, z * 2 + x)


def remote(src, dst, sem, target):
    return pltpu.make_async_remote_copy(
        src_ref=src,
        dst_ref=dst,
        send_sem=sem.at[0],
        recv_sem=sem.at[1],
        device_id=target,
        device_id_type=MESH,
    )


def greet():
    x, y, z, c = place()
    barrier = pltpu.get_barrier_semaphore()
    near = [dev(x, y, z_partner(z, k), c) for k in (1, 2, 3)]
    near += [dev(1 - x, y, z, c), dev(x, 1 - y, z, c), dev(x, y, z, 1 - c)]
    for who in near:
        pl.semaphore_signal(barrier, inc=1, device_id=who, device_id_type=MESH)
    pl.semaphore_wait(barrier, len(near))


class Gather:
    def __init__(self, part, full, piece, sems, slot):
        self.part, self.full = part, full
        self.zs, self.xs, self.ys, self.cs, self.es, self.own = [s.at[slot] for s in sems]
        self.shard_rows = part.shape[0]
        self.row, self.rows, self.col, self.cols = piece
        edge = self.cols * 3 // 8 // 128 * 128
        span = self.cols - edge
        self.x, self.y, self.z, self.c = place()
        self.duty = pl.ds(pl.multiple_of(self.col + self.y * edge, 128), span)
        self.mine = pl.ds(pl.multiple_of(self.col + self.y * span, 128), edge)
        self.other = pl.ds(pl.multiple_of(self.col + (1 - self.y) * span, 128), edge)

    def half(self, k, j):
        x = self.x if j == 0 else 1 - self.x
        shard = z_partner(self.z, k) * 2 + x
        half = self.rows // 2
        first = shard * self.shard_rows + self.row + self.c * half
        return pl.ds(pl.multiple_of(first, 16), half)

    def copy(self, k, j, cols, sem, target, local=False):
        at = (self.half(k, j), cols)
        src = self.full.at[at]
        if local:
            half = self.rows // 2
            src = self.part.at[pl.ds(pl.multiple_of(self.row + self.c * half, 16), half), cols]
        return remote(src, self.full.at[at], sem, target)

    def over_z(self, k):
        target = dev(self.x, self.y, z_partner(self.z, k), self.c)
        return self.copy(0, 0, self.duty, self.zs.at[k - 1], target, local=True)

    def over_x(self, k):
        target = dev(1 - self.x, self.y, self.z, self.c)
        return self.copy(k, 0, self.duty, self.xs.at[k], target, local=k == 0)

    def over_y(self, k, j):
        target = dev(self.x, 1 - self.y, self.z, self.c)
        return self.copy(k, j, self.mine, self.ys.at[k * 2 + j], target)

    def over_core(self, k, j):
        target = dev(self.x, self.y, self.z, 1 - self.c)
        return self.copy(k, j, self.duty, self.cs.at[k * 2 + j], target)

    def over_core_rest(self, k, j):
        target = dev(self.x, self.y, self.z, 1 - self.c)
        return self.copy(k, j, self.other, self.es.at[k * 2 + j], target)

    def own_copy(self):
        shard = self.z * 2 + self.x
        cols = pl.ds(self.col, self.cols)
        rows = pl.ds(pl.multiple_of(shard * self.shard_rows + self.row, 16), self.rows)
        src = self.part.at[pl.ds(self.row, self.rows), cols]
        return pltpu.make_async_copy(src, self.full.at[rows, cols], self.own.at[0])

    def step0(self):
        for k in (1, 2, 3):
            self.over_z(k).start()
        self.over_x(0).start()
        self.own_copy().start()

    def step1(self):
        for k in (1, 2, 3):
            self.over_z(k).wait_recv()
            self.over_x(k).start()
            self.over_y(k, 0).start()
            self.over_core(k, 0).start()

    def step2(self):
        for k in (0, 1, 2, 3):
            self.over_x(k).wait_recv()
            self.over_y(k, 1).start()
            self.over_core(k, 1).start()

    def others(self):
        return [(k, 0) for k in (1, 2, 3)] + [(k, 1) for k in (0, 1, 2, 3)]

    def step3(self):
        for k, j in self.others():
            self.over_y(k, j).wait_recv()
            self.over_core_rest(k, j).start()

    def step4(self):
        for k, j in self.others():
            self.over_core(k, j).wait()
            self.over_core_rest(k, j).wait()
            self.over_y(k, j).wait_send()
        for k in (1, 2, 3):
            self.over_z(k).wait_send()
        for k in range(4):
            self.over_x(k).wait_send()
        self.own_copy().wait()


class SmallGather:
    def __init__(self, part, full, zs, xs, own):
        self.part, self.full, self.zs, self.xs, self.own = part, full, zs, xs, own
        self.x, self.y, self.z, self.c = place()

    def at(self, k):
        rows = self.part.shape[0]
        shard = z_partner(self.z, k) * 2 + self.x
        return pl.ds(pl.multiple_of(shard * rows, rows), rows)

    def over_z(self, k):
        target = dev(self.x, self.y, z_partner(self.z, k), self.c)
        return remote(self.part, self.full.at[self.at(0)], self.zs.at[k - 1], target)

    def over_x(self, k):
        target = dev(1 - self.x, self.y, self.z, self.c)
        src = self.full.at[self.at(k)] if k else self.part
        return remote(src, self.full.at[self.at(k)], self.xs.at[k], target)

    def own_copy(self):
        return pltpu.make_async_copy(self.part, self.full.at[self.at(0)], self.own.at[0])

    def step0(self):
        for k in (1, 2, 3):
            self.over_z(k).start()
        self.over_x(0).start()
        self.own_copy().start()

    def step1(self):
        for k in (1, 2, 3):
            self.over_z(k).wait_recv()
            self.over_x(k).start()

    def step4(self):
        for k in range(4):
            self.over_x(k).wait()
        for k in (1, 2, 3):
            self.over_z(k).wait_send()
        self.own_copy().wait()


def dot(left, right, left_axis=1, right_axis=0):
    return lax.dot_general(
        left,
        right,
        (((left_axis,), (right_axis,)), ((), ())),
        preferred_element_type=F32,
    )


def norm_parts(value):
    center = value - jnp.mean(value, axis=-1, keepdims=True)
    inverse = lax.rsqrt(jnp.mean(center * center, axis=-1, keepdims=True) + 1e-06)
    return center * inverse, inverse


def norm_back(grad, gain, hat, inverse):
    scaled = grad * gain
    mean = jnp.mean(scaled, axis=-1, keepdims=True)
    return inverse * (scaled - mean - hat * jnp.mean(scaled * hat, axis=-1, keepdims=True))


def keep_keys(scores):
    row = lax.broadcasted_iota(jnp.int32, (LEN - CUT, scores.shape[1]), 0) + CUT
    last = jnp.where(row < VALID, scores[CUT:], -1000000000.0)
    return jnp.concatenate([scores[:CUT], last], axis=0)


def by_head(value):
    lane = lax.broadcasted_iota(jnp.int32, value.shape, 1)
    none = jnp.zeros_like(value)
    return jnp.where(lane < HEAD_DIM, value, none), jnp.where(lane < HEAD_DIM, none, value)


def attend_pair(query, keys, values, store_logsum):
    total_ctx = None
    for i, (q, v) in enumerate(zip(by_head(query), by_head(values))):
        scores = keep_keys(dot(keys, q, 1, 1))
        top = jnp.max(scores, axis=0, keepdims=True)
        expo = jnp.exp(scores - top)
        total = jnp.sum(expo, axis=0, keepdims=True)
        store_logsum(i, top + jnp.log(total))
        ctx = dot((expo * (1.0 / total)).astype(LOW), v, 0, 0)
        total_ctx = ctx if total_ctx is None else total_ctx + ctx
    return total_ctx


def vector_row(table, rows, first, count):
    at = [s * rows + first + i for s in range(8) for i in range(count)]
    pieces = [table[r : r + 1] for r in at]
    return jnp.concatenate(pieces, axis=1)


def front_plan(shapes):
    (dj, cj), (do, co), (de, ce), (dr, cr) = shapes
    plan = [(0, (0, dj, i * (cj // 3), cj // 3)) for i in range(3)]
    plan += [(1, (0, do, 0, co))]
    plan += [(2, (0, de, i * (ce // 4), ce // 4)) for i in range(4)]
    plan += [(3, (i * (dr // 4), dr // 4, 0, cr)) for i in range(4)]
    return plan


def front_kernel(x_part, d_part, packed, wj, wo, w1, w2, *refs):
    fulls, outs, refs = refs[:4], refs[4:17], refs[17:]
    (rows_out, b1_out), hbm_outs = outs[:2], outs[2:]
    dout, image, active, joint, ctx, logsum, active2, hidden, slope = refs[:9]
    table, own_half, far_half, weight, xf, grad, sent, out_sem, tile_sem, *sems = refs[9:]
    parts = (wj, wo, w1, w2)
    half_sem, fetch_sem, small_sems, sems = sems[0], sems[1], sems[2:5], sems[5:]
    x, y, z, c = place()
    greet()
    small = SmallGather(packed, table, *small_sems)
    small.step0()
    partner = dev(x, y, z, 1 - c)
    swaps, keeps = [], []
    for i, source in enumerate((x_part, d_part)):
        swaps.append(remote(source.at[1 - c], far_half.at[i], half_sem.at[2 * i], partner))
        keeps.append(
            pltpu.make_async_copy(source.at[c], own_half.at[i], half_sem.at[2 * i + 1, 0])
        )
        swaps[i].start()
        keeps[i].start()

    def whole(i):
        keeps[i].wait()
        swaps[i].wait()
        own, far = own_half[i].astype(F32), far_half[i].astype(F32)
        first, second = jnp.where(c == 0, own, far), jnp.where(c == 0, far, own)
        return jnp.concatenate([first, second], axis=0)

    plan = front_plan([p.shape for p in parts])
    pieces = [
        Gather(parts[w], fulls[w], piece, sems, i % SLOTS) for i, (w, piece) in enumerate(plan)
    ]

    def turn(t):
        for step in (4, 3, 2, 1, 0):
            i = t - LEAD[step]
            if 0 <= i < len(pieces):
                getattr(pieces[i], f"step{step}")()

    stores = []

    def store(src, n, at=None):
        dst = hbm_outs[n] if at is None else hbm_outs[n].at[at]
        stores.append(pltpu.make_async_copy(src, dst, out_sem.at[len(stores)]))
        stores[-1].start()

    def fetch(source, cols, slot=0):
        copy = pltpu.make_async_copy(source.at[:, cols], weight.at[slot], fetch_sem.at[slot])
        copy.start()
        return copy

    width = active.shape[1]
    rows = packed.shape[0]
    for t in range(9):
        turn(t)
        if t == 1:
            small.step1()
        if t == 2:
            xf[...] = whole(0)
            image[...] = xf[...].astype(LOW)
            store(image, 1)
        if t == 3:
            small.step4()
            hat, _ = norm_parts(xf[...])
            vectors = table[...].astype(F32)
            gain, shift = vector_row(vectors, rows, 0, 1), vector_row(vectors, rows, 1, 1)
            active[...] = (hat * gain + shift).astype(LOW)
            store(active, 2)
            for i, first in enumerate((4, 5, 6, 11, 0, 0, 0, 0)):
                rows_out[i : i + 1] = vector_row(vectors, rows, first, 1)
            b1_out[...] = vector_row(vectors, rows, 7, 4)
        if t == 4:
            token = lax.broadcasted_iota(jnp.int32, (LEN, 1), 0)
            dout[...] = jnp.where(token < VALID, whole(1), 0.0).astype(LOW)
            store(dout, 0)
        if t >= 6:
            cols = pl.ds((t - 6) * width, width)
            fetch(fulls[0], cols).wait()
            product = dot(active[...], weight[0])
            if t != 7:
                bias = vector_row(table[...].astype(F32), rows, 2, 2)
                product += bias[:, :width] if t == 6 else bias[:, width:]
            joint[:, cols] = product.astype(LOW)
    store(joint, 3)

    @pl.loop(0, width // 128)
    def _(t):
        for i in range(2):
            pl.when(t == 3 * i + 2)(functools.partial(turn, 9 + i))

        def at(i):
            return pl.ds(pl.multiple_of(i * width + t * 128, 128), 128)

        def put(i, value):
            logsum[t, i : i + 1, :] = value

        query = joint[:, at(0)] * jnp.asarray(HEAD_DIM**-0.5, LOW)
        ctx[:, at(0)] = attend_pair(query, joint[:, at(1)], joint[:, at(2)], put).astype(LOW)

    store(ctx, 4)
    store(logsum, 5)
    coming = fetch(fulls[1], pl.ds(0, width))
    turn(11)
    coming.wait()
    coming = fetch(fulls[2], pl.ds(0, width), 1)
    attn = dot(ctx[...], weight[0]) + rows_out[0:1]
    keep = lax.broadcasted_iota(jnp.int32, (LEN, 1), 0) < VALID
    rows_out[5:6] = jnp.sum(jnp.where(keep, attn * attn, 0.0), axis=0, keepdims=True)
    xf[...] += attn
    store(xf, 6)
    hat, _ = norm_parts(xf[...])
    active2[...] = (hat * rows_out[1:2] + rows_out[2:3]).astype(LOW)
    store(active2, 7)
    chunks = b1_out.shape[1] // width
    begin = len(stores)

    def reduce_grad(yy):
        def rows_at(j):
            return pl.ds(pl.multiple_of(yy * width + j * 256, 256), 256)

        def copy(j):
            slot = sent.at[lax.rem(j, 2)]
            return remote(slot, grad.at[rows_at(j)], tile_sem.at[yy, j], partner)

        def product(core, j):
            cols = pl.ds(pl.multiple_of(j * 256, 256), 256)
            return dot(hidden[core, :, cols], dout[...], 0, 0)

        @pl.loop(0, width // 256)
        def _(j):
            @pl.when(j > 1)
            def _():
                copy(j - 2).wait_send()

            sent[lax.rem(j, 2)] = product(1 - c, j).astype(LOW)
            copy(j).start()

        @pl.loop(0, width // 256)
        def _(j):
            copy(j).wait_recv()
            at = rows_at(j)
            grad[at] = (product(c, j) + grad[at].astype(F32)).astype(LOW)

        for j in range(width // 256 - 2, width // 256):
            copy(j).wait_send()

    for j in range(chunks):
        turn(12 + j)
        coming.wait()
        slot = j % 2
        if j + 1 < chunks:
            coming = fetch(fulls[2], pl.ds((j + 1) * width, width), 1 - (j + 1) % 2)
        if j > 1:
            for copy in stores[begin + 4 * j - 8 : begin + 4 * j - 4]:
                copy.wait()
        for i in range(2):
            cols = pl.ds(i * width // 2, width // 2)
            there = pl.ds(j * width + i * width // 2, width // 2)
            upper = dot(active2[...], weight[1 - slot, :, cols]) + b1_out[:, there]
            share = 0.5 * (1.0 + lax.erf(upper * 0.7071067811865476))
            density = jnp.exp(upper * upper * -0.5) * 0.3989422804014327
            hidden[slot, :, cols] = (upper * share).astype(LOW)
            slope[slot, :, cols] = (share + upper * density).astype(LOW)
            store(hidden.at[slot, :, cols], 8, (slice(None), there))
            store(slope.at[slot, :, cols], 9, (slice(None), there))
        if j % 2:
            reduce_grad(j // 2)
    for t in range(12 + chunks, len(pieces) + LEAD[4]):
        turn(t)
    store(grad, 10)
    for n, copy in enumerate(stores):
        if not begin <= n < begin + 4 * chunks - 8:
            copy.wait()


def front(x_part, d_part, packed, parts):
    sds, vmem, dma = jax.ShapeDtypeStruct, pltpu.VMEM, pltpu.SemaphoreType.DMA
    tokens, width = x_part.shape[1:]
    wide = parts[2].shape[1]
    pairs = width // 128
    hbm, in_vmem = pl.BlockSpec(memory_space=pl.ANY), pl.BlockSpec(memory_space=pltpu.VMEM)
    full = (LEN, width)
    return pl.pallas_call(
        front_kernel,
        out_shape=[sds((p.shape[0] * 8, p.shape[1]), LOW) for p in parts]
        + [
            sds((8, width), F32),
            sds((1, wide), F32),
            sds(full, LOW),
            sds(full, LOW),
            sds(full, LOW),
            sds((LEN, 3 * width), LOW),
            sds(full, LOW),
            sds((pairs, 8, LEN), F32),
            sds(full, F32),
            sds(full, LOW),
            sds((LEN, wide), LOW),
            sds((LEN, wide), LOW),
            sds((wide // 2, width), LOW),
        ],
        in_specs=[hbm] * 7,
        out_specs=[hbm] * 4 + [in_vmem] * 2 + [hbm] * 11,
        scratch_shapes=[
            vmem(full, LOW),
            vmem(full, LOW),
            vmem(full, LOW),
            vmem((LEN, 3 * width), LOW),
            vmem(full, LOW),
            vmem((pairs, 8, LEN), F32),
            vmem(full, LOW),
            vmem((2, LEN, width), LOW),
            vmem((2, LEN, width), LOW),
            vmem((packed.shape[0] * 8, 128), LOW),
            vmem((2, tokens, width), LOW),
            vmem((2, tokens, width), LOW),
            vmem((2, width, width), LOW),
            vmem(full, F32),
            vmem((wide // 2, width), LOW),
            vmem((2, 256, width), LOW),
            dma((9 + 4 * (wide // width),)),
            dma((2, width // 256, 2)),
            dma((4, 2)),
            dma((2,)),
            dma((3, 2)),
            dma((4, 2)),
            dma((1,)),
            dma((SLOTS, 3, 2)),
            dma((SLOTS, 4, 2)),
            dma((SLOTS, 8, 2)),
            dma((SLOTS, 8, 2)),
            dma((SLOTS, 8, 2)),
            dma((SLOTS, 1)),
        ],
        compiler_params=pltpu.CompilerParams(
            collective_id=1, has_side_effects=True, vmem_limit_bytes=VMEM_LIMIT
        ),
    )(x_part, d_part, packed, *parts)


def attend_pair_back(query, keys, values, logsum, dctx):
    heads = [by_head(v) for v in (query, keys, dctx)]
    sums = None
    for i in range(2):
        q, k, d = [h[i] for h in heads]
        probs = jnp.exp(keep_keys(dot(keys, q, 1, 1)) - logsum[i : i + 1])
        dprobs = dot(values, d, 1, 1)
        inner = jnp.sum(probs * dprobs, axis=0, keepdims=True)
        dscore = (probs * (dprobs - inner)).astype(LOW)
        grads = (dot(dscore, k, 0, 0), dot(dscore, q), dot(probs.astype(LOW), d))
        sums = grads if sums is None else tuple(a + b for a, b in zip(sums, grads))
    return sums


ORDER = (3, 2, 1, 0)


class Scatter:
    def __init__(self, grad, got1, got2, got3, sems, x_first):
        self.grad, self.got1, self.got2, self.got3 = grad, got1, got2, got3
        self.sem1, self.sem2, self.sem3 = sems
        self.x_first = x_first
        self.size = grad.shape[0] // 16
        self.x, self.y, self.z, self.c = place()
        self.over_x = dev(1 - self.x, self.y, self.z, self.c)
        self.over_y = dev(self.x, 1 - self.y, self.z, self.c)

    def rows(self, index, count=1):
        return pl.ds(pl.multiple_of(index * self.size, 16), count * self.size)

    def block(self, y, z, x):
        return self.rows((y * 4 + z) * 2 + x)

    def add(self, rows, got, at):
        self.grad[rows] = (self.grad[rows].astype(F32) + got[at].astype(F32)).astype(LOW)

    def firsts(self, k):
        z = z_partner(self.z, k)
        if self.x_first:
            return [
                (self.block(y, z, 1 - self.x), self.rows(2 * k + i), self.block(y, z, self.x))
                for i, y in enumerate((1 - self.y, self.y))
            ]
        theirs, own = [(y * 4 + z) * 2 for y in (1 - self.y, self.y)]
        return [(self.rows(theirs, 2), self.rows(2 * k, 2), self.rows(own, 2))]

    def copy1(self, k, i):
        src, dst, _ = self.firsts(k)[i]
        target = self.over_x if self.x_first else self.over_y
        return remote(self.grad.at[src], self.got1.at[dst], self.sem1.at[2 * k + i], target)

    def copy2(self, k):
        z = z_partner(self.z, k)
        if self.x_first:
            src, target = self.block(1 - self.y, z, self.x), self.over_y
        else:
            src, target = self.block(self.y, z, 1 - self.x), self.over_x
        return remote(self.grad.at[src], self.got2.at[self.rows(k)], self.sem2.at[k], target)

    def copy3(self, k):
        z = z_partner(self.z, k)
        src = self.grad.at[self.block(self.y, z, self.x)]
        target = dev(self.x, self.y, z, self.c)
        return remote(src, self.got3.at[self.rows(k - 1)], self.sem3.at[k - 1], target)

    def start(self, i=0):
        for k in ORDER:
            self.copy1(k, i).start()

    def step1(self, k):
        for i, (_, at, own) in enumerate(self.firsts(k)):
            self.copy1(k, i).wait_recv()
            self.add(own, self.got1, at)
            if i == 0:
                self.copy2(k).start()

    def step2(self, k):
        self.copy2(k).wait_recv()
        z = z_partner(self.z, k)
        self.add(self.block(self.y, z, self.x), self.got2, self.rows(k))
        if k:
            self.copy3(k).start()

    def steps1(self):
        for k in ORDER:
            self.step1(k)

    def steps2(self):
        for k in ORDER:
            self.step2(k)

    def finish(self, store):
        total = self.grad[self.block(self.y, self.z, self.x)].astype(F32)
        for k in (1, 2, 3):
            self.copy3(k).wait_recv()
            total += self.got3[self.rows(k - 1)].astype(F32)
        store(total)
        for k in range(4):
            for i in range(len(self.firsts(k))):
                self.copy1(k, i).wait_send()
            self.copy2(k).wait_send()
            if k:
                self.copy3(k).wait_send()


X_FIRST = (False, True, False, True, False, True, True, False, True, False, True)
STEP = 256


def back_kernel(*refs):
    hbm, rows, refs = refs[:15], refs[15], refs[16:]
    hid_h, slope_h, dout_h, a2_h, ctx_h, resid_h, joint_h, a1_h = hbm[:8]
    image_h, logsum_h, grad_h, wj_h, wo_h, w1_h, w2_h = hbm[8:]
    (layer_out, input_grad, own_wj, own_wo, own_w1, own_w2, totals), refs = refs[:7], refs[7:]
    (hid, slope, du, dout, a2, qkv, logsum, resid), refs = refs[:8], refs[8:]
    (wide_w, tall_w, total, dtotal, halves, sent, sums, got_sums), refs = refs[:8], refs[8:]
    stages, refs = [refs[11 * i : 11 * i + 11] for i in range(4)], refs[44:]
    (load_sem, stream_sem, tile_sem, sum_sem, swap_sem), refs = refs[:5], refs[5:]
    x, y, z, c = place()
    width = a2.shape[1]
    partner = dev(x, y, z, 1 - c)
    scatters = [
        Scatter(*[s[i] for s in stages], refs[3 * i : 3 * i + 3], X_FIRST[i]) for i in range(11)
    ]
    w1, w2, wo, wj = scatters[:4], scatters[4:6], scatters[6], scatters[7:]
    greet()

    def load(src, dst, n):
        copy = pltpu.make_async_copy(src, dst, load_sem.at[n])
        copy.start()
        return copy

    def span(index, size):
        return pl.ds(pl.multiple_of(index * size, 128), size)

    def load_quarter(q):
        cols = pl.ds(q * width, width)
        return [
            load(hid_h.at[:, cols], hid.at[q % 2], 2 * (q % 2)),
            load(slope_h.at[:, cols], slope.at[q % 2], 2 * (q % 2) + 1),
        ]

    def stream(q, s, slot):
        at = span(q * (width // STEP) + s, STEP)
        return (
            pltpu.make_async_copy(w1_h.at[:, at], wide_w.at[slot], stream_sem.at[slot, 0]),
            pltpu.make_async_copy(w2_h.at[at], tall_w.at[slot], stream_sem.at[slot, 1]),
        )

    parts = width // STEP
    halves_w2 = [
        load(grad_h.at[:, pl.ds(i * width // 2, width // 2)], w2[i].grad, 10 + i) for i in range(2)
    ]
    for copy in stream(0, 0, 0):
        copy.start()
    loads = load_quarter(0)
    loads += [load(dout_h, dout, 4), load(a2_h, a2, 5)]
    late = load(resid_h, resid, 6)
    total[...] = jnp.zeros_like(total)
    dtotal[...] = jnp.zeros_like(dtotal)

    def tile_copy(phase, j, slot, grad, at):
        src = sent.at[slot, :, pl.ds(0, at[1].size)]
        return remote(src, grad.at[at[0], at[1]], tile_sem.at[phase, j], partner)

    def merge(copy, grad, at, product):
        copy.wait_recv()
        grad[at] = (product + grad[at].astype(F32)).astype(LOW)

    def left(array, yy, own):
        return array[:, span(yy * 2 + (c if own else 1 - c), 256)]

    def both(phase, grad, product):
        def at(j):
            return span(j, 256), pl.ds(0, grad.shape[1])

        @pl.loop(0, 2)
        def _(j):
            sent[j, :, pl.ds(0, grad.shape[1])] = product(j, False).astype(LOW)
            tile_copy(phase, j, j, grad, at(j)).start()

        @pl.loop(0, 2)
        def _(j):
            merge(tile_copy(phase, j, j, grad, at(j)), grad, at(j), product(j, True))

        def drain():
            @pl.loop(0, 2)
            def _(j):
                tile_copy(phase, j, j, grad, at(j)).wait_send()

        return drain

    def feed_forward(q):
        for copy in loads:
            copy.wait()
        del loads[:]
        if q < 3:
            loads.extend(load_quarter(q + 1))

        @pl.loop(0, parts)
        def _(s):
            slot = lax.rem(s, 2)
            for copy in stream(q, s, slot):
                copy.wait()

            @pl.when(s + 1 < parts)
            def _():
                for copy in stream(q, s + 1, 1 - slot):
                    copy.start()

            if q < 3:

                @pl.when(s + 1 == parts)
                def _():
                    for copy in stream(q + 1, 0, 0):
                        copy.start()

            cols = span(s, STEP)
            low = (dot(dout[...], tall_w[slot], 1, 1) * slope[q % 2, :, cols].astype(F32)).astype(
                LOW
            )
            du[:, cols] = low
            total[...] += dot(hid[q % 2, :, cols], tall_w[slot])
            dtotal[...] += dot(low, wide_w[slot], 1, 1)

        sums[0, 8 + q : 9 + q, :] = column_sum(du[...])

    def column_sum(value):
        return jnp.sum(value.astype(F32), axis=0, keepdims=True)

    for i in range(2):
        halves_w2[i].wait()
        w2[i].start(0)
        if w2[i].x_first:
            w2[i].start(1)
    drain = None
    for q in range(4):
        feed_forward(q)
        if drain is not None:
            drain()
        drain = both(q, w1[q].grad, lambda j, own: dot(left(a2, j, own), du[...], 0, 0))
        w1[q].start(0)
        if w1[q].x_first:
            w1[q].start(1)
        if q == 2:
            w2[0].steps1()
            w2[1].steps1()
        if q == 3:
            w1[0].steps1()
            w1[1].steps1()
    ctx, dattn, dctx, a1 = hid.at[0], hid.at[1], slope.at[0], slope.at[1]
    loads = [load(ctx_h, ctx, 0), load(a1_h, a1, 1), load(joint_h, qkv, 2)]
    loads += [load(logsum_h, logsum, 3), load(image_h, a2, 5)]
    wo_loads = [load(wo_h.at[pl.ds(i * 256, 256)], tall_w.at[i], 7 + i) for i in range(2)]
    late.wait()
    gain, b2 = rows[1:2], rows[3:4]
    blocks = ((0, 304), (304, LEN - 304))
    pieces = [[] for _ in range(4)]
    for first, count in blocks:
        at = pl.ds(first, count)
        token = lax.broadcasted_iota(jnp.int32, (count, 1), 0) + first
        branch = total[at] + b2
        value = resid[at]
        result = value + branch
        total[at] = result
        hat, inverse = norm_parts(value)
        dactive = dtotal[at]
        grad = dout[at].astype(F32)
        pieces[3].append(column_sum(grad))
        resid[at] = grad + norm_back(dactive, gain, hat, inverse)
        pieces[0].append(column_sum(dactive * hat))
        pieces[1].append(column_sum(dactive))
        keep = token < VALID
        pieces[2].append(
            jnp.concatenate(
                [
                    column_sum(jnp.where(keep, result * result, 0.0)),
                    column_sum(jnp.where(keep, branch * branch, 0.0)),
                ],
                axis=0,
            )
        )
    add = [a + b for a, b in pieces]
    sums[0, 5:6] = add[0]
    sums[0, 6:7] = add[1]
    sums[0, 7:8] = add[3]
    sums[0, 12:13] = rows[5:6]
    sums[0, 13:15] = add[2]
    sums[0, 15:16] = jnp.zeros_like(add[0])
    half = LEN // 2
    for i in range(2):
        halves[i] = total[i * half : (i + 1) * half].astype(LOW)
    give = remote(halves.at[1 - c], layer_out.at[c], swap_sem.at[0], partner)
    give.start()
    hold = load(halves.at[c], layer_out.at[c], 9)
    dattn[...] = resid[...].astype(LOW)
    sums[0, 4:5] = column_sum(dattn[...])
    for i in range(4):
        wo_loads[i].wait()
        dctx[:, pl.ds(i * 256, 256)] = dot(dattn[...], tall_w[i % 2], 1, 1).astype(LOW)
        if i < 2:
            rows_at = pl.ds((i + 2) * 256, 256)
            wo_loads.append(load(wo_h.at[rows_at], tall_w.at[i], 7 + i))
    for copy in loads:
        copy.wait()
    drain()
    drain = both(4, wo.grad, lambda j, own: dot(left(ctx, j, own), dattn[...], 0, 0))
    wo.start(0)
    wo.start(1)
    w1[2].steps1()
    w1[3].steps1()
    factor = HEAD_DIM**-0.5
    pairs = width // 128

    def attend_back(t):
        def at(i):
            return span(i * pairs + t, 128)

        scaled = qkv[:, at(0)] * jnp.asarray(factor, LOW)
        dq, dk, dv = attend_pair_back(
            scaled, qkv[:, at(1)], qkv[:, at(2)], logsum[t], dctx[:, at(0)]
        )
        for i, grad in enumerate((dq * factor, dk, dv)):
            qkv[:, at(i)] = grad.astype(LOW)

    fetch = [load(wj_h.at[:, pl.ds(i * 256, 256)], wide_w.at[i], 7 + i) for i in range(2)]
    for n in range(4):
        pl.loop(2 * n, 2 * n + 2)(attend_back)
        drain()

        def product(j, own, n=n):
            rows_of = left(a1, j, own)
            columns = [qkv[:, pl.ds(i * width + n * 256, 256)] for i in range(3)]
            return jnp.concatenate([dot(rows_of, part, 0, 0) for part in columns], axis=1)

        drain = both(5 + n, wj[n].grad, product)
        wj[n].start(0)
        if wj[n].x_first:
            wj[n].start(1)
        if n == 0:
            w2[0].steps2()
            w2[1].steps2()
        if n == 1:
            w1[0].steps2()
            w1[1].steps2()
            wo.steps1()
        if n == 2:
            w1[2].steps2()
            w1[3].steps2()
        if n == 3:
            wj[0].steps1()
            wo.steps2()
    chunks = qkv.shape[1] // 256
    for i in range(chunks):
        fetch[i].wait()
        product = dot(qkv[:, pl.ds(i * 256, 256)], wide_w[i % 2], 1, 1)
        dtotal[...] = dtotal[...] + product if i else product
        if i + 2 < chunks:
            at = pl.ds((i + 2) * 256, 256)
            fetch.append(load(wj_h.at[:, at], wide_w.at[i % 2], 7 + i % 2))
        if i == 5:
            wj[1].steps1()
    wj[0].steps2()
    hold.wait()
    give.wait_send()
    pieces = [[] for _ in range(2)]
    for first, count in blocks:
        at = pl.ds(first, count)
        hat, inverse = norm_parts(a2[at].astype(F32))
        dactive = dtotal[at]
        resid[at] += norm_back(dactive, rows[4:5], hat, inverse)
        pieces[0].append(column_sum(dactive * hat))
        pieces[1].append(column_sum(dactive))
    for i in range(2):
        halves[i] = resid[i * half : (i + 1) * half].astype(LOW)
    give_grad = remote(halves.at[1 - c], input_grad.at[c], swap_sem.at[1], partner)
    give_grad.start()
    keep_grad = load(halves.at[c], input_grad.at[c], 9)
    sums[0, 0:1] = pieces[0][0] + pieces[0][1]
    sums[0, 1:2] = pieces[1][0] + pieces[1][1]
    sums[0, 2:3] = column_sum(qkv[:, :width])
    sums[0, 3:4] = column_sum(qkv[:, 2 * width :])
    near = [partner, dev(1 - x, y, z, c), dev(x, 1 - y, z, c)]
    near += [dev(x, y, z_partner(z, k), c) for k in (1, 2, 3)]
    sum_copies = [
        remote(sums.at[min(n, 3)], got_sums.at[n], sum_sem.at[n], near[n]) for n in range(6)
    ]
    sum_copies[0].start()

    def finish_w1(q):
        def store(value):
            own_w1[:, pl.ds(q * width, width)] = value

        w1[q].finish(store)

    def finish_wj(n):
        def store(value):
            for i in range(3):
                at = pl.ds(i * width + n * 256, 256)
                own_wj[:, at] = value[:, i * 256 : (i + 1) * 256]

        wj[n].finish(store)

    def put(out, first):
        def store(value):
            out[:, pl.ds(first, value.shape[1])] = value

        return store

    wj[2].steps1()
    for n in range(3):
        sum_copies[n].wait_recv()
        sums[n + 1] = sums[n] + got_sums[n]
        for copy in sum_copies[n + 1 : n + 2 if n < 2 else 6]:
            copy.start()
        if n == 0:
            wj[3].steps1()
        if n == 1:
            wj[1].steps2()
    wj[2].steps2()
    wj[3].steps2()
    for q in range(4):
        finish_w1(q)
    for i in range(2):
        w2[i].finish(put(own_w2, i * width // 2))
    wo.finish(put(own_wo, 0))
    for copy in sum_copies[3:]:
        copy.wait_recv()
    totals[...] = (sums[3] + got_sums[3]) + (got_sums[4] + got_sums[5])
    for n in range(4):
        finish_wj(n)
    drain()
    for copy in sum_copies:
        copy.wait_send()
    give.wait_recv()
    keep_grad.wait()
    give_grad.wait()


def back(hidden, slope, dout, active2, ctx, resid, joint, active1, image, logsum, *others):
    sds, vmem, dma = jax.ShapeDtypeStruct, pltpu.VMEM, pltpu.SemaphoreType.DMA
    width, wide = image.shape[1], hidden.shape[1]
    grads = [(width // 2, width)] * 4 + [(wide // 2, width // 2)] * 2 + [(width // 2, width)]
    grads += [(width // 2, 3 * width // 4)] * 4
    in_hbm = pl.BlockSpec(memory_space=pl.ANY)
    in_vmem = pl.BlockSpec(memory_space=pltpu.VMEM)
    low, full = vmem((LEN, width), LOW), vmem((LEN, width), F32)

    def stage(top, bottom):
        return [vmem((r * top // bottom, n), LOW) for r, n in grads]

    return pl.pallas_call(
        back_kernel,
        out_shape=[
            sds((2, LEN // 2, width), LOW),
            sds((2, LEN // 2, width), LOW),
            sds((width // 32, 3 * width), F32),
            sds((width // 32, width), F32),
            sds((width // 32, wide), F32),
            sds((wide // 32, width), F32),
            sds((16, width), F32),
        ],
        in_specs=[in_hbm] * 15 + [in_vmem],
        out_specs=[in_hbm] * 2 + [in_vmem] * 5,
        scratch_shapes=[
            vmem((2, LEN, width), LOW),
            vmem((2, LEN, width), LOW),
            low,
            low,
            low,
            vmem((LEN, 3 * width), LOW),
            vmem(logsum.shape, F32),
            full,
            vmem((2, width, STEP), LOW),
            vmem((2, STEP, width), LOW),
            full,
            full,
            vmem((2, LEN // 2, width), LOW),
            vmem((2, 256, width), LOW),
            vmem((4, 16, width), F32),
            vmem((6, 16, width), F32),
            *stage(1, 1),
            *stage(1, 2),
            *stage(1, 4),
            *stage(3, 16),
            dma((12,)),
            dma((2, 2)),
            dma((9, 2, 2)),
            dma((6, 2)),
            dma((2, 2)),
            *[s for _ in grads for s in (dma((8, 2)), dma((4, 2)), dma((3, 2)))],
        ],
        compiler_params=pltpu.CompilerParams(
            collective_id=2, has_side_effects=True, vmem_limit_bytes=VMEM_LIMIT
        ),
    )(hidden, slope, dout, active2, ctx, resid, joint, active1, image, logsum, *others)


def on_chip(
    inputs,
    cotangent,
    first_gain,
    first_shift,
    joint_weight,
    joint_bias,
    output_weight,
    output_bias,
    second_gain,
    second_shift,
    expand_weight,
    expand_bias,
    reduce_weight,
    reduce_bias,
):
    width = inputs.shape[2]
    smalls = [
        first_gain,
        first_shift,
        joint_bias,
        output_bias,
        second_gain,
        second_shift,
        expand_bias,
        reduce_bias,
    ]
    packed = jnp.concatenate([v.reshape(-1, 128) for v in smalls])
    packed = jnp.pad(packed, ((0, -packed.shape[0] % 16), (0, 0)))

    wj, wo, w1, w2, rows, b1, dout, image, active1, joint, ctx, logsum, *mid = front(
        inputs, cotangent, packed, (joint_weight, output_weight, expand_weight, reduce_weight)
    )
    resid, active2, hidden, slope, grad_w2 = mid
    held = (hidden, slope, dout, active2, ctx, resid, joint, active1, image, logsum)
    layer_out, input_grad, own_wj, own_wo, own_w1, own_w2, totals = back(
        *held, grad_w2, wj, wo, w1, w2, rows
    )
    rank = lax.axis_index("seq") * 8 + lax.axis_index("shard")

    def own(first, count=1):
        size = count * width // 32
        return lax.dynamic_slice(totals.reshape(-1), (first * width + rank * size,), (size,))

    own_g1, own_s1, own_bj, own_bo = own(0), own(1), own(2, 2), own(4)
    own_g2, own_s2, own_b2, own_b1 = own(5), own(6), own(7), own(8, b1.shape[1] // width)
    means = jnp.sum(totals[12:15], axis=1) / (VALID * width * 32)
    root_means = jnp.sqrt(means[jnp.array([1, 0, 2])] + 1e-06)
    return (
        layer_out,
        input_grad,
        own_g1,
        own_s1,
        own_wj,
        own_bj,
        own_wo,
        own_bo,
        own_g2,
        own_s2,
        own_w1,
        own_b1,
        own_w2,
        own_b2,
        root_means,
    )


def solution(mesh):
    whole_images = mesh.shape["seq"] == 4 and mesh.shape["shard"] == 8
    return jax.shard_map(
        on_chip if whole_images else on_device,
        mesh=mesh,
        in_specs=(
            P("shard", "seq", None),
            P("shard", "seq", None),
            P("shard"),
            P("shard"),
            P("shard", None),
            P("shard"),
            P("shard", None),
            P("shard"),
            P("shard"),
            P("shard"),
            P("shard", None),
            P("shard"),
            P("shard", None),
            P("shard"),
        ),
        out_specs=(
            P("shard", "seq", None),
            P("shard", "seq", None),
            P(("seq", "shard")),
            P(("seq", "shard")),
            P(("seq", "shard"), None),
            P(("seq", "shard")),
            P(("seq", "shard"), None),
            P(("seq", "shard")),
            P(("seq", "shard")),
            P(("seq", "shard")),
            P(("seq", "shard"), None),
            P(("seq", "shard")),
            P(("seq", "shard"), None),
            P(("seq", "shard")),
            P(),
        ),
        check_vma=False,
    )
```

```python
import functools

import jax
import jax.numpy as jnp
from jax import lax
from jax.experimental import pallas as pl
from jax.experimental.pallas import tpu as pltpu
from jax.sharding import PartitionSpec as P

MESH = pl.DeviceIdType.MESH
F32 = jnp.float32
LOW = jnp.bfloat16
HEAD_DIM = 64
LEN = 592
VALID = 577
PACK = 2
CUT = VALID // 16 * 16
SLOTS = 8
LEAD = (0, 2, 3, 4, 6)
VMEM_LIMIT = 61 << 20


def layer_norm(value, gain, shift):
    center = value - jnp.mean(value, axis=-1, keepdims=True)
    spread = jnp.mean(center * center, axis=-1, keepdims=True)
    return center * lax.rsqrt(spread + 1e-06) * gain + shift


def weight_grad(left, right):
    return lax.dot_general(
        left, right, (((0, 1), (0, 1)), ((), ())), preferred_element_type=jnp.float32
    )


def back_product(grad, matrix):
    return lax.dot_general(
        grad, matrix, (((2,), (1,)), ((), ())), preferred_element_type=jnp.float32
    )


def exact_gelu(value):
    return jax.nn.gelu(value, approximate=False)


def on_device(
    inputs,
    cotangent,
    first_gain,
    first_shift,
    joint_weight,
    joint_bias,
    output_weight,
    output_bias,
    second_gain,
    second_shift,
    expand_weight,
    expand_bias,
    reduce_weight,
    reduce_bias,
):
    images = inputs.shape[0]
    tokens = inputs.shape[1]
    full_seq = PACK * LEN
    pieces = images * PACK
    factor = HEAD_DIM ** (-0.5)
    begin = lax.axis_index("seq") * tokens
    local_places = begin + jnp.arange(tokens, dtype=jnp.int32)
    local_row = (local_places % LEN < VALID).astype(jnp.float32)
    local_mask = jnp.broadcast_to(local_row[None, :], (images, tokens))
    key_keep = jnp.arange(LEN, dtype=jnp.int32) < VALID
    weighting = local_mask[:, :, None]
    g1w, s1w, wj, bj, wo, bo, g2w, s2w, w1, b1, w2, b2 = (
        lax.all_gather(first_gain, "shard", axis=0, tiled=True),
        lax.all_gather(first_shift, "shard", axis=0, tiled=True),
        lax.all_gather(joint_weight, "shard", axis=0, tiled=True),
        lax.all_gather(joint_bias, "shard", axis=0, tiled=True),
        lax.all_gather(output_weight, "shard", axis=0, tiled=True),
        lax.all_gather(output_bias, "shard", axis=0, tiled=True),
        lax.all_gather(second_gain, "shard", axis=0, tiled=True),
        lax.all_gather(second_shift, "shard", axis=0, tiled=True),
        lax.all_gather(expand_weight, "shard", axis=0, tiled=True),
        lax.all_gather(expand_bias, "shard", axis=0, tiled=True),
        lax.all_gather(reduce_weight, "shard", axis=0, tiled=True),
        lax.all_gather(reduce_bias, "shard", axis=0, tiled=True),
    )
    g1f = g1w.astype(jnp.float32)
    s1f = s1w.astype(jnp.float32)
    bjf = bj.astype(jnp.float32)
    bof = bo.astype(jnp.float32)
    g2f = g2w.astype(jnp.float32)
    s2f = s2w.astype(jnp.float32)
    b1f = b1.astype(jnp.float32)
    b2f = b2.astype(jnp.float32)
    width = g1f.shape[0]
    xfull = inputs.astype(jnp.float32)
    normed1, first_back = jax.vjp(layer_norm, xfull, g1f, s1f)
    active1 = normed1.astype(jnp.bfloat16)
    bias_full = jnp.concatenate([bjf[:width], jnp.zeros((width,), jnp.float32), bjf[width:]])
    joint = (jnp.dot(active1, wj, preferred_element_type=jnp.float32) + bias_full).astype(
        jnp.bfloat16
    )
    joint = joint.reshape(images, tokens, 3, width)
    heads = lax.all_to_all(joint, "seq", split_axis=3, concat_axis=1, tiled=True)
    local_width = heads.shape[3]
    local_heads = local_width // HEAD_DIM
    query = heads[:, :, 0].reshape(pieces, LEN, local_heads, HEAD_DIM)
    keys = heads[:, :, 1].reshape(pieces, LEN, local_heads, HEAD_DIM)
    values = heads[:, :, 2].reshape(pieces, LEN, local_heads, HEAD_DIM)

    def score_block(qpart, kpart):
        raw = jnp.einsum("qhd,khd->hqk", qpart, kpart, preferred_element_type=jnp.float32) * factor
        return jnp.where(key_keep[None, None, :], raw, -1000000000.0)

    def attend(item):
        qpart, kpart, vpart = item
        scores = score_block(qpart, kpart)
        top = jnp.max(scores, axis=-1, keepdims=True)
        expo = jnp.exp(scores - top)
        total = jnp.sum(expo, axis=-1, keepdims=True)
        probs = expo / total
        logsum = (top + jnp.log(total))[:, :, 0]
        context = jnp.einsum(
            "hqk,khd->qhd", probs.astype(jnp.bfloat16), vpart, preferred_element_type=jnp.float32
        )
        return (context.astype(jnp.bfloat16).reshape(LEN, local_width), logsum)

    context, logsums = lax.map(attend, (query, keys, values))
    context = context.reshape(images, full_seq, local_width)
    gathered_ctx = lax.all_to_all(context, "seq", split_axis=1, concat_axis=2, tiled=True)
    attn = jnp.dot(gathered_ctx, wo, preferred_element_type=jnp.float32) + bof
    resid = xfull + attn
    normed2, second_back = jax.vjp(layer_norm, resid, g2f, s2f)
    active2 = normed2.astype(jnp.bfloat16)
    upper = jnp.dot(active2, w1, preferred_element_type=jnp.float32) + b1f
    activated, gelu_back = jax.vjp(exact_gelu, upper)
    hidden = activated.astype(jnp.bfloat16)
    branch = jnp.dot(hidden, w2, preferred_element_type=jnp.float32) + b2f
    result = resid + branch
    sums = jnp.stack(
        [
            jnp.sum(result * result * weighting),
            jnp.sum(attn * attn * weighting),
            jnp.sum(branch * branch * weighting),
        ]
    )
    counted = jnp.sum(local_mask) * width
    total_sums, total_count = lax.psum((sums, counted), ("seq", "shard"))
    root_means = jnp.sqrt(total_sums / total_count + 1e-06)
    wj, wo, w1, w2 = (
        lax.all_gather(joint_weight, "shard", axis=0, tiled=True),
        lax.all_gather(output_weight, "shard", axis=0, tiled=True),
        lax.all_gather(expand_weight, "shard", axis=0, tiled=True),
        lax.all_gather(reduce_weight, "shard", axis=0, tiled=True),
    )
    dout = cotangent.astype(jnp.float32) * weighting
    dout_low = dout.astype(jnp.bfloat16)
    grad_w2 = weight_grad(hidden, dout_low)
    grad_b2 = jnp.sum(dout, axis=(0, 1))
    dhidden = back_product(dout_low, w2)
    dupper = gelu_back(dhidden)[0].astype(jnp.bfloat16)
    grad_w1 = weight_grad(active2, dupper)
    grad_b1 = jnp.sum(dupper.astype(jnp.float32), axis=(0, 1))
    dactive2 = back_product(dupper, w1)
    dresid_norm, grad_g2, grad_s2 = second_back(dactive2)
    dresid = dout + dresid_norm
    dattn = dresid.astype(jnp.bfloat16)
    grad_wo = weight_grad(gathered_ctx, dattn)
    grad_bo = jnp.sum(dattn.astype(jnp.float32), axis=(0, 1))
    dcontext = back_product(dattn, wo).astype(jnp.bfloat16)
    dctx_heads = lax.all_to_all(dcontext, "seq", split_axis=2, concat_axis=1, tiled=True)
    dctx_heads = dctx_heads.reshape(pieces, LEN, local_heads, HEAD_DIM)

    def attend_back(item):
        qpart, kpart, vpart, logsum, dpart = item
        scores = score_block(qpart, kpart)
        probs = jnp.exp(scores - logsum[:, :, None])
        dprobs = jnp.einsum("qhd,khd->hqk", dpart, vpart, preferred_element_type=jnp.float32)
        dscore = (probs * (dprobs - jnp.sum(probs * dprobs, axis=-1, keepdims=True))).astype(
            jnp.bfloat16
        )
        dquery = (
            jnp.einsum("hqk,khd->qhd", dscore, kpart, preferred_element_type=jnp.float32) * factor
        )
        dkeys = (
            jnp.einsum("hqk,qhd->khd", dscore, qpart, preferred_element_type=jnp.float32) * factor
        )
        dvalues = jnp.einsum(
            "hqk,qhd->khd", probs.astype(jnp.bfloat16), dpart, preferred_element_type=jnp.float32
        )
        stacked = jnp.stack([dquery, dkeys, dvalues], axis=1).astype(jnp.bfloat16)
        return stacked.reshape(LEN, 3, local_width)

    dheads = lax.map(attend_back, (query, keys, values, logsums, dctx_heads))
    dheads = dheads.reshape(images, full_seq, 3, local_width)
    djoint = lax.all_to_all(dheads, "seq", split_axis=1, concat_axis=3, tiled=True)
    djoint = djoint.reshape(images, tokens, 3 * width)
    grad_wj = weight_grad(active1, djoint)
    joint_sums = jnp.sum(djoint.astype(jnp.float32), axis=(0, 1))
    grad_bj = jnp.concatenate([joint_sums[:width], joint_sums[2 * width :]])
    dactive1 = back_product(djoint, wj)
    dinput_norm, grad_g1, grad_s1 = first_back(dactive1)
    dinput = (dresid + dinput_norm).astype(jnp.bfloat16)
    (
        own_g1,
        own_s1,
        own_wj,
        own_bj,
        own_wo,
        own_bo,
        own_g2,
        own_s2,
        own_w1,
        own_b1,
        own_w2,
        own_b2,
    ) = (
        lax.psum_scatter(grad_g1, ("seq", "shard"), scatter_dimension=0, tiled=True),
        lax.psum_scatter(grad_s1, ("seq", "shard"), scatter_dimension=0, tiled=True),
        lax.psum_scatter(grad_wj, ("seq", "shard"), scatter_dimension=0, tiled=True),
        lax.psum_scatter(grad_bj, ("seq", "shard"), scatter_dimension=0, tiled=True),
        lax.psum_scatter(grad_wo, ("seq", "shard"), scatter_dimension=0, tiled=True),
        lax.psum_scatter(grad_bo, ("seq", "shard"), scatter_dimension=0, tiled=True),
        lax.psum_scatter(grad_g2, ("seq", "shard"), scatter_dimension=0, tiled=True),
        lax.psum_scatter(grad_s2, ("seq", "shard"), scatter_dimension=0, tiled=True),
        lax.psum_scatter(grad_w1, ("seq", "shard"), scatter_dimension=0, tiled=True),
        lax.psum_scatter(grad_b1, ("seq", "shard"), scatter_dimension=0, tiled=True),
        lax.psum_scatter(grad_w2, ("seq", "shard"), scatter_dimension=0, tiled=True),
        lax.psum_scatter(grad_b2, ("seq", "shard"), scatter_dimension=0, tiled=True),
    )
    return (
        result.astype(jnp.bfloat16),
        dinput,
        own_g1,
        own_s1,
        own_wj,
        own_bj,
        own_wo,
        own_bo,
        own_g2,
        own_s2,
        own_w1,
        own_b1,
        own_w2,
        own_b2,
        root_means,
    )


def place():
    seq = lax.axis_index("seq")
    shard = lax.axis_index("shard")
    return lax.rem(shard, 2), lax.div(seq, 2), lax.div(shard, 2), lax.rem(seq, 2)


def z_partner(z, k):
    if k == 0:
        return z
    if k == 1:
        return z + 1 - 2 * lax.rem(z, 2)
    if k == 2:
        return lax.rem(z + 2, 4)
    return 3 - z


def dev(x, y, z, c):
    return (y * 2 + c, z * 2 + x)


def remote(src, dst, sem, target):
    return pltpu.make_async_remote_copy(
        src_ref=src,
        dst_ref=dst,
        send_sem=sem.at[0],
        recv_sem=sem.at[1],
        device_id=target,
        device_id_type=MESH,
    )


def greet():
    x, y, z, c = place()
    barrier = pltpu.get_barrier_semaphore()
    near = [dev(x, y, z_partner(z, k), c) for k in (1, 2, 3)]
    near += [dev(1 - x, y, z, c), dev(x, 1 - y, z, c), dev(x, y, z, 1 - c)]
    for who in near:
        pl.semaphore_signal(barrier, inc=1, device_id=who, device_id_type=MESH)
    pl.semaphore_wait(barrier, len(near))


class Gather:
    def __init__(self, part, full, piece, sems, slot):
        self.part, self.full = part, full
        self.zs, self.xs, self.ys, self.cs, self.es, self.own = [s.at[slot] for s in sems]
        self.shard_rows = part.shape[0]
        self.row, self.rows, self.col, self.cols = piece
        edge = self.cols * 3 // 8 // 128 * 128
        span = self.cols - edge
        self.x, self.y, self.z, self.c = place()
        self.duty = pl.ds(pl.multiple_of(self.col + self.y * edge, 128), span)
        self.mine = pl.ds(pl.multiple_of(self.col + self.y * span, 128), edge)
        self.other = pl.ds(pl.multiple_of(self.col + (1 - self.y) * span, 128), edge)

    def half(self, k, j):
        x = self.x if j == 0 else 1 - self.x
        shard = z_partner(self.z, k) * 2 + x
        half = self.rows // 2
        first = shard * self.shard_rows + self.row + self.c * half
        return pl.ds(pl.multiple_of(first, 16), half)

    def copy(self, k, j, cols, sem, target, local=False):
        at = (self.half(k, j), cols)
        src = self.full.at[at]
        if local:
            half = self.rows // 2
            src = self.part.at[pl.ds(pl.multiple_of(self.row + self.c * half, 16), half), cols]
        return remote(src, self.full.at[at], sem, target)

    def over_z(self, k):
        target = dev(self.x, self.y, z_partner(self.z, k), self.c)
        return self.copy(0, 0, self.duty, self.zs.at[k - 1], target, local=True)

    def over_x(self, k):
        target = dev(1 - self.x, self.y, self.z, self.c)
        return self.copy(k, 0, self.duty, self.xs.at[k], target, local=k == 0)

    def over_y(self, k, j):
        target = dev(self.x, 1 - self.y, self.z, self.c)
        return self.copy(k, j, self.mine, self.ys.at[k * 2 + j], target)

    def over_core(self, k, j):
        target = dev(self.x, self.y, self.z, 1 - self.c)
        return self.copy(k, j, self.duty, self.cs.at[k * 2 + j], target)

    def over_core_rest(self, k, j):
        target = dev(self.x, self.y, self.z, 1 - self.c)
        return self.copy(k, j, self.other, self.es.at[k * 2 + j], target)

    def own_copy(self):
        shard = self.z * 2 + self.x
        cols = pl.ds(self.col, self.cols)
        rows = pl.ds(pl.multiple_of(shard * self.shard_rows + self.row, 16), self.rows)
        src = self.part.at[pl.ds(self.row, self.rows), cols]
        target = dev(self.x, self.y, self.z, 1 - self.c)
        return remote(src, self.full.at[rows, cols], self.own, target)

    def step0(self):
        for k in (1, 2, 3):
            self.over_z(k).start()
        self.over_x(0).start()
        self.own_copy().start()

    def step1(self):
        for k in (1, 2, 3):
            self.over_z(k).wait_recv()
            self.over_x(k).start()
            self.over_y(k, 0).start()
            self.over_core(k, 0).start()

    def step2(self):
        for k in (0, 1, 2, 3):
            self.over_x(k).wait_recv()
            self.over_y(k, 1).start()
            self.over_core(k, 1).start()

    def others(self):
        return [(k, 0) for k in (1, 2, 3)] + [(k, 1) for k in (0, 1, 2, 3)]

    def step3(self):
        for k, j in self.others():
            self.over_y(k, j).wait_recv()
            self.over_core_rest(k, j).start()

    def step4(self):
        for k, j in self.others():
            self.over_core(k, j).wait()
            self.over_core_rest(k, j).wait()
            self.over_y(k, j).wait_send()
        for k in (1, 2, 3):
            self.over_z(k).wait_send()
        for k in range(4):
            self.over_x(k).wait_send()
        self.own_copy().wait()


class SmallGather:
    def __init__(self, part, full, zs, xs, own):
        self.part, self.full, self.zs, self.xs, self.own = part, full, zs, xs, own
        self.x, self.y, self.z, self.c = place()

    def at(self, k):
        rows = self.part.shape[0]
        shard = z_partner(self.z, k) * 2 + self.x
        return pl.ds(pl.multiple_of(shard * rows, rows), rows)

    def over_z(self, k):
        target = dev(self.x, self.y, z_partner(self.z, k), self.c)
        return remote(self.part, self.full.at[self.at(0)], self.zs.at[k - 1], target)

    def over_x(self, k):
        target = dev(1 - self.x, self.y, self.z, self.c)
        src = self.full.at[self.at(k)] if k else self.part
        return remote(src, self.full.at[self.at(k)], self.xs.at[k], target)

    def own_copy(self):
        return pltpu.make_async_copy(self.part, self.full.at[self.at(0)], self.own.at[0])

    def step0(self):
        for k in (1, 2, 3):
            self.over_z(k).start()
        self.over_x(0).start()
        self.own_copy().start()

    def step1(self):
        for k in (1, 2, 3):
            self.over_z(k).wait_recv()
            self.over_x(k).start()

    def step4(self):
        for k in range(4):
            self.over_x(k).wait()
        for k in (1, 2, 3):
            self.over_z(k).wait_send()
        self.own_copy().wait()


def dot(left, right, left_axis=1, right_axis=0):
    return lax.dot_general(
        left,
        right,
        (((left_axis,), (right_axis,)), ((), ())),
        preferred_element_type=F32,
    )


def norm_parts(value):
    center = value - jnp.mean(value, axis=-1, keepdims=True)
    inverse = lax.rsqrt(jnp.mean(center * center, axis=-1, keepdims=True) + 1e-06)
    return center * inverse, inverse


def norm_back(grad, gain, hat, inverse):
    scaled = grad * gain
    mean = jnp.mean(scaled, axis=-1, keepdims=True)
    return inverse * (scaled - mean - hat * jnp.mean(scaled * hat, axis=-1, keepdims=True))


def keep_keys(scores):
    row = lax.broadcasted_iota(jnp.int32, (LEN - CUT, scores.shape[1]), 0) + CUT
    last = jnp.where(row < VALID, scores[CUT:], -1000000000.0)
    return jnp.concatenate([scores[:CUT], last], axis=0)


def by_head(value):
    lane = lax.broadcasted_iota(jnp.int32, value.shape, 1)
    none = jnp.zeros_like(value)
    return jnp.where(lane < HEAD_DIM, value, none), jnp.where(lane < HEAD_DIM, none, value)


def attend_pair(query, keys, values, store):
    total_ctx = None
    for i, (q, v) in enumerate(zip(by_head(query), by_head(values))):
        scores = keep_keys(dot(keys, q, 1, 1))
        top = jnp.max(scores, axis=0, keepdims=True)
        expo = jnp.exp(scores - top)
        total = jnp.sum(expo, axis=0, keepdims=True)
        probs = (expo * (1.0 / total)).astype(LOW)
        store(i, probs)
        ctx = dot(probs, v, 0, 0)
        total_ctx = ctx if total_ctx is None else total_ctx + ctx
    return total_ctx


def vector_row(table, rows, first, count):
    at = [s * rows + first + i for s in range(8) for i in range(count)]
    pieces = [table[r : r + 1] for r in at]
    return jnp.concatenate(pieces, axis=1)


def front_plan(shapes):
    (dj, cj), (do, co), (de, ce), (dr, cr) = shapes
    plan = [(0, (0, dj, i * (cj // 3), cj // 3)) for i in range(3)]
    plan += [(1, (0, do, 0, co))]
    plan += [(2, (0, de, i * (ce // 4), ce // 4)) for i in range(4)]
    plan += [(3, (i * (dr // 4), dr // 4, 0, cr)) for i in range(4)]
    return plan


def front_kernel(x_part, d_part, packed, wj, wo, w1, w2, *refs):
    fulls, outs, refs = refs[:4], refs[4:17], refs[17:]
    (rows_out, b1_out), hbm_outs = outs[:2], outs[2:]
    dout, image, active, joint, ctx, probs, active2, hidden, slope = refs[:9]
    table, own_half, far_half, weight, xf, grad, sent, out_sem, tile_sem, probs_sem, *sems = refs[9:]
    parts = (wj, wo, w1, w2)
    half_sem, fetch_sem, small_sems, sems = sems[0], sems[1], sems[2:5], sems[5:]
    x, y, z, c = place()
    greet()
    small = SmallGather(packed, table, *small_sems)
    small.step0()
    partner = dev(x, y, z, 1 - c)
    swaps, keeps = [], []
    for i, source in enumerate((x_part, d_part)):
        swaps.append(remote(source.at[1 - c], far_half.at[i], half_sem.at[2 * i], partner))
        keeps.append(
            pltpu.make_async_copy(source.at[c], own_half.at[i], half_sem.at[2 * i + 1, 0])
        )
        swaps[i].start()
        keeps[i].start()

    def whole(i):
        keeps[i].wait()
        swaps[i].wait()
        own, far = own_half[i].astype(F32), far_half[i].astype(F32)
        first, second = jnp.where(c == 0, own, far), jnp.where(c == 0, far, own)
        return jnp.concatenate([first, second], axis=0)

    plan = front_plan([p.shape for p in parts])
    pieces = [
        Gather(parts[w], fulls[w], piece, sems, i % SLOTS) for i, (w, piece) in enumerate(plan)
    ]

    last = len(pieces) - 4

    def turn(t):
        for step in (4, 3, 2, 1, 0):
            i = t - LEAD[step]
            if 0 <= i < (last if step == 4 else len(pieces)):
                getattr(pieces[i], f"step{step}")()

    stores = []

    def store(src, n, at=None):
        dst = hbm_outs[n] if at is None else hbm_outs[n].at[at]
        stores.append(pltpu.make_async_copy(src, dst, out_sem.at[len(stores)]))
        stores[-1].start()

    def fetch(source, cols, slot=0):
        copy = pltpu.make_async_copy(source.at[:, cols], weight.at[slot], fetch_sem.at[slot])
        copy.start()
        return copy

    width = active.shape[1]
    rows = packed.shape[0]
    for t in range(9):
        turn(t)
        if t == 1:
            small.step1()
        if t == 2:
            xf[...] = whole(0)
            image[...] = xf[...].astype(LOW)
            store(image, 1)
        if t == 3:
            small.step4()
            hat, _ = norm_parts(xf[...])
            vectors = table[...].astype(F32)
            gain, shift = vector_row(vectors, rows, 0, 1), vector_row(vectors, rows, 1, 1)
            active[...] = (hat * gain + shift).astype(LOW)
            store(active, 2)
            for i, first in enumerate((4, 5, 6, 11, 0, 0, 0, 0)):
                rows_out[i : i + 1] = vector_row(vectors, rows, first, 1)
            b1_out[...] = vector_row(vectors, rows, 7, 4)
        if t == 4:
            token = lax.broadcasted_iota(jnp.int32, (LEN, 1), 0)
            dout[...] = jnp.where(token < VALID, whole(1), 0.0).astype(LOW)
            store(dout, 0)
        if t >= 6:
            cols = pl.ds((t - 6) * width, width)
            fetch(fulls[0], cols).wait()
            product = dot(active[...], weight[0])
            if t != 7:
                bias = vector_row(table[...].astype(F32), rows, 2, 2)
                product += bias[:, :width] if t == 6 else bias[:, width:]
            joint[:, cols] = product.astype(LOW)
    store(joint, 3)

    pairs = width // 128

    def save(t):
        slot = lax.rem(t, 2)
        return pltpu.make_async_copy(probs.at[slot], hbm_outs[5].at[t], probs_sem.at[slot])

    @pl.loop(0, pairs)
    def _(t):
        for i in range(3):
            pl.when(t == 2 * i + 2)(functools.partial(turn, 9 + i))

        def at(i):
            return pl.ds(pl.multiple_of(i * width + t * 128, 128), 128)

        slot = lax.rem(t, 2)

        @pl.when(t > 1)
        def _():
            save(t - 2).wait()

        def put(i, value):
            probs[slot, i] = value

        query = joint[:, at(0)] * jnp.asarray(HEAD_DIM**-0.5, LOW)
        ctx[:, at(0)] = attend_pair(query, joint[:, at(1)], joint[:, at(2)], put).astype(LOW)
        save(t).start()

    store(ctx, 4)
    for t in (pairs - 2, pairs - 1):
        save(jnp.int32(t)).wait()
    fetch(fulls[1], pl.ds(0, width)).wait()
    coming = fetch(fulls[2], pl.ds(0, width), 1)
    attn = dot(ctx[...], weight[0]) + rows_out[0:1]
    keep = lax.broadcasted_iota(jnp.int32, (LEN, 1), 0) < VALID
    rows_out[5:6] = jnp.sum(jnp.where(keep, attn * attn, 0.0), axis=0, keepdims=True)
    xf[...] += attn
    store(xf, 6)
    hat, _ = norm_parts(xf[...])
    active2[...] = (hat * rows_out[1:2] + rows_out[2:3]).astype(LOW)
    store(active2, 7)
    chunks = b1_out.shape[1] // width
    begin = len(stores)

    def reduce_grad(yy):
        def rows_at(j):
            return pl.ds(pl.multiple_of(yy * width + j * 256, 256), 256)

        def copy(j):
            slot = sent.at[lax.rem(j, 2)]
            return remote(slot, grad.at[rows_at(j)], tile_sem.at[yy, j], partner)

        def product(core, j):
            cols = pl.ds(pl.multiple_of(j * 256, 256), 256)
            return dot(hidden[core, :, cols], dout[...], 0, 0)

        @pl.loop(0, width // 256)
        def _(j):
            @pl.when(j > 1)
            def _():
                copy(j - 2).wait_send()

            sent[lax.rem(j, 2)] = product(1 - c, j).astype(LOW)
            copy(j).start()

        @pl.loop(0, width // 256)
        def _(j):
            copy(j).wait_recv()
            at = rows_at(j)
            grad[at] = (product(c, j) + grad[at].astype(F32)).astype(LOW)

        for j in range(width // 256 - 2, width // 256):
            copy(j).wait_send()

    for j in range(chunks):
        if j in (0, 3):
            turn(12 if j == 0 else 14)
        coming.wait()
        slot = j % 2
        if j + 1 < chunks:
            coming = fetch(fulls[2], pl.ds((j + 1) * width, width), 1 - (j + 1) % 2)
        if j > 1:
            for copy in stores[begin + 4 * j - 8 : begin + 4 * j - 4]:
                copy.wait()
        for i in range(2):
            cols = pl.ds(i * width // 2, width // 2)
            there = pl.ds(j * width + i * width // 2, width // 2)
            upper = dot(active2[...], weight[1 - slot, :, cols]) + b1_out[:, there]
            share = 0.5 * (1.0 + lax.erf(upper * 0.7071067811865476))
            density = jnp.exp(upper * upper * -0.5) * 0.3989422804014327
            hidden[slot, :, cols] = (upper * share).astype(LOW)
            slope[slot, :, cols] = (share + upper * density).astype(LOW)
            store(hidden.at[slot, :, cols], 8, (slice(None), there))
            store(slope.at[slot, :, cols], 9, (slice(None), there))
        if j % 2:
            turn(13 if j == 1 else 15)
            reduce_grad(j // 2)
    store(grad, 10)
    for piece in pieces[last:]:
        piece.step4()
    for n, copy in enumerate(stores):
        if not begin <= n < begin + 4 * chunks - 8:
            copy.wait()


def front(x_part, d_part, packed, parts):
    sds, vmem, dma = jax.ShapeDtypeStruct, pltpu.VMEM, pltpu.SemaphoreType.DMA
    tokens, width = x_part.shape[1:]
    wide = parts[2].shape[1]
    pairs = width // 128
    hbm, in_vmem = pl.BlockSpec(memory_space=pl.ANY), pl.BlockSpec(memory_space=pltpu.VMEM)
    full = (LEN, width)
    return pl.pallas_call(
        front_kernel,
        out_shape=[sds((p.shape[0] * 8, p.shape[1]), LOW) for p in parts]
        + [
            sds((8, width), F32),
            sds((1, wide), F32),
            sds(full, LOW),
            sds(full, LOW),
            sds(full, LOW),
            sds((LEN, 3 * width), LOW),
            sds(full, LOW),
            sds((pairs, 2, LEN, LEN), LOW),
            sds(full, F32),
            sds(full, LOW),
            sds((LEN, wide), LOW),
            sds((LEN, wide), LOW),
            sds((wide // 2, width), LOW),
        ],
        in_specs=[hbm] * 7,
        out_specs=[hbm] * 4 + [in_vmem] * 2 + [hbm] * 11,
        scratch_shapes=[
            vmem(full, LOW),
            vmem(full, LOW),
            vmem(full, LOW),
            vmem((LEN, 3 * width), LOW),
            vmem(full, LOW),
            vmem((2, 2, LEN, LEN), LOW),
            vmem(full, LOW),
            vmem((2, LEN, width), LOW),
            vmem((2, LEN, width), LOW),
            vmem((packed.shape[0] * 8, 128), LOW),
            vmem((2, tokens, width), LOW),
            vmem((2, tokens, width), LOW),
            vmem((2, width, width), LOW),
            vmem(full, F32),
            vmem((wide // 2, width), LOW),
            vmem((2, 256, width), LOW),
            dma((8 + 4 * (wide // width),)),
            dma((2, width // 256, 2)),
            dma((2,)),
            dma((4, 2)),
            dma((2,)),
            dma((3, 2)),
            dma((4, 2)),
            dma((1,)),
            dma((SLOTS, 3, 2)),
            dma((SLOTS, 4, 2)),
            dma((SLOTS, 8, 2)),
            dma((SLOTS, 8, 2)),
            dma((SLOTS, 8, 2)),
            dma((SLOTS, 2)),
        ],
        compiler_params=pltpu.CompilerParams(
            collective_id=1, has_side_effects=True, vmem_limit_bytes=VMEM_LIMIT
        ),
    )(x_part, d_part, packed, *parts)


def attend_pair_back(query, keys, values, probs, dctx):
    heads = [by_head(v) for v in (query, keys, dctx)]
    sums = None
    for i in range(2):
        q, k, d = [h[i] for h in heads]
        low = probs[i]
        wide = low.astype(F32)
        dprobs = dot(values, d, 1, 1)
        inner = jnp.sum(wide * dprobs, axis=0, keepdims=True)
        dscore = (wide * (dprobs - inner)).astype(LOW)
        grads = (dot(dscore, k, 0, 0), dot(dscore, q), dot(low, d))
        sums = grads if sums is None else tuple(a + b for a, b in zip(sums, grads))
    return sums


class Scatter:
    def __init__(self, grad, got, sems, order):
        self.grad, self.got, self.sems, self.order = grad, got, sems, order
        self.size = grad.shape[0] // 16
        x, y, z, c = place()
        self.own = {"y": y, "x": x, "n": lax.rem(z, 2), "f": lax.div(z, 2)}
        self.targets = {
            "y": dev(x, 1 - y, z, c),
            "x": dev(1 - x, y, z, c),
            "n": dev(x, y, z_partner(z, 1), c),
            "f": dev(x, y, z_partner(z, 2), c),
        }

    def block(self, away):
        at = {d: 1 - v if d in away else v for d, v in self.own.items()}
        index = (at["y"] * 4 + at["f"] * 2 + at["n"]) * 2 + at["x"]
        return pl.ds(pl.multiple_of(index * self.size, 16), self.size)

    def choices(self, stage):
        found = [()]
        for d in reversed(self.order[stage + 1 :]):
            found = [(d, *f) for f in found] + found
        return found

    def copy(self, stage, n):
        away = self.choices(stage)[n]
        slot = (0, 8, 12, 14)[stage] + n
        src = self.grad.at[self.block((self.order[stage], *away))]
        dst = self.got.at[pl.ds(slot * self.size, self.size)]
        return remote(src, dst, self.sems.at[slot], self.targets[self.order[stage]])

    def start(self):
        for n in range(8):
            self.copy(0, n).start()

    def step(self, stage):
        later = self.choices(stage + 1)
        choices = self.choices(stage)
        for n, away in enumerate(choices):
            self.copy(stage, n).wait_recv()
            rows = self.block(away)
            slot = (0, 8, 12, 14)[stage] + n
            got = self.got[pl.ds(slot * self.size, self.size)]
            self.grad[rows] = self.grad[rows] + got
            if self.order[stage + 1] in away:
                rest = tuple(d for d in away if d != self.order[stage + 1])
                self.copy(stage + 1, later.index(rest)).start()

    def finish(self, store):
        self.copy(3, 0).wait_recv()
        got = self.got[pl.ds(14 * self.size, self.size)]
        store(self.grad[self.block(())].astype(F32) + got.astype(F32))
        for stage in range(4):
            for n in range(8 >> stage):
                self.copy(stage, n).wait_send()


ORDERS = ("nyxf", "nxyf", "nyxf", "nxyf", "yxnf", "xynf", "yxnf", "yxnf", "xynf", "yxnf", "xynf")
STEP = 512
AFTER_HEADS = (
    ((3, 0), (1, 1), (4, 2), (5, 2), (0, 2), (2, 1)),
    ((6, 0), (1, 2), (3, 1)),
    ((7, 0), (2, 2), (6, 1)),
    ((8, 0), (3, 2), (7, 1), (6, 2)),
)


def back_kernel(*refs):
    hbm, rows, refs = refs[:15], refs[15], refs[16:]
    hid_h, slope_h, dout_h, a2_h, ctx_h, resid_h, joint_h, a1_h = hbm[:8]
    image_h, probs_h, grad_h, wj_h, wo_h, w1_h, w2_h = hbm[8:]
    (layer_out, input_grad, own_wj, own_wo, own_w1, own_w2, totals), refs = refs[:7], refs[7:]
    (hid, slope, du, dout, a2, qkv, probs, resid), refs = refs[:8], refs[8:]
    (wide_w, tall_w, total, dtotal, halves, sent, sums, got_sums), refs = refs[:8], refs[8:]
    (grads, gots), refs = (refs[:11], refs[11:22]), refs[22:]
    (load_sem, stream_sem, tile_sem, sum_sem, swap_sem), sems = refs[:5], refs[5:]
    x, y, z, c = place()
    width = a2.shape[1]
    partner = dev(x, y, z, 1 - c)
    scatters = [Scatter(*args) for args in zip(grads, gots, sems, ORDERS)]
    w1, w2, wo, wj = scatters[:4], scatters[4:6], scatters[6], scatters[7:]
    greet()

    def load(src, dst, n):
        copy = pltpu.make_async_copy(src, dst, load_sem.at[n])
        copy.start()
        return copy

    def span(index, size):
        return pl.ds(pl.multiple_of(index * size, 128), size)

    def load_quarter(q):
        cols = pl.ds(q * width, width)
        return [
            load(hid_h.at[:, cols], hid.at[q % 2], 2 * (q % 2)),
            load(slope_h.at[:, cols], slope.at[q % 2], 2 * (q % 2) + 1),
        ]

    def stream(q, s, slot):
        at = span(q * (width // STEP) + s, STEP)
        return (
            pltpu.make_async_copy(w1_h.at[:, at], wide_w.at[slot], stream_sem.at[slot, 0]),
            pltpu.make_async_copy(w2_h.at[at], tall_w.at[slot], stream_sem.at[slot, 1]),
        )

    parts = width // STEP
    halves_w2 = [
        load(grad_h.at[:, pl.ds(i * width // 2, width // 2)], w2[i].grad, 10 + i) for i in range(2)
    ]
    for copy in stream(0, 0, 0):
        copy.start()
    loads = load_quarter(0)
    loads += [load(dout_h, dout, 4), load(a2_h, a2, 5)]
    late = load(resid_h, resid, 6)
    total[...] = jnp.zeros_like(total)
    dtotal[...] = jnp.zeros_like(dtotal)

    def left(array, own):
        core = c if own else 1 - c
        return jnp.concatenate([array[:, span(core, 256)], array[:, span(2 + core, 256)]], axis=1)

    def both(phase, grad, product):
        slot = sent.at[:, pl.ds(0, grad.shape[1])]
        slot[...] = product(False).astype(LOW)
        copy = remote(slot, grad, tile_sem.at[phase], partner)
        copy.start()
        own = product(True)
        copy.wait_recv()
        grad[...] = (own + grad[...].astype(F32)).astype(LOW)
        return copy.wait_send

    def feed_forward(q):
        for copy in loads:
            copy.wait()
        del loads[:]
        if q < 3:
            loads.extend(load_quarter(q + 1))

        @pl.loop(0, parts)
        def _(s):
            slot = lax.rem(s, 2)
            for copy in stream(q, s, slot):
                copy.wait()

            @pl.when(s + 1 < parts)
            def _():
                for copy in stream(q, s + 1, 1 - slot):
                    copy.start()

            if q < 3:

                @pl.when(s + 1 == parts)
                def _():
                    for copy in stream(q + 1, 0, 0):
                        copy.start()

            cols = span(s, STEP)
            low = (dot(dout[...], tall_w[slot], 1, 1) * slope[q % 2, :, cols].astype(F32)).astype(
                LOW
            )
            du[:, cols] = low
            total[...] += dot(hid[q % 2, :, cols], tall_w[slot])
            dtotal[...] += dot(low, wide_w[slot], 1, 1)

        sums[0, 8 + q : 9 + q, :] = column_sum(du[...])

    def column_sum(value):
        return jnp.sum(value.astype(F32), axis=0, keepdims=True)

    for i in range(2):
        halves_w2[i].wait()
        w2[i].start()
    drain = None
    for q in range(4):
        feed_forward(q)
        if drain is not None:
            drain()
        drain = both(q, w1[q].grad, lambda own: dot(left(a2, own), du[...], 0, 0))
        w1[q].start()
        if q == 2:
            w2[0].step(0)
            w2[1].step(0)
            w1[0].step(0)
        if q == 3:
            w1[1].step(0)
    ctx, dattn, dctx, a1 = hid.at[0], hid.at[1], slope.at[0], slope.at[1]
    loads = [load(ctx_h, ctx, 0), load(a1_h, a1, 1), load(joint_h, qkv, 2)]
    loads += [load(probs_h.at[i], probs.at[i], 14 + i) for i in range(2)]
    loads += [load(image_h, a2, 5)]
    wo_loads = [load(wo_h.at[pl.ds(i * STEP, STEP)], tall_w.at[i], 7 + i) for i in range(2)]
    late.wait()
    gain, b2 = rows[1:2], rows[3:4]
    blocks = ((0, 304), (304, LEN - 304))
    pieces = [[] for _ in range(4)]
    for first, count in blocks:
        at = pl.ds(first, count)
        token = lax.broadcasted_iota(jnp.int32, (count, 1), 0) + first
        branch = total[at] + b2
        value = resid[at]
        result = value + branch
        total[at] = result
        hat, inverse = norm_parts(value)
        dactive = dtotal[at]
        grad = dout[at].astype(F32)
        pieces[3].append(column_sum(grad))
        resid[at] = grad + norm_back(dactive, gain, hat, inverse)
        pieces[0].append(column_sum(dactive * hat))
        pieces[1].append(column_sum(dactive))
        keep = token < VALID
        pieces[2].append(
            jnp.concatenate(
                [
                    column_sum(jnp.where(keep, result * result, 0.0)),
                    column_sum(jnp.where(keep, branch * branch, 0.0)),
                ],
                axis=0,
            )
        )
    add = [a + b for a, b in pieces]
    sums[0, 5:6] = add[0]
    sums[0, 6:7] = add[1]
    sums[0, 7:8] = add[3]
    sums[0, 12:13] = rows[5:6]
    sums[0, 13:15] = add[2]
    sums[0, 15:16] = jnp.zeros_like(add[0])
    half = LEN // 2
    for i in range(2):
        halves[i] = total[i * half : (i + 1) * half].astype(LOW)
    give = remote(halves.at[1 - c], layer_out.at[c], swap_sem.at[0], partner)
    give.start()
    hold = load(halves.at[c], layer_out.at[c], 9)
    w2[0].step(1)
    w2[1].step(1)
    dattn[...] = resid[...].astype(LOW)
    sums[0, 4:5] = column_sum(dattn[...])
    for i in range(2):
        wo_loads[i].wait()
        dctx[:, pl.ds(i * STEP, STEP)] = dot(dattn[...], tall_w[i], 1, 1).astype(LOW)
    for copy in loads:
        copy.wait()
    drain()
    drain = both(4, wo.grad, lambda own: dot(left(ctx, own), dattn[...], 0, 0))
    wo.start()
    w1[2].step(0)
    w1[0].step(1)
    factor = HEAD_DIM**-0.5
    pairs = width // 128

    def attend_back(t):
        def at(i):
            return span(i * pairs + t, 128)

        def fetch_probs(t):
            slot = lax.rem(t, 2)
            return pltpu.make_async_copy(probs_h.at[t], probs.at[slot], load_sem.at[14 + slot])

        @pl.when(t > 1)
        def _():
            fetch_probs(t).wait()

        scaled = qkv[:, at(0)] * jnp.asarray(factor, LOW)
        dq, dk, dv = attend_pair_back(
            scaled, qkv[:, at(1)], qkv[:, at(2)], probs.at[lax.rem(t, 2)], dctx[:, at(0)]
        )
        for i, grad in enumerate((dq * factor, dk, dv)):
            qkv[:, at(i)] = grad.astype(LOW)

        @pl.when(t + 2 < pairs)
        def _():
            fetch_probs(t + 2).start()

    fetch = [load(wj_h.at[:, pl.ds(i * STEP, STEP)], wide_w.at[i], 7 + i) for i in range(2)]
    for n in range(4):
        pl.loop(2 * n, 2 * n + 2)(attend_back)
        drain()

        def product(own, n=n):
            rows_of = left(a1, own)
            columns = [qkv[:, pl.ds(i * width + n * 256, 256)] for i in range(3)]
            return jnp.concatenate([dot(rows_of, part, 0, 0) for part in columns], axis=1)

        drain = both(5 + n, wj[n].grad, product)
        wj[n].start()
        for scatter, stage in AFTER_HEADS[n]:
            scatters[scatter].step(stage)
    chunks = qkv.shape[1] // STEP
    for i in range(chunks):
        fetch[i].wait()
        product = dot(qkv[:, pl.ds(i * STEP, STEP)], wide_w[i % 2], 1, 1)
        dtotal[...] = dtotal[...] + product if i else product
        if i + 2 < chunks:
            at = pl.ds((i + 2) * STEP, STEP)
            fetch.append(load(wj_h.at[:, at], wide_w.at[i % 2], 7 + i % 2))
        if i == 2:
            wj[2].step(0)
            wj[1].step(1)
    wj[3].step(0)
    wj[0].step(2)
    wj[2].step(1)
    hold.wait()
    give.wait_send()
    pieces = [[] for _ in range(2)]
    for first, count in blocks:
        at = pl.ds(first, count)
        hat, inverse = norm_parts(a2[at].astype(F32))
        dactive = dtotal[at]
        resid[at] += norm_back(dactive, rows[4:5], hat, inverse)
        pieces[0].append(column_sum(dactive * hat))
        pieces[1].append(column_sum(dactive))
    for i in range(2):
        halves[i] = resid[i * half : (i + 1) * half].astype(LOW)
    give_grad = remote(halves.at[1 - c], input_grad.at[c], swap_sem.at[1], partner)
    give_grad.start()
    keep_grad = load(halves.at[c], input_grad.at[c], 9)
    sums[0, 0:1] = pieces[0][0] + pieces[0][1]
    sums[0, 1:2] = pieces[1][0] + pieces[1][1]
    sums[0, 2:3] = column_sum(qkv[:, :width])
    sums[0, 3:4] = column_sum(qkv[:, 2 * width :])
    near = [partner, dev(1 - x, y, z, c), dev(x, 1 - y, z, c)]
    near += [dev(x, y, z_partner(z, k), c) for k in (1, 2, 3)]
    sum_copies = [
        remote(sums.at[min(n, 3)], got_sums.at[n], sum_sem.at[n], near[n]) for n in range(6)
    ]
    sum_copies[0].start()

    def finish_w1(q):
        def store(value):
            own_w1[:, pl.ds(q * width, width)] = value

        w1[q].finish(store)

    def finish_wj(n):
        def store(value):
            for i in range(3):
                at = pl.ds(i * width + n * 256, 256)
                own_wj[:, at] = value[:, i * 256 : (i + 1) * 256]

        wj[n].finish(store)

    def put(out, first):
        def store(value):
            out[:, pl.ds(first, value.shape[1])] = value

        return store

    wj[3].step(1)
    wj[1].step(2)
    for n in range(3):
        sum_copies[n].wait_recv()
        sums[n + 1] = sums[n] + got_sums[n]
        for copy in sum_copies[n + 1 : n + 2 if n < 2 else 6]:
            copy.start()
        if n == 0:
            wj[2].step(2)
        if n == 1:
            wj[3].step(2)
    for q in range(4):
        finish_w1(q)
    for i in range(2):
        w2[i].finish(put(own_w2, i * width // 2))
    wo.finish(put(own_wo, 0))
    for copy in sum_copies[3:]:
        copy.wait_recv()
    totals[...] = (sums[3] + got_sums[3]) + (got_sums[4] + got_sums[5])
    for n in range(4):
        finish_wj(n)
    drain()
    for copy in sum_copies:
        copy.wait_send()
    give.wait_recv()
    keep_grad.wait()
    give_grad.wait()


def back(hidden, slope, dout, active2, ctx, resid, joint, active1, image, probs, *others):
    sds, vmem, dma = jax.ShapeDtypeStruct, pltpu.VMEM, pltpu.SemaphoreType.DMA
    width, wide = image.shape[1], hidden.shape[1]
    grads = [(width // 2, width)] * 4 + [(wide // 2, width // 2)] * 2 + [(width // 2, width)]
    grads += [(width // 2, 3 * width // 4)] * 4
    in_hbm = pl.BlockSpec(memory_space=pl.ANY)
    in_vmem = pl.BlockSpec(memory_space=pltpu.VMEM)
    low, full = vmem((LEN, width), LOW), vmem((LEN, width), F32)

    return pl.pallas_call(
        back_kernel,
        out_shape=[
            sds((2, LEN // 2, width), LOW),
            sds((2, LEN // 2, width), LOW),
            sds((width // 32, 3 * width), F32),
            sds((width // 32, width), F32),
            sds((width // 32, wide), F32),
            sds((wide // 32, width), F32),
            sds((16, width), F32),
        ],
        in_specs=[in_hbm] * 15 + [in_vmem],
        out_specs=[in_hbm] * 2 + [in_vmem] * 5,
        scratch_shapes=[
            vmem((2, LEN, width), LOW),
            vmem((2, LEN, width), LOW),
            low,
            low,
            low,
            vmem((LEN, 3 * width), LOW),
            vmem((2, 2, LEN, LEN), LOW),
            full,
            vmem((2, width, STEP), LOW),
            vmem((2, STEP, width), LOW),
            full,
            full,
            vmem((2, LEN // 2, width), LOW),
            vmem((512, width), LOW),
            vmem((4, 16, width), F32),
            vmem((6, 16, width), F32),
            *[vmem(shape, LOW) for shape in grads],
            *[vmem((r * 15 // 16, n), LOW) for r, n in grads],
            dma((16,)),
            dma((2, 2)),
            dma((9, 2)),
            dma((6, 2)),
            dma((2, 2)),
            *[dma((15, 2)) for _ in grads],
        ],
        compiler_params=pltpu.CompilerParams(
            collective_id=2, has_side_effects=True, vmem_limit_bytes=VMEM_LIMIT
        ),
    )(hidden, slope, dout, active2, ctx, resid, joint, active1, image, probs, *others)


def hand_out_kernel(*refs):
    sources, totals, refs = refs[:6], refs[6], refs[7:]
    outs, (g1, s1, bj, bo, g2, s2, b1, b2, means) = refs[:6], refs[6:15]
    for src, dst in zip(sources, outs):
        dst[...] = src[...]
    rank = lax.axis_index("seq") * 8 + lax.axis_index("shard")
    width = totals.shape[1]

    def own(first, count=1):
        size = count * width // 32
        row, at = lax.div(rank * size, width), lax.rem(rank * size, width)
        value = totals[first : first + count]
        kept = lax.broadcasted_iota(jnp.int32, value.shape, 0) == row
        value = jnp.sum(jnp.where(kept, value, 0.0), axis=0, keepdims=True)
        value = jnp.broadcast_to(value, (8, width))
        return pltpu.roll(value, lax.rem(width - at, width), 1)[:1, :size]

    firsts = (0, 1, 2, 4, 5, 6, 8, 7)
    for out, first in zip((g1, s1, bj, bo, g2, s2, b1, b2), firsts):
        out[...] = own(first, out.shape[1] * 32 // width)
    for i, row in enumerate((13, 12, 14)):
        mean = jnp.sum(totals[row : row + 1], axis=1, keepdims=True) / (VALID * width * 32)
        means[:, i : i + 1] = jnp.sqrt(mean + 1e-06)


def hand_out(results, totals, sizes):
    sds = jax.ShapeDtypeStruct
    vmem = pl.BlockSpec(memory_space=pltpu.VMEM)
    return pl.pallas_call(
        hand_out_kernel,
        out_shape=[sds(r.shape, r.dtype) for r in results]
        + [sds((1, n), F32) for n in sizes]
        + [sds((1, 3), F32)],
        in_specs=[vmem] * 7,
        out_specs=[vmem] * 15,
        compiler_params=pltpu.CompilerParams(vmem_limit_bytes=VMEM_LIMIT),
    )(*results, totals)


def on_chip(
    inputs,
    cotangent,
    first_gain,
    first_shift,
    joint_weight,
    joint_bias,
    output_weight,
    output_bias,
    second_gain,
    second_shift,
    expand_weight,
    expand_bias,
    reduce_weight,
    reduce_bias,
):
    width = inputs.shape[2]
    smalls = [
        first_gain,
        first_shift,
        joint_bias,
        output_bias,
        second_gain,
        second_shift,
        expand_bias,
        reduce_bias,
    ]
    packed = jnp.concatenate([v.reshape(-1, 128) for v in smalls])
    packed = jnp.pad(packed, ((0, -packed.shape[0] % 16), (0, 0)))

    wj, wo, w1, w2, rows, b1, dout, image, active1, joint, ctx, probs, *mid = front(
        inputs, cotangent, packed, (joint_weight, output_weight, expand_weight, reduce_weight)
    )
    resid, active2, hidden, slope, grad_w2 = mid
    held = (hidden, slope, dout, active2, ctx, resid, joint, active1, image, probs)
    *results, totals = back(*held, grad_w2, wj, wo, w1, w2, rows)
    sizes = [v.shape[0] * 8 // 32 for v in smalls]
    *results, root_means = hand_out(results, totals, sizes)
    layer_out, input_grad, own_wj, own_wo, own_w1, own_w2, *own = results
    own_g1, own_s1, own_bj, own_bo, own_g2, own_s2, own_b1, own_b2 = [v[0] for v in own]
    root_means = root_means[0]
    return (
        layer_out,
        input_grad,
        own_g1,
        own_s1,
        own_wj,
        own_bj,
        own_wo,
        own_bo,
        own_g2,
        own_s2,
        own_w1,
        own_b1,
        own_w2,
        own_b2,
        root_means,
    )


def solution(mesh):
    whole_images = mesh.shape["seq"] == 4 and mesh.shape["shard"] == 8
    return jax.shard_map(
        on_chip if whole_images else on_device,
        mesh=mesh,
        in_specs=(
            P("shard", "seq", None),
            P("shard", "seq", None),
            P("shard"),
            P("shard"),
            P("shard", None),
            P("shard"),
            P("shard", None),
            P("shard"),
            P("shard"),
            P("shard"),
            P("shard", None),
            P("shard"),
            P("shard", None),
            P("shard"),
        ),
        out_specs=(
            P("shard", "seq", None),
            P("shard", "seq", None),
            P(("seq", "shard")),
            P(("seq", "shard")),
            P(("seq", "shard"), None),
            P(("seq", "shard")),
            P(("seq", "shard"), None),
            P(("seq", "shard")),
            P(("seq", "shard")),
            P(("seq", "shard")),
            P(("seq", "shard"), None),
            P(("seq", "shard")),
            P(("seq", "shard"), None),
            P(("seq", "shard")),
            P(),
        ),
        check_vma=False,
    )
```

```python
import functools

import jax
import jax.numpy as jnp
from jax import lax
from jax.experimental import pallas as pl
from jax.experimental.pallas import tpu as pltpu
from jax.sharding import PartitionSpec as P

MESH = pl.DeviceIdType.MESH
F32 = jnp.float32
LOW = jnp.bfloat16
HEAD_DIM = 64
LEN = 592
VALID = 577
PACK = 2
CUT = VALID // 16 * 16
SLOTS = 8
LEAD = (0, 2, 3, 4, 6)
VMEM_LIMIT = 61 << 20


def layer_norm(value, gain, shift):
    center = value - jnp.mean(value, axis=-1, keepdims=True)
    spread = jnp.mean(center * center, axis=-1, keepdims=True)
    return center * lax.rsqrt(spread + 1e-06) * gain + shift


def weight_grad(left, right):
    return lax.dot_general(
        left, right, (((0, 1), (0, 1)), ((), ())), preferred_element_type=jnp.float32
    )


def back_product(grad, matrix):
    return lax.dot_general(
        grad, matrix, (((2,), (1,)), ((), ())), preferred_element_type=jnp.float32
    )


def exact_gelu(value):
    return jax.nn.gelu(value, approximate=False)


def on_device(
    inputs,
    cotangent,
    first_gain,
    first_shift,
    joint_weight,
    joint_bias,
    output_weight,
    output_bias,
    second_gain,
    second_shift,
    expand_weight,
    expand_bias,
    reduce_weight,
    reduce_bias,
):
    images = inputs.shape[0]
    tokens = inputs.shape[1]
    full_seq = PACK * LEN
    pieces = images * PACK
    factor = HEAD_DIM ** (-0.5)
    begin = lax.axis_index("seq") * tokens
    local_places = begin + jnp.arange(tokens, dtype=jnp.int32)
    local_row = (local_places % LEN < VALID).astype(jnp.float32)
    local_mask = jnp.broadcast_to(local_row[None, :], (images, tokens))
    key_keep = jnp.arange(LEN, dtype=jnp.int32) < VALID
    weighting = local_mask[:, :, None]
    g1w, s1w, wj, bj, wo, bo, g2w, s2w, w1, b1, w2, b2 = (
        lax.all_gather(first_gain, "shard", axis=0, tiled=True),
        lax.all_gather(first_shift, "shard", axis=0, tiled=True),
        lax.all_gather(joint_weight, "shard", axis=0, tiled=True),
        lax.all_gather(joint_bias, "shard", axis=0, tiled=True),
        lax.all_gather(output_weight, "shard", axis=0, tiled=True),
        lax.all_gather(output_bias, "shard", axis=0, tiled=True),
        lax.all_gather(second_gain, "shard", axis=0, tiled=True),
        lax.all_gather(second_shift, "shard", axis=0, tiled=True),
        lax.all_gather(expand_weight, "shard", axis=0, tiled=True),
        lax.all_gather(expand_bias, "shard", axis=0, tiled=True),
        lax.all_gather(reduce_weight, "shard", axis=0, tiled=True),
        lax.all_gather(reduce_bias, "shard", axis=0, tiled=True),
    )
    g1f = g1w.astype(jnp.float32)
    s1f = s1w.astype(jnp.float32)
    bjf = bj.astype(jnp.float32)
    bof = bo.astype(jnp.float32)
    g2f = g2w.astype(jnp.float32)
    s2f = s2w.astype(jnp.float32)
    b1f = b1.astype(jnp.float32)
    b2f = b2.astype(jnp.float32)
    width = g1f.shape[0]
    xfull = inputs.astype(jnp.float32)
    normed1, first_back = jax.vjp(layer_norm, xfull, g1f, s1f)
    active1 = normed1.astype(jnp.bfloat16)
    bias_full = jnp.concatenate([bjf[:width], jnp.zeros((width,), jnp.float32), bjf[width:]])
    joint = (jnp.dot(active1, wj, preferred_element_type=jnp.float32) + bias_full).astype(
        jnp.bfloat16
    )
    joint = joint.reshape(images, tokens, 3, width)
    heads = lax.all_to_all(joint, "seq", split_axis=3, concat_axis=1, tiled=True)
    local_width = heads.shape[3]
    local_heads = local_width // HEAD_DIM
    query = heads[:, :, 0].reshape(pieces, LEN, local_heads, HEAD_DIM)
    keys = heads[:, :, 1].reshape(pieces, LEN, local_heads, HEAD_DIM)
    values = heads[:, :, 2].reshape(pieces, LEN, local_heads, HEAD_DIM)

    def score_block(qpart, kpart):
        raw = jnp.einsum("qhd,khd->hqk", qpart, kpart, preferred_element_type=jnp.float32) * factor
        return jnp.where(key_keep[None, None, :], raw, -1000000000.0)

    def attend(item):
        qpart, kpart, vpart = item
        scores = score_block(qpart, kpart)
        top = jnp.max(scores, axis=-1, keepdims=True)
        expo = jnp.exp(scores - top)
        total = jnp.sum(expo, axis=-1, keepdims=True)
        probs = expo / total
        logsum = (top + jnp.log(total))[:, :, 0]
        context = jnp.einsum(
            "hqk,khd->qhd", probs.astype(jnp.bfloat16), vpart, preferred_element_type=jnp.float32
        )
        return (context.astype(jnp.bfloat16).reshape(LEN, local_width), logsum)

    context, logsums = lax.map(attend, (query, keys, values))
    context = context.reshape(images, full_seq, local_width)
    gathered_ctx = lax.all_to_all(context, "seq", split_axis=1, concat_axis=2, tiled=True)
    attn = jnp.dot(gathered_ctx, wo, preferred_element_type=jnp.float32) + bof
    resid = xfull + attn
    normed2, second_back = jax.vjp(layer_norm, resid, g2f, s2f)
    active2 = normed2.astype(jnp.bfloat16)
    upper = jnp.dot(active2, w1, preferred_element_type=jnp.float32) + b1f
    activated, gelu_back = jax.vjp(exact_gelu, upper)
    hidden = activated.astype(jnp.bfloat16)
    branch = jnp.dot(hidden, w2, preferred_element_type=jnp.float32) + b2f
    result = resid + branch
    sums = jnp.stack(
        [
            jnp.sum(result * result * weighting),
            jnp.sum(attn * attn * weighting),
            jnp.sum(branch * branch * weighting),
        ]
    )
    counted = jnp.sum(local_mask) * width
    total_sums, total_count = lax.psum((sums, counted), ("seq", "shard"))
    root_means = jnp.sqrt(total_sums / total_count + 1e-06)
    wj, wo, w1, w2 = (
        lax.all_gather(joint_weight, "shard", axis=0, tiled=True),
        lax.all_gather(output_weight, "shard", axis=0, tiled=True),
        lax.all_gather(expand_weight, "shard", axis=0, tiled=True),
        lax.all_gather(reduce_weight, "shard", axis=0, tiled=True),
    )
    dout = cotangent.astype(jnp.float32) * weighting
    dout_low = dout.astype(jnp.bfloat16)
    grad_w2 = weight_grad(hidden, dout_low)
    grad_b2 = jnp.sum(dout, axis=(0, 1))
    dhidden = back_product(dout_low, w2)
    dupper = gelu_back(dhidden)[0].astype(jnp.bfloat16)
    grad_w1 = weight_grad(active2, dupper)
    grad_b1 = jnp.sum(dupper.astype(jnp.float32), axis=(0, 1))
    dactive2 = back_product(dupper, w1)
    dresid_norm, grad_g2, grad_s2 = second_back(dactive2)
    dresid = dout + dresid_norm
    dattn = dresid.astype(jnp.bfloat16)
    grad_wo = weight_grad(gathered_ctx, dattn)
    grad_bo = jnp.sum(dattn.astype(jnp.float32), axis=(0, 1))
    dcontext = back_product(dattn, wo).astype(jnp.bfloat16)
    dctx_heads = lax.all_to_all(dcontext, "seq", split_axis=2, concat_axis=1, tiled=True)
    dctx_heads = dctx_heads.reshape(pieces, LEN, local_heads, HEAD_DIM)

    def attend_back(item):
        qpart, kpart, vpart, logsum, dpart = item
        scores = score_block(qpart, kpart)
        probs = jnp.exp(scores - logsum[:, :, None])
        dprobs = jnp.einsum("qhd,khd->hqk", dpart, vpart, preferred_element_type=jnp.float32)
        dscore = (probs * (dprobs - jnp.sum(probs * dprobs, axis=-1, keepdims=True))).astype(
            jnp.bfloat16
        )
        dquery = (
            jnp.einsum("hqk,khd->qhd", dscore, kpart, preferred_element_type=jnp.float32) * factor
        )
        dkeys = (
            jnp.einsum("hqk,qhd->khd", dscore, qpart, preferred_element_type=jnp.float32) * factor
        )
        dvalues = jnp.einsum(
            "hqk,qhd->khd", probs.astype(jnp.bfloat16), dpart, preferred_element_type=jnp.float32
        )
        stacked = jnp.stack([dquery, dkeys, dvalues], axis=1).astype(jnp.bfloat16)
        return stacked.reshape(LEN, 3, local_width)

    dheads = lax.map(attend_back, (query, keys, values, logsums, dctx_heads))
    dheads = dheads.reshape(images, full_seq, 3, local_width)
    djoint = lax.all_to_all(dheads, "seq", split_axis=1, concat_axis=3, tiled=True)
    djoint = djoint.reshape(images, tokens, 3 * width)
    grad_wj = weight_grad(active1, djoint)
    joint_sums = jnp.sum(djoint.astype(jnp.float32), axis=(0, 1))
    grad_bj = jnp.concatenate([joint_sums[:width], joint_sums[2 * width :]])
    dactive1 = back_product(djoint, wj)
    dinput_norm, grad_g1, grad_s1 = first_back(dactive1)
    dinput = (dresid + dinput_norm).astype(jnp.bfloat16)
    (
        own_g1,
        own_s1,
        own_wj,
        own_bj,
        own_wo,
        own_bo,
        own_g2,
        own_s2,
        own_w1,
        own_b1,
        own_w2,
        own_b2,
    ) = (
        lax.psum_scatter(grad_g1, ("seq", "shard"), scatter_dimension=0, tiled=True),
        lax.psum_scatter(grad_s1, ("seq", "shard"), scatter_dimension=0, tiled=True),
        lax.psum_scatter(grad_wj, ("seq", "shard"), scatter_dimension=0, tiled=True),
        lax.psum_scatter(grad_bj, ("seq", "shard"), scatter_dimension=0, tiled=True),
        lax.psum_scatter(grad_wo, ("seq", "shard"), scatter_dimension=0, tiled=True),
        lax.psum_scatter(grad_bo, ("seq", "shard"), scatter_dimension=0, tiled=True),
        lax.psum_scatter(grad_g2, ("seq", "shard"), scatter_dimension=0, tiled=True),
        lax.psum_scatter(grad_s2, ("seq", "shard"), scatter_dimension=0, tiled=True),
        lax.psum_scatter(grad_w1, ("seq", "shard"), scatter_dimension=0, tiled=True),
        lax.psum_scatter(grad_b1, ("seq", "shard"), scatter_dimension=0, tiled=True),
        lax.psum_scatter(grad_w2, ("seq", "shard"), scatter_dimension=0, tiled=True),
        lax.psum_scatter(grad_b2, ("seq", "shard"), scatter_dimension=0, tiled=True),
    )
    return (
        result.astype(jnp.bfloat16),
        dinput,
        own_g1,
        own_s1,
        own_wj,
        own_bj,
        own_wo,
        own_bo,
        own_g2,
        own_s2,
        own_w1,
        own_b1,
        own_w2,
        own_b2,
        root_means,
    )


def place():
    seq = lax.axis_index("seq")
    shard = lax.axis_index("shard")
    return lax.rem(shard, 2), lax.div(seq, 2), lax.div(shard, 2), lax.rem(seq, 2)


def z_partner(z, k):
    if k == 0:
        return z
    if k == 1:
        return z + 1 - 2 * lax.rem(z, 2)
    if k == 2:
        return lax.rem(z + 2, 4)
    return 3 - z


def dev(x, y, z, c):
    return (y * 2 + c, z * 2 + x)


def remote(src, dst, sem, target):
    return pltpu.make_async_remote_copy(
        src_ref=src,
        dst_ref=dst,
        send_sem=sem.at[0],
        recv_sem=sem.at[1],
        device_id=target,
        device_id_type=MESH,
    )


def greet():
    x, y, z, c = place()
    barrier = pltpu.get_barrier_semaphore()
    near = [dev(x, y, z_partner(z, k), c) for k in (1, 2, 3)]
    near += [dev(1 - x, y, z, c), dev(x, 1 - y, z, c), dev(x, y, z, 1 - c)]
    for who in near:
        pl.semaphore_signal(barrier, inc=1, device_id=who, device_id_type=MESH)
    pl.semaphore_wait(barrier, len(near))


class Gather:
    def __init__(self, part, full, piece, sems, slot):
        self.part, self.full = part, full
        self.zs, self.xs, self.ys, self.cs, self.es, self.own = [s.at[slot] for s in sems]
        self.shard_rows = part.shape[0]
        self.row, self.rows, self.col, self.cols = piece
        edge = self.cols * 3 // 8 // 128 * 128
        span = self.cols - edge
        self.x, self.y, self.z, self.c = place()
        self.duty = pl.ds(pl.multiple_of(self.col + self.y * edge, 128), span)
        self.mine = pl.ds(pl.multiple_of(self.col + self.y * span, 128), edge)
        self.other = pl.ds(pl.multiple_of(self.col + (1 - self.y) * span, 128), edge)

    def half(self, k, j):
        x = self.x if j == 0 else 1 - self.x
        shard = z_partner(self.z, k) * 2 + x
        half = self.rows // 2
        first = shard * self.shard_rows + self.row + self.c * half
        return pl.ds(pl.multiple_of(first, 16), half)

    def copy(self, k, j, cols, sem, target, local=False):
        at = (self.half(k, j), cols)
        src = self.full.at[at]
        if local:
            half = self.rows // 2
            src = self.part.at[pl.ds(pl.multiple_of(self.row + self.c * half, 16), half), cols]
        return remote(src, self.full.at[at], sem, target)

    def over_z(self, k):
        target = dev(self.x, self.y, z_partner(self.z, k), self.c)
        return self.copy(0, 0, self.duty, self.zs.at[k - 1], target, local=True)

    def over_x(self, k):
        target = dev(1 - self.x, self.y, self.z, self.c)
        return self.copy(k, 0, self.duty, self.xs.at[k], target, local=k == 0)

    def over_y(self, k, j):
        target = dev(self.x, 1 - self.y, self.z, self.c)
        return self.copy(k, j, self.mine, self.ys.at[k * 2 + j], target)

    def over_core(self, k, j):
        target = dev(self.x, self.y, self.z, 1 - self.c)
        return self.copy(k, j, self.duty, self.cs.at[k * 2 + j], target)

    def over_core_rest(self, k, j):
        target = dev(self.x, self.y, self.z, 1 - self.c)
        return self.copy(k, j, self.other, self.es.at[k * 2 + j], target)

    def own_copy(self):
        shard = self.z * 2 + self.x
        cols = pl.ds(self.col, self.cols)
        rows = pl.ds(pl.multiple_of(shard * self.shard_rows + self.row, 16), self.rows)
        src = self.part.at[pl.ds(self.row, self.rows), cols]
        target = dev(self.x, self.y, self.z, 1 - self.c)
        return remote(src, self.full.at[rows, cols], self.own, target)

    def step0(self):
        for k in (1, 2, 3):
            self.over_z(k).start()
        self.over_x(0).start()
        self.own_copy().start()

    def step1(self):
        for k in (1, 2, 3):
            self.over_z(k).wait_recv()
            self.over_x(k).start()
            self.over_y(k, 0).start()
            self.over_core(k, 0).start()

    def step2(self):
        for k in (0, 1, 2, 3):
            self.over_x(k).wait_recv()
            self.over_y(k, 1).start()
            self.over_core(k, 1).start()

    def others(self):
        return [(k, 0) for k in (1, 2, 3)] + [(k, 1) for k in (0, 1, 2, 3)]

    def step3(self):
        for k, j in self.others():
            self.over_y(k, j).wait_recv()
            self.over_core_rest(k, j).start()

    def step4(self):
        for k, j in self.others():
            self.over_core(k, j).wait()
            self.over_core_rest(k, j).wait()
            self.over_y(k, j).wait_send()
        for k in (1, 2, 3):
            self.over_z(k).wait_send()
        for k in range(4):
            self.over_x(k).wait_send()
        self.own_copy().wait()


class SmallGather:
    def __init__(self, part, full, zs, xs, own):
        self.part, self.full, self.zs, self.xs, self.own = part, full, zs, xs, own
        self.x, self.y, self.z, self.c = place()

    def at(self, k):
        rows = self.part.shape[0]
        shard = z_partner(self.z, k) * 2 + self.x
        return pl.ds(pl.multiple_of(shard * rows, rows), rows)

    def over_z(self, k):
        target = dev(self.x, self.y, z_partner(self.z, k), self.c)
        return remote(self.part, self.full.at[self.at(0)], self.zs.at[k - 1], target)

    def over_x(self, k):
        target = dev(1 - self.x, self.y, self.z, self.c)
        src = self.full.at[self.at(k)] if k else self.part
        return remote(src, self.full.at[self.at(k)], self.xs.at[k], target)

    def own_copy(self):
        return pltpu.make_async_copy(self.part, self.full.at[self.at(0)], self.own.at[0])

    def step0(self):
        for k in (1, 2, 3):
            self.over_z(k).start()
        self.over_x(0).start()
        self.own_copy().start()

    def step1(self):
        for k in (1, 2, 3):
            self.over_z(k).wait_recv()
            self.over_x(k).start()

    def step4(self):
        for k in range(4):
            self.over_x(k).wait()
        for k in (1, 2, 3):
            self.over_z(k).wait_send()
        self.own_copy().wait()


def dot(left, right, left_axis=1, right_axis=0):
    return lax.dot_general(
        left,
        right,
        (((left_axis,), (right_axis,)), ((), ())),
        preferred_element_type=F32,
    )


def norm_parts(value):
    center = value - jnp.mean(value, axis=-1, keepdims=True)
    inverse = lax.rsqrt(jnp.mean(center * center, axis=-1, keepdims=True) + 1e-06)
    return center * inverse, inverse


def norm_back(grad, gain, hat, inverse):
    scaled = grad * gain
    mean = jnp.mean(scaled, axis=-1, keepdims=True)
    return inverse * (scaled - mean - hat * jnp.mean(scaled * hat, axis=-1, keepdims=True))


def keep_keys(scores):
    row = lax.broadcasted_iota(jnp.int32, (LEN - CUT, scores.shape[1]), 0) + CUT
    last = jnp.where(row < VALID, scores[CUT:], -1000000000.0)
    return jnp.concatenate([scores[:CUT], last], axis=0)


def by_head(value):
    lane = lax.broadcasted_iota(jnp.int32, value.shape, 1)
    none = jnp.zeros_like(value)
    return jnp.where(lane < HEAD_DIM, value, none), jnp.where(lane < HEAD_DIM, none, value)


def attend_pair(query, keys, values, store):
    total_ctx = None
    for i, (q, v) in enumerate(zip(by_head(query), by_head(values))):
        scores = keep_keys(dot(keys, q, 1, 1))
        top = jnp.max(scores, axis=0, keepdims=True)
        expo = jnp.exp(scores - top)
        total = jnp.sum(expo, axis=0, keepdims=True)
        probs = (expo * (1.0 / total)).astype(LOW)
        store(i, probs)
        ctx = dot(probs, v, 0, 0)
        total_ctx = ctx if total_ctx is None else total_ctx + ctx
    return total_ctx


def vector_row(table, rows, first, count):
    at = [s * rows + first + i for s in range(8) for i in range(count)]
    pieces = [table[r : r + 1] for r in at]
    return jnp.concatenate(pieces, axis=1)


def front_plan(shapes):
    (dj, cj), (do, co), (de, ce), (dr, cr) = shapes
    plan = [(0, (0, dj, i * (cj // 3), cj // 3)) for i in range(3)]
    plan += [(1, (0, do, 0, co))]
    plan += [(2, (0, de, i * (ce // 4), ce // 4)) for i in range(4)]
    plan += [(3, (i * (dr // 4), dr // 4, 0, cr)) for i in range(4)]
    return plan


def front_kernel(x_part, d_part, packed, wj, wo, w1, w2, *refs):
    fulls, outs, refs = refs[:4], refs[4:17], refs[17:]
    (rows_out, b1_out), hbm_outs = outs[:2], outs[2:]
    dout, image, active, joint, ctx, probs, active2, hidden, slope = refs[:9]
    table, own_half, far_half, weight, xf, grad, sent, out_sem, tile_sem, probs_sem, *sems = refs[9:]
    parts = (wj, wo, w1, w2)
    half_sem, fetch_sem, small_sems, sems = sems[0], sems[1], sems[2:5], sems[5:]
    x, y, z, c = place()
    greet()
    small = SmallGather(packed, table, *small_sems)
    small.step0()
    partner = dev(x, y, z, 1 - c)
    swaps, keeps = [], []
    for i, source in enumerate((x_part, d_part)):
        swaps.append(remote(source.at[1 - c], far_half.at[i], half_sem.at[2 * i], partner))
        keeps.append(
            pltpu.make_async_copy(source.at[c], own_half.at[i], half_sem.at[2 * i + 1, 0])
        )
        swaps[i].start()
        keeps[i].start()

    def whole(i):
        keeps[i].wait()
        swaps[i].wait()
        own, far = own_half[i].astype(F32), far_half[i].astype(F32)
        first, second = jnp.where(c == 0, own, far), jnp.where(c == 0, far, own)
        return jnp.concatenate([first, second], axis=0)

    plan = front_plan([p.shape for p in parts])
    pieces = [
        Gather(parts[w], fulls[w], piece, sems, i % SLOTS) for i, (w, piece) in enumerate(plan)
    ]

    last = len(pieces) - 4

    def turn(t):
        for step in (4, 3, 2, 1, 0):
            i = t - LEAD[step]
            if 0 <= i < (last if step == 4 else len(pieces)):
                getattr(pieces[i], f"step{step}")()

    stores = []

    def store(src, n, at=None):
        dst = hbm_outs[n] if at is None else hbm_outs[n].at[at]
        stores.append(pltpu.make_async_copy(src, dst, out_sem.at[len(stores)]))
        stores[-1].start()

    def fetch(source, cols, slot=0):
        copy = pltpu.make_async_copy(source.at[:, cols], weight.at[slot], fetch_sem.at[slot])
        copy.start()
        return copy

    width = active.shape[1]
    rows = packed.shape[0]
    for t in range(9):
        turn(t)
        if t == 1:
            small.step1()
        if t == 2:
            xf[...] = whole(0)
            image[...] = xf[...].astype(LOW)
            store(image, 1)
        if t == 3:
            small.step4()
            hat, _ = norm_parts(xf[...])
            vectors = table[...].astype(F32)
            gain, shift = vector_row(vectors, rows, 0, 1), vector_row(vectors, rows, 1, 1)
            active[...] = (hat * gain + shift).astype(LOW)
            store(active, 2)
            for i, first in enumerate((4, 5, 6, 11, 0, 0, 0, 0)):
                rows_out[i : i + 1] = vector_row(vectors, rows, first, 1)
            b1_out[...] = vector_row(vectors, rows, 7, 4)
        if t == 4:
            token = lax.broadcasted_iota(jnp.int32, (LEN, 1), 0)
            dout[...] = jnp.where(token < VALID, whole(1), 0.0).astype(LOW)
            store(dout, 0)
        if t >= 6:
            cols = pl.ds((t - 6) * width, width)
            fetch(fulls[0], cols).wait()
            product = dot(active[...], weight[0])
            if t != 7:
                bias = vector_row(table[...].astype(F32), rows, 2, 2)
                product += bias[:, :width] if t == 6 else bias[:, width:]
            joint[:, cols] = product.astype(LOW)
    store(joint, 3)

    pairs = width // 128

    def save(t):
        slot = lax.rem(t, 2)
        return pltpu.make_async_copy(probs.at[slot], hbm_outs[5].at[t], probs_sem.at[slot])

    @pl.loop(0, pairs)
    def _(t):
        for i in range(3):
            pl.when(t == 2 * i + 2)(functools.partial(turn, 9 + i))

        def at(i):
            return pl.ds(pl.multiple_of(i * width + t * 128, 128), 128)

        slot = lax.rem(t, 2)

        @pl.when(t > 1)
        def _():
            save(t - 2).wait()

        def put(i, value):
            probs[slot, i] = value

        query = joint[:, at(0)] * jnp.asarray(HEAD_DIM**-0.5, LOW)
        ctx[:, at(0)] = attend_pair(query, joint[:, at(1)], joint[:, at(2)], put).astype(LOW)
        save(t).start()

    store(ctx, 4)
    for t in (pairs - 2, pairs - 1):
        save(jnp.int32(t)).wait()
    fetch(fulls[1], pl.ds(0, width)).wait()
    coming = fetch(fulls[2], pl.ds(0, width), 1)
    attn = dot(ctx[...], weight[0]) + rows_out[0:1]
    keep = lax.broadcasted_iota(jnp.int32, (LEN, 1), 0) < VALID
    rows_out[5:6] = jnp.sum(jnp.where(keep, attn * attn, 0.0), axis=0, keepdims=True)
    xf[...] += attn
    store(xf, 6)
    hat, _ = norm_parts(xf[...])
    active2[...] = (hat * rows_out[1:2] + rows_out[2:3]).astype(LOW)
    store(active2, 7)
    chunks = b1_out.shape[1] // width
    begin = len(stores)

    def reduce_grad(yy):
        def rows_at(j):
            return pl.ds(pl.multiple_of(yy * width + j * 256, 256), 256)

        def copy(j):
            slot = sent.at[lax.rem(j, 2)]
            return remote(slot, grad.at[rows_at(j)], tile_sem.at[yy, j], partner)

        def product(core, j):
            cols = pl.ds(pl.multiple_of(j * 256, 256), 256)
            return dot(hidden[core, :, cols], dout[...], 0, 0)

        @pl.loop(0, width // 256)
        def _(j):
            @pl.when(j > 1)
            def _():
                copy(j - 2).wait_send()

            sent[lax.rem(j, 2)] = product(1 - c, j).astype(LOW)
            copy(j).start()

        @pl.loop(0, width // 256)
        def _(j):
            copy(j).wait_recv()
            at = rows_at(j)
            grad[at] = (product(c, j) + grad[at].astype(F32)).astype(LOW)

        for j in range(width // 256 - 2, width // 256):
            copy(j).wait_send()

    for j in range(chunks):
        if j in (0, 3):
            turn(12 if j == 0 else 14)
        coming.wait()
        slot = j % 2
        if j + 1 < chunks:
            coming = fetch(fulls[2], pl.ds((j + 1) * width, width), 1 - (j + 1) % 2)
        if j > 1:
            for copy in stores[begin + 4 * j - 8 : begin + 4 * j - 4]:
                copy.wait()
        for i in range(2):
            cols = pl.ds(i * width // 2, width // 2)
            there = pl.ds(j * width + i * width // 2, width // 2)
            upper = dot(active2[...], weight[1 - slot, :, cols]) + b1_out[:, there]
            share = 0.5 * (1.0 + lax.erf(upper * 0.7071067811865476))
            density = jnp.exp(upper * upper * -0.5) * 0.3989422804014327
            hidden[slot, :, cols] = (upper * share).astype(LOW)
            slope[slot, :, cols] = (share + upper * density).astype(LOW)
            store(hidden.at[slot, :, cols], 8, (slice(None), there))
            store(slope.at[slot, :, cols], 9, (slice(None), there))
        if j % 2:
            turn(13 if j == 1 else 15)
            reduce_grad(j // 2)
    store(grad, 10)
    for piece in pieces[last:]:
        piece.step4()
    for n, copy in enumerate(stores):
        if not begin <= n < begin + 4 * chunks - 8:
            copy.wait()


def front(x_part, d_part, packed, parts):
    sds, vmem, dma = jax.ShapeDtypeStruct, pltpu.VMEM, pltpu.SemaphoreType.DMA
    tokens, width = x_part.shape[1:]
    wide = parts[2].shape[1]
    pairs = width // 128
    hbm, in_vmem = pl.BlockSpec(memory_space=pl.ANY), pl.BlockSpec(memory_space=pltpu.VMEM)
    full = (LEN, width)
    return pl.pallas_call(
        front_kernel,
        out_shape=[sds((p.shape[0] * 8, p.shape[1]), LOW) for p in parts]
        + [
            sds((8, width), F32),
            sds((1, wide), F32),
            sds(full, LOW),
            sds(full, LOW),
            sds(full, LOW),
            sds((LEN, 3 * width), LOW),
            sds(full, LOW),
            sds((pairs, 2, LEN, LEN), LOW),
            sds(full, F32),
            sds(full, LOW),
            sds((LEN, wide), LOW),
            sds((LEN, wide), LOW),
            sds((wide // 2, width), LOW),
        ],
        in_specs=[hbm] * 7,
        out_specs=[hbm] * 4 + [in_vmem] * 2 + [hbm] * 11,
        scratch_shapes=[
            vmem(full, LOW),
            vmem(full, LOW),
            vmem(full, LOW),
            vmem((LEN, 3 * width), LOW),
            vmem(full, LOW),
            vmem((2, 2, LEN, LEN), LOW),
            vmem(full, LOW),
            vmem((2, LEN, width), LOW),
            vmem((2, LEN, width), LOW),
            vmem((packed.shape[0] * 8, 128), LOW),
            vmem((2, tokens, width), LOW),
            vmem((2, tokens, width), LOW),
            vmem((2, width, width), LOW),
            vmem(full, F32),
            vmem((wide // 2, width), LOW),
            vmem((2, 256, width), LOW),
            dma((8 + 4 * (wide // width),)),
            dma((2, width // 256, 2)),
            dma((2,)),
            dma((4, 2)),
            dma((2,)),
            dma((3, 2)),
            dma((4, 2)),
            dma((1,)),
            dma((SLOTS, 3, 2)),
            dma((SLOTS, 4, 2)),
            dma((SLOTS, 8, 2)),
            dma((SLOTS, 8, 2)),
            dma((SLOTS, 8, 2)),
            dma((SLOTS, 2)),
        ],
        compiler_params=pltpu.CompilerParams(
            collective_id=1, has_side_effects=True, vmem_limit_bytes=VMEM_LIMIT
        ),
    )(x_part, d_part, packed, *parts)


def attend_pair_back(query, keys, values, probs, dctx):
    heads = [by_head(v) for v in (query, keys, dctx)]
    sums = None
    for i in range(2):
        q, k, d = [h[i] for h in heads]
        low = probs[i]
        wide = low.astype(F32)
        dprobs = dot(values, d, 1, 1)
        inner = jnp.sum(wide * dprobs, axis=0, keepdims=True)
        dscore = (wide * (dprobs - inner)).astype(LOW)
        grads = (dot(dscore, k, 0, 0), dot(dscore, q), dot(low, d))
        sums = grads if sums is None else tuple(a + b for a, b in zip(sums, grads))
    return sums


class Scatter:
    def __init__(self, grad, got, sems, order):
        self.grad, self.got, self.sems, self.order = grad, got, sems, order
        self.size = grad.shape[0] // 16
        x, y, z, c = place()
        self.own = {"y": y, "x": x, "n": lax.rem(z, 2), "f": lax.div(z, 2)}
        self.targets = {
            "y": dev(x, 1 - y, z, c),
            "x": dev(1 - x, y, z, c),
            "n": dev(x, y, z_partner(z, 1), c),
            "f": dev(x, y, z_partner(z, 2), c),
        }

    def block(self, away):
        at = {d: 1 - v if d in away else v for d, v in self.own.items()}
        index = (at["y"] * 4 + at["f"] * 2 + at["n"]) * 2 + at["x"]
        return pl.ds(pl.multiple_of(index * self.size, 16), self.size)

    def choices(self, stage):
        found = [()]
        for d in reversed(self.order[stage + 1 :]):
            found = [(d, *f) for f in found] + found
        return found

    def copy(self, stage, n):
        away = self.choices(stage)[n]
        slot = (0, 8, 12, 14)[stage] + n
        src = self.grad.at[self.block((self.order[stage], *away))]
        dst = self.got.at[pl.ds(slot * self.size, self.size)]
        return remote(src, dst, self.sems.at[slot], self.targets[self.order[stage]])

    def start(self):
        for n in range(8):
            self.copy(0, n).start()

    def step(self, stage):
        later = self.choices(stage + 1)
        choices = self.choices(stage)
        for n, away in enumerate(choices):
            self.copy(stage, n).wait_recv()
            rows = self.block(away)
            slot = (0, 8, 12, 14)[stage] + n
            got = self.got[pl.ds(slot * self.size, self.size)]
            self.grad[rows] = self.grad[rows] + got
            if self.order[stage + 1] in away:
                rest = tuple(d for d in away if d != self.order[stage + 1])
                self.copy(stage + 1, later.index(rest)).start()

    def finish(self, store):
        self.copy(3, 0).wait_recv()
        got = self.got[pl.ds(14 * self.size, self.size)]
        store(self.grad[self.block(())].astype(F32) + got.astype(F32))
        for stage in range(4):
            for n in range(8 >> stage):
                self.copy(stage, n).wait_send()


ORDERS = ("nyxf", "nxyf", "nyxf", "nxyf", "yxnf", "xynf", "nxyf", "yxnf", "nxyf", "xynf", "nyxf")
STEP = 512
AFTER_HEADS = (
    ((3, 0), (1, 1), (4, 2), (5, 2), (0, 2), (2, 1)),
    ((6, 0), (1, 2), (3, 1)),
    ((7, 0), (2, 2), (6, 1)),
    ((8, 0), (3, 2), (7, 1), (6, 2)),
)


def back_kernel(*refs):
    hbm, rows, refs = refs[:15], refs[15], refs[16:]
    hid_h, slope_h, dout_h, a2_h, ctx_h, resid_h, joint_h, a1_h = hbm[:8]
    image_h, probs_h, grad_h, wj_h, wo_h, w1_h, w2_h = hbm[8:]
    (layer_out, input_grad, own_wj, own_wo, own_w1, own_w2, totals), refs = refs[:7], refs[7:]
    (hid, slope, du, dout, a2, qkv, probs, resid), refs = refs[:8], refs[8:]
    (wide_w, tall_w, total, dtotal, halves, sent, sums, got_sums), refs = refs[:8], refs[8:]
    (grads, gots), refs = (refs[:11], refs[11:22]), refs[22:]
    (load_sem, stream_sem, tile_sem, sum_sem, swap_sem), sems = refs[:5], refs[5:]
    x, y, z, c = place()
    width = a2.shape[1]
    partner = dev(x, y, z, 1 - c)
    scatters = [Scatter(*args) for args in zip(grads, gots, sems, ORDERS)]
    w1, w2, wo, wj = scatters[:4], scatters[4:6], scatters[6], scatters[7:]
    greet()

    def load(src, dst, n):
        copy = pltpu.make_async_copy(src, dst, load_sem.at[n])
        copy.start()
        return copy

    def span(index, size):
        return pl.ds(pl.multiple_of(index * size, 128), size)

    def load_quarter(q):
        cols = pl.ds(q * width, width)
        return [
            load(hid_h.at[:, cols], hid.at[q % 2], 2 * (q % 2)),
            load(slope_h.at[:, cols], slope.at[q % 2], 2 * (q % 2) + 1),
        ]

    def stream(q, s, slot):
        at = span(q * (width // STEP) + s, STEP)
        return (
            pltpu.make_async_copy(w1_h.at[:, at], wide_w.at[slot], stream_sem.at[slot, 0]),
            pltpu.make_async_copy(w2_h.at[at], tall_w.at[slot], stream_sem.at[slot, 1]),
        )

    parts = width // STEP
    loads = load_quarter(0)
    loads += [load(dout_h, dout, 4), load(a2_h, a2, 5)]
    halves_w2 = [
        load(grad_h.at[:, pl.ds(i * width // 2, width // 2)], w2[i].grad, 10 + i) for i in range(2)
    ]
    for copy in stream(0, 0, 0):
        copy.start()
    late = load(resid_h, resid, 6)
    total[...] = jnp.zeros_like(total)
    dtotal[...] = jnp.zeros_like(dtotal)

    def left(array, own):
        core = c if own else 1 - c
        return jnp.concatenate([array[:, span(core, 256)], array[:, span(2 + core, 256)]], axis=1)

    def both(phase, grad, product):
        slot = sent.at[:, pl.ds(0, grad.shape[1])]
        slot[...] = product(False).astype(LOW)
        copy = remote(slot, grad, tile_sem.at[phase], partner)
        copy.start()
        own = product(True)
        copy.wait_recv()
        grad[...] = (own + grad[...].astype(F32)).astype(LOW)
        return copy.wait_send

    def feed_forward(q):
        for copy in loads:
            copy.wait()
        del loads[:]
        if q < 3:
            loads.extend(load_quarter(q + 1))

        @pl.loop(0, parts)
        def _(s):
            slot = lax.rem(s, 2)
            for copy in stream(q, s, slot):
                copy.wait()

            @pl.when(s + 1 < parts)
            def _():
                for copy in stream(q, s + 1, 1 - slot):
                    copy.start()

            if q < 3:

                @pl.when(s + 1 == parts)
                def _():
                    for copy in stream(q + 1, 0, 0):
                        copy.start()

            cols = span(s, STEP)
            low = (dot(dout[...], tall_w[slot], 1, 1) * slope[q % 2, :, cols].astype(F32)).astype(
                LOW
            )
            du[:, cols] = low
            total[...] += dot(hid[q % 2, :, cols], tall_w[slot])
            dtotal[...] += dot(low, wide_w[slot], 1, 1)

        sums[0, 8 + q : 9 + q, :] = column_sum(du[...])

    def column_sum(value):
        return jnp.sum(value.astype(F32), axis=0, keepdims=True)

    for i in range(2):
        halves_w2[i].wait()
        w2[i].start()
    drain = None
    for q in range(4):
        feed_forward(q)
        if drain is not None:
            drain()
        drain = both(q, w1[q].grad, lambda own: dot(left(a2, own), du[...], 0, 0))
        w1[q].start()
        if q == 2:
            w2[0].step(0)
            w2[1].step(0)
            w1[0].step(0)
        if q == 3:
            w1[1].step(0)
    ctx, dattn, dctx, a1 = hid.at[0], hid.at[1], slope.at[0], slope.at[1]
    loads = [load(ctx_h, ctx, 0), load(a1_h, a1, 1), load(joint_h, qkv, 2)]
    loads += [load(probs_h.at[i], probs.at[i], 14 + i) for i in range(2)]
    loads += [load(image_h, a2, 5)]
    wo_loads = [load(wo_h.at[pl.ds(i * STEP, STEP)], tall_w.at[i], 7 + i) for i in range(2)]
    late.wait()
    gain, b2 = rows[1:2], rows[3:4]
    blocks = ((0, 304), (304, LEN - 304))
    pieces = [[] for _ in range(4)]
    for first, count in blocks:
        at = pl.ds(first, count)
        token = lax.broadcasted_iota(jnp.int32, (count, 1), 0) + first
        branch = total[at] + b2
        value = resid[at]
        result = value + branch
        total[at] = result
        hat, inverse = norm_parts(value)
        dactive = dtotal[at]
        grad = dout[at].astype(F32)
        pieces[3].append(column_sum(grad))
        resid[at] = grad + norm_back(dactive, gain, hat, inverse)
        pieces[0].append(column_sum(dactive * hat))
        pieces[1].append(column_sum(dactive))
        keep = token < VALID
        pieces[2].append(
            jnp.concatenate(
                [
                    column_sum(jnp.where(keep, result * result, 0.0)),
                    column_sum(jnp.where(keep, branch * branch, 0.0)),
                ],
                axis=0,
            )
        )
    add = [a + b for a, b in pieces]
    sums[0, 5:6] = add[0]
    sums[0, 6:7] = add[1]
    sums[0, 7:8] = add[3]
    sums[0, 12:13] = rows[5:6]
    sums[0, 13:15] = add[2]
    sums[0, 15:16] = jnp.zeros_like(add[0])
    half = LEN // 2
    for i in range(2):
        halves[i] = total[i * half : (i + 1) * half].astype(LOW)
    give = remote(halves.at[1 - c], layer_out.at[c], swap_sem.at[0], partner)
    give.start()
    hold = load(halves.at[c], layer_out.at[c], 9)
    w2[0].step(1)
    w2[1].step(1)
    dattn[...] = resid[...].astype(LOW)
    sums[0, 4:5] = column_sum(dattn[...])
    for i in range(2):
        wo_loads[i].wait()
        dctx[:, pl.ds(i * STEP, STEP)] = dot(dattn[...], tall_w[i], 1, 1).astype(LOW)
    for copy in loads:
        copy.wait()
    drain()
    drain = both(4, wo.grad, lambda own: dot(left(ctx, own), dattn[...], 0, 0))
    wo.start()
    w1[2].step(0)
    w1[0].step(1)
    factor = HEAD_DIM**-0.5
    pairs = width // 128

    def attend_back(t):
        def at(i):
            return span(i * pairs + t, 128)

        def fetch_probs(t):
            slot = lax.rem(t, 2)
            return pltpu.make_async_copy(probs_h.at[t], probs.at[slot], load_sem.at[14 + slot])

        @pl.when(t > 1)
        def _():
            fetch_probs(t).wait()

        scaled = qkv[:, at(0)] * jnp.asarray(factor, LOW)
        dq, dk, dv = attend_pair_back(
            scaled, qkv[:, at(1)], qkv[:, at(2)], probs.at[lax.rem(t, 2)], dctx[:, at(0)]
        )
        for i, grad in enumerate((dq * factor, dk, dv)):
            qkv[:, at(i)] = grad.astype(LOW)

        @pl.when(t + 2 < pairs)
        def _():
            fetch_probs(t + 2).start()

    fetch = [load(wj_h.at[:, pl.ds(i * STEP, STEP)], wide_w.at[i], 7 + i) for i in range(2)]
    for n in range(4):
        pl.loop(2 * n, 2 * n + 2)(attend_back)
        drain()

        def product(own, n=n):
            rows_of = left(a1, own)
            columns = [qkv[:, pl.ds(i * width + n * 256, 256)] for i in range(3)]
            return jnp.concatenate([dot(rows_of, part, 0, 0) for part in columns], axis=1)

        drain = both(5 + n, wj[n].grad, product)
        wj[n].start()
        for scatter, stage in AFTER_HEADS[n]:
            scatters[scatter].step(stage)
    chunks = qkv.shape[1] // STEP
    for i in range(chunks):
        fetch[i].wait()
        product = dot(qkv[:, pl.ds(i * STEP, STEP)], wide_w[i % 2], 1, 1)
        dtotal[...] = dtotal[...] + product if i else product
        if i + 2 < chunks:
            at = pl.ds((i + 2) * STEP, STEP)
            fetch.append(load(wj_h.at[:, at], wide_w.at[i % 2], 7 + i % 2))
        if i == 2:
            wj[2].step(0)
            wj[1].step(1)
    wj[3].step(0)
    wj[0].step(2)
    wj[2].step(1)
    hold.wait()
    give.wait_send()
    pieces = [[] for _ in range(2)]
    for first, count in blocks:
        at = pl.ds(first, count)
        hat, inverse = norm_parts(a2[at].astype(F32))
        dactive = dtotal[at]
        resid[at] += norm_back(dactive, rows[4:5], hat, inverse)
        pieces[0].append(column_sum(dactive * hat))
        pieces[1].append(column_sum(dactive))
    for i in range(2):
        halves[i] = resid[i * half : (i + 1) * half].astype(LOW)
    give_grad = remote(halves.at[1 - c], input_grad.at[c], swap_sem.at[1], partner)
    give_grad.start()
    keep_grad = load(halves.at[c], input_grad.at[c], 9)
    sums[0, 0:1] = pieces[0][0] + pieces[0][1]
    sums[0, 1:2] = pieces[1][0] + pieces[1][1]
    sums[0, 2:3] = column_sum(qkv[:, :width])
    sums[0, 3:4] = column_sum(qkv[:, 2 * width :])
    near = [partner, dev(1 - x, y, z, c), dev(x, 1 - y, z, c)]
    near += [dev(x, y, z_partner(z, k), c) for k in (1, 2, 3)]
    sum_copies = [
        remote(sums.at[min(n, 3)], got_sums.at[n], sum_sem.at[n], near[n]) for n in range(6)
    ]
    sum_copies[0].start()

    def finish_w1(q):
        def store(value):
            own_w1[:, pl.ds(q * width, width)] = value

        w1[q].finish(store)

    def finish_wj(n):
        def store(value):
            for i in range(3):
                at = pl.ds(i * width + n * 256, 256)
                own_wj[:, at] = value[:, i * 256 : (i + 1) * 256]

        wj[n].finish(store)

    def put(out, first):
        def store(value):
            out[:, pl.ds(first, value.shape[1])] = value

        return store

    wj[3].step(1)
    wj[1].step(2)
    for n in range(3):
        sum_copies[n].wait_recv()
        sums[n + 1] = sums[n] + got_sums[n]
        for copy in sum_copies[n + 1 : n + 2 if n < 2 else 6]:
            copy.start()
        if n == 0:
            wj[2].step(2)
        if n == 1:
            wj[3].step(2)
    for q in range(4):
        finish_w1(q)
    for i in range(2):
        w2[i].finish(put(own_w2, i * width // 2))
    wo.finish(put(own_wo, 0))
    for copy in sum_copies[3:]:
        copy.wait_recv()
    totals[...] = (sums[3] + got_sums[3]) + (got_sums[4] + got_sums[5])
    for n in range(4):
        finish_wj(n)
    drain()
    for copy in sum_copies:
        copy.wait_send()
    give.wait_recv()
    keep_grad.wait()
    give_grad.wait()


def back(hidden, slope, dout, active2, ctx, resid, joint, active1, image, probs, *others):
    sds, vmem, dma = jax.ShapeDtypeStruct, pltpu.VMEM, pltpu.SemaphoreType.DMA
    width, wide = image.shape[1], hidden.shape[1]
    grads = [(width // 2, width)] * 4 + [(wide // 2, width // 2)] * 2 + [(width // 2, width)]
    grads += [(width // 2, 3 * width // 4)] * 4
    in_hbm = pl.BlockSpec(memory_space=pl.ANY)
    in_vmem = pl.BlockSpec(memory_space=pltpu.VMEM)
    low, full = vmem((LEN, width), LOW), vmem((LEN, width), F32)

    return pl.pallas_call(
        back_kernel,
        out_shape=[
            sds((2, LEN // 2, width), LOW),
            sds((2, LEN // 2, width), LOW),
            sds((width // 32, 3 * width), F32),
            sds((width // 32, width), F32),
            sds((width // 32, wide), F32),
            sds((wide // 32, width), F32),
            sds((16, width), F32),
        ],
        in_specs=[in_hbm] * 15 + [in_vmem],
        out_specs=[in_hbm] * 2 + [in_vmem] * 5,
        scratch_shapes=[
            vmem((2, LEN, width), LOW),
            vmem((2, LEN, width), LOW),
            low,
            low,
            low,
            vmem((LEN, 3 * width), LOW),
            vmem((2, 2, LEN, LEN), LOW),
            full,
            vmem((2, width, STEP), LOW),
            vmem((2, STEP, width), LOW),
            full,
            full,
            vmem((2, LEN // 2, width), LOW),
            vmem((512, width), LOW),
            vmem((4, 16, width), F32),
            vmem((6, 16, width), F32),
            *[vmem(shape, LOW) for shape in grads],
            *[vmem((r * 15 // 16, n), LOW) for r, n in grads],
            dma((16,)),
            dma((2, 2)),
            dma((9, 2)),
            dma((6, 2)),
            dma((2, 2)),
            *[dma((15, 2)) for _ in grads],
        ],
        compiler_params=pltpu.CompilerParams(
            collective_id=2, has_side_effects=True, vmem_limit_bytes=VMEM_LIMIT
        ),
    )(hidden, slope, dout, active2, ctx, resid, joint, active1, image, probs, *others)


def hand_out_kernel(*refs):
    sources, totals, refs = refs[:6], refs[6], refs[7:]
    outs, (g1, s1, bj, bo, g2, s2, b1, b2, means) = refs[:6], refs[6:15]
    for src, dst in zip(sources, outs):
        dst[...] = src[...]
    rank = lax.axis_index("seq") * 8 + lax.axis_index("shard")
    width = totals.shape[1]

    def own(first, count=1):
        size = count * width // 32
        row, at = lax.div(rank * size, width), lax.rem(rank * size, width)
        value = totals[first : first + count]
        kept = lax.broadcasted_iota(jnp.int32, value.shape, 0) == row
        value = jnp.sum(jnp.where(kept, value, 0.0), axis=0, keepdims=True)
        value = jnp.broadcast_to(value, (8, width))
        return pltpu.roll(value, lax.rem(width - at, width), 1)[:1, :size]

    firsts = (0, 1, 2, 4, 5, 6, 8, 7)
    for out, first in zip((g1, s1, bj, bo, g2, s2, b1, b2), firsts):
        out[...] = own(first, out.shape[1] * 32 // width)
    for i, row in enumerate((13, 12, 14)):
        mean = jnp.sum(totals[row : row + 1], axis=1, keepdims=True) / (VALID * width * 32)
        means[:, i : i + 1] = jnp.sqrt(mean + 1e-06)


def hand_out(results, totals, sizes):
    sds = jax.ShapeDtypeStruct
    vmem = pl.BlockSpec(memory_space=pltpu.VMEM)
    return pl.pallas_call(
        hand_out_kernel,
        out_shape=[sds(r.shape, r.dtype) for r in results]
        + [sds((1, n), F32) for n in sizes]
        + [sds((1, 3), F32)],
        in_specs=[vmem] * 7,
        out_specs=[vmem] * 15,
        compiler_params=pltpu.CompilerParams(vmem_limit_bytes=VMEM_LIMIT),
    )(*results, totals)


def on_chip(
    inputs,
    cotangent,
    first_gain,
    first_shift,
    joint_weight,
    joint_bias,
    output_weight,
    output_bias,
    second_gain,
    second_shift,
    expand_weight,
    expand_bias,
    reduce_weight,
    reduce_bias,
):
    width = inputs.shape[2]
    smalls = [
        first_gain,
        first_shift,
        joint_bias,
        output_bias,
        second_gain,
        second_shift,
        expand_bias,
        reduce_bias,
    ]
    packed = jnp.concatenate([v.reshape(-1, 128) for v in smalls])
    packed = jnp.pad(packed, ((0, -packed.shape[0] % 16), (0, 0)))

    wj, wo, w1, w2, rows, b1, dout, image, active1, joint, ctx, probs, *mid = front(
        inputs, cotangent, packed, (joint_weight, output_weight, expand_weight, reduce_weight)
    )
    resid, active2, hidden, slope, grad_w2 = mid
    held = (hidden, slope, dout, active2, ctx, resid, joint, active1, image, probs)
    *results, totals = back(*held, grad_w2, wj, wo, w1, w2, rows)
    sizes = [v.shape[0] * 8 // 32 for v in smalls]
    *results, root_means = hand_out(results, totals, sizes)
    layer_out, input_grad, own_wj, own_wo, own_w1, own_w2, *own = results
    own_g1, own_s1, own_bj, own_bo, own_g2, own_s2, own_b1, own_b2 = [v[0] for v in own]
    root_means = root_means[0]
    return (
        layer_out,
        input_grad,
        own_g1,
        own_s1,
        own_wj,
        own_bj,
        own_wo,
        own_bo,
        own_g2,
        own_s2,
        own_w1,
        own_b1,
        own_w2,
        own_b2,
        root_means,
    )


def solution(mesh):
    whole_images = mesh.shape["seq"] == 4 and mesh.shape["shard"] == 8
    return jax.shard_map(
        on_chip if whole_images else on_device,
        mesh=mesh,
        in_specs=(
            P("shard", "seq", None),
            P("shard", "seq", None),
            P("shard"),
            P("shard"),
            P("shard", None),
            P("shard"),
            P("shard", None),
            P("shard"),
            P("shard"),
            P("shard"),
            P("shard", None),
            P("shard"),
            P("shard", None),
            P("shard"),
        ),
        out_specs=(
            P("shard", "seq", None),
            P("shard", "seq", None),
            P(("seq", "shard")),
            P(("seq", "shard")),
            P(("seq", "shard"), None),
            P(("seq", "shard")),
            P(("seq", "shard"), None),
            P(("seq", "shard")),
            P(("seq", "shard")),
            P(("seq", "shard")),
            P(("seq", "shard"), None),
            P(("seq", "shard")),
            P(("seq", "shard"), None),
            P(("seq", "shard")),
            P(),
        ),
        check_vma=False,
    )
```
